128 devices in a mesh: section: 2 (over x_lo), fsdp: 16 (over y, x_hi, core), replica: 4 (over z).
Axes of the slice: x: 4 (x_hi: 2, x_lo: 2; x = x_hi * 2 + x_lo), y: 4, z: 4, core: 2. Of those that a mesh axis runs over, the one named last changes fastest.
Arguments:
- inputs: bfloat16 [8, 1024, 1088], P('replica', 'fsdp'), may hold values from -6 to 6
- segment_ids: int32 [8, 1024], P('replica'), may hold values from 0 to 5, as said below
- sequence_order: int32 [4, 2], P('replica'), may hold values from 0 to 1, each once within a row
- ln1_gain: bfloat16 [2, 1088], P('section', 'fsdp'), may hold values from 0.5 to 1.5
- ln1_bias: bfloat16 [2, 1088], P('section', 'fsdp'), may hold values from -1.75 to 1.75
- w_qkv: bfloat16 [2, 1088, 3264], P('section', 'fsdp'), may hold values from -0.1875 to 0.1875
- qv_bias: bfloat16 [2, 2176], P('section', 'fsdp'), may hold values from -1.75 to 1.75
- w_out: bfloat16 [2, 1088, 1088], P('section', 'fsdp'), may hold values from -1.5 to 1.5
- out_bias: bfloat16 [2, 1088], P('section', 'fsdp'), may hold values from -1.75 to 1.75
- ln2_gain: bfloat16 [2, 1088], P('section', 'fsdp'), may hold values from 0.5 to 1.5
- ln2_bias: bfloat16 [2, 1088], P('section', 'fsdp'), may hold values from -1.75 to 1.75
- w_fc: bfloat16 [2, 1088, 4352], P('section', 'fsdp'), may hold values from -0.1875 to 0.1875
- fc_bias: bfloat16 [2, 4352], P('section', 'fsdp'), may hold values from -1.75 to 1.75
- w_proj: bfloat16 [2, 4352, 1088], P('section', 'fsdp'), may hold values from -0.09375 to 0.09375
- proj_bias: bfloat16 [2, 1088], P('section', 'fsdp'), may hold values from -1.75 to 1.75
- cotangent: bfloat16 [8, 1024, 1088], P('replica', 'fsdp'), may hold values from -6 to 6
Outputs:
- activations: bfloat16 [2, 8, 1024, 1088], P('section', 'replica', 'fsdp')
- input_grads: bfloat16 [2, 8, 1024, 1088], P('section', 'replica', 'fsdp')
- grad_ln1_gain: float32 [2, 1088], P('section', 'fsdp')
- grad_ln1_bias: float32 [2, 1088], P('section', 'fsdp')
- grad_w_qkv: float32 [2, 1088, 3264], P('section', 'fsdp')
- grad_qv_bias: float32 [2, 2176], P('section', 'fsdp')
- grad_w_out: float32 [2, 1088, 1088], P('section', 'fsdp')
- grad_out_bias: float32 [2, 1088], P('section', 'fsdp')
- grad_ln2_gain: float32 [2, 1088], P('section', 'fsdp')
- grad_ln2_bias: float32 [2, 1088], P('section', 'fsdp')
- grad_w_fc: float32 [2, 1088, 4352], P('section', 'fsdp')
- grad_fc_bias: float32 [2, 4352], P('section', 'fsdp')
- grad_w_proj: float32 [2, 4352, 1088], P('section', 'fsdp')
- grad_proj_bias: float32 [2, 1088], P('section', 'fsdp')
The draws below stay inside these ranges and needn't reach their ends.
Inputs may be any that keep to these rules, and one draw needn't show every extreme that they name: `segment_ids`: within each sequence the document numbers start at 0 and rise by one at each document boundary; every document but a sequence's last has at least 204 tokens; in each replica group one of its 2 sequences, drawn from the seed, is a single document; the most is reached. `sequence_order`: each row is a permutation.
All inputs are finite; a program needn't handle non-finite values.
Results may differ from the reference program's by a relative error of at most 0.02.
Values may be sent and summed in bfloat16 or wider, within the bound.
No kernel may reach another device: no remote copies, remote signals or barrier semaphores. Data moves between devices by JAX's collectives and lax.ppermute only.
A program may use at most 256 MiB of HBM per device.

```python
import jax
import jax.numpy as jnp
from jax import lax

D = 1088
HEADS = 17
HEAD_DIM = 64
FF = 4352
MB = 2
SEQ = 1024
LAYERS = 2
SEQS = 8
N_REPLICA = 4


def draw_segment_ids(key, part):
    key = jax.random.fold_in(key, 11)
    key_lengths, key_whole = jax.random.split(key)
    shortest = max(SEQ // 5, 1)
    doc_count = SEQ // shortest + 1
    lengths = jax.random.randint(key_lengths, (SEQS, doc_count), shortest, SEQ + 1)
    groups = SEQS // MB
    chosen = jax.random.randint(key_whole, (groups,), 0, MB)
    densest = (chosen[0] + 1) % MB
    is_densest = jnp.arange(SEQS) == densest
    lengths = jnp.where(is_densest[:, None], shortest, lengths)
    doc_ends = jnp.cumsum(lengths, axis=1)
    positions = jnp.arange(SEQ)
    numbers = jnp.sum((doc_ends[:, None, :] <= positions[None, :, None]).astype(jnp.int32), axis=2)
    single = jnp.arange(SEQS) % MB == jnp.repeat(chosen, MB)
    numbers = jnp.where(single[:, None], 0, numbers)
    return numbers.astype(jnp.int32)


def block_scale(stream_key, dims, pieces, least, largest):
    loudness = 1.0
    for axis_at, parts in pieces:
        draws = jax.random.uniform(jax.random.fold_in(jax.random.fold_in(stream_key, 6), axis_at), (parts,), jnp.float32, least / len(pieces), largest / len(pieces))
        loudness = loudness * jnp.repeat(jnp.exp(draws), dims[axis_at] // parts).reshape((-1,) + (1,) * (len(dims) - 1 - axis_at))
    return loudness


def normal_values(key, shape, scale, most, cuts=(), held_as=jnp.bfloat16):
    result = scale * jax.random.normal(key, shape, jnp.float32)
    if cuts:
        result = result * block_scale(key, shape, cuts, -0.22, 0.18)
    return jnp.clip(result, -most, most).astype(held_as)


def setup_inputs(seed: int = 0) -> dict:
    seeds = jax.random.split(jax.random.key(seed), 17)
    return {
        "inputs": normal_values(seeds[0], (SEQS, SEQ, D), 1.0, 6.0, ((0, 4), (1, 16))),
        "segment_ids": draw_segment_ids(jax.random.fold_in(seeds[16], 71), 0),
        "sequence_order": jax.vmap(lambda own: jax.random.permutation(own, MB))(jax.random.split(seeds[2], N_REPLICA)).reshape((N_REPLICA, MB)).astype(jnp.int32),
        "ln1_gain": jnp.clip(1.0 + 0.1 * jax.random.normal(seeds[3], (LAYERS, D), jnp.float32), 0.5, 1.5).astype(jnp.bfloat16),
        "ln1_bias": normal_values(seeds[4], (LAYERS, D), 0.3, 1.75, ((0, 2), (1, 16))),
        "w_qkv": normal_values(seeds[5], (LAYERS, D, 3 * D), D ** -0.5, 0.1875, ((0, 2), (1, 16))),
        "qv_bias": normal_values(seeds[6], (LAYERS, 2 * D), 0.3, 1.75, ((0, 2), (1, 16))),
        "w_out": normal_values(seeds[7], (LAYERS, D, D), (D // 64) ** -0.5, 1.5, ((0, 2), (1, 16))),
        "out_bias": normal_values(seeds[8], (LAYERS, D), 0.3, 1.75, ((0, 2), (1, 16))),
        "ln2_gain": jnp.clip(1.0 + 0.1 * jax.random.normal(seeds[9], (LAYERS, D), jnp.float32), 0.5, 1.5).astype(jnp.bfloat16),
        "ln2_bias": normal_values(seeds[10], (LAYERS, D), 0.3, 1.75, ((0, 2), (1, 16))),
        "w_fc": normal_values(seeds[11], (LAYERS, D, FF), D ** -0.5, 0.1875, ((0, 2), (1, 16))),
        "fc_bias": normal_values(seeds[12], (LAYERS, FF), 0.3, 1.75, ((0, 2), (1, 16))),
        "w_proj": normal_values(seeds[13], (LAYERS, FF, D), FF ** -0.5, 0.09375, ((0, 2), (1, 16))),
        "proj_bias": normal_values(seeds[14], (LAYERS, D), 0.3, 1.75, ((0, 2), (1, 16))),
        "cotangent": normal_values(seeds[15], (SEQS, SEQ, D), 1.0, 6.0, ((0, 4), (1, 16))),
    }


@jax.custom_vjp
def low(v):
    return lax.optimization_barrier(v.astype(jnp.bfloat16)).astype(jnp.float32)

@jax.custom_vjp
def low_back(v):
    return v

def low_keep(v):
    return (low(v), None)

def low_pass(kept, grad):
    return (grad,)

def back_keep(v):
    return (v, None)

def back_low(kept, grad):
    return (low(grad),)
low.defvjp(low_keep, low_pass)
low_back.defvjp(back_keep, back_low)
epsilon = 1e-05
highest = lax.Precision.HIGHEST

def layer_norm(values, gain_vec, bias_vec):
    average = lax.optimization_barrier(jnp.mean(values, axis=-1, keepdims=True))
    centred = values - average
    variance = lax.optimization_barrier(jnp.mean(centred * centred, axis=-1, keepdims=True))
    return centred * lax.rsqrt(variance + epsilon) * gain_vec + bias_vec

def one_layer(sequence, layer_params, segments):
    gain_one, bias_one, full_qkv, qv_full, full_out, out_shift, gain_two, bias_two, full_fc, fc_shift, full_proj, proj_shift = layer_params
    normed_one = low(layer_norm(sequence, gain_one, bias_one))
    qkv_shift = jnp.concatenate([qv_full[:D], jnp.zeros((D,), jnp.float32), qv_full[D:]])
    packed = low_back(low(jnp.dot(normed_one, full_qkv, precision=highest) + qkv_shift))
    queries = packed[:, :D].reshape(SEQ, HEADS, HEAD_DIM)
    keys_all = packed[:, D:2 * D].reshape(SEQ, HEADS, HEAD_DIM)
    values_all = packed[:, 2 * D:].reshape(SEQ, HEADS, HEAD_DIM)
    scores = low_back(jnp.einsum('qhd,khd->hqk', queries, keys_all, precision=highest) * HEAD_DIM ** (-0.5))
    positions = jnp.arange(SEQ)
    allowed = (positions[None, :] <= positions[:, None]) & (segments[None, :] == segments[:, None])
    masked = jnp.where(allowed[None], scores, -1e+30)
    probs = low(jax.nn.softmax(masked, axis=-1))
    attended = low_back(low(jnp.einsum('hqk,khd->qhd', probs, values_all, precision=highest).reshape(SEQ, D)))
    branch_one = low_back(jnp.dot(attended, full_out, precision=highest) + out_shift)
    hidden = sequence + branch_one
    normed_two = low(layer_norm(hidden, gain_two, bias_two))
    pre_act = low_back(jnp.dot(normed_two, full_fc, precision=highest) + fc_shift)
    activ = low(jax.nn.gelu(pre_act, approximate=True))
    branch_two = low_back(jnp.dot(activ, full_proj, precision=highest) + proj_shift)
    return hidden + branch_two

def pick_rows(block, order_row):
    return jnp.take(block, order_row, axis=0)

def reference(inputs, segment_ids, sequence_order, ln1_gain, ln1_bias, w_qkv, qv_bias, w_out, out_bias, ln2_gain, ln2_bias, w_fc, fc_bias, w_proj, proj_bias, cotangent):

    def arrange(stacked):
        shaped = stacked.reshape((N_REPLICA, MB) + stacked.shape[1:])
        picked = jax.vmap(pick_rows)(shaped, sequence_order)
        return picked.reshape(stacked.shape)
    ordered = arrange(inputs).astype(jnp.float32)
    segments_all = arrange(segment_ids)
    params = tuple((tensor.astype(jnp.float32) for tensor in (ln1_gain, ln1_bias, w_qkv, qv_bias, w_out, out_bias, ln2_gain, ln2_bias, w_fc, fc_bias, w_proj, proj_bias)))
    probe_in = jnp.zeros((SEQS, SEQ, D), jnp.float32)

    def forward(source, weights, probe_zero):

        def per_sequence(carried, slices):
            sequence, seg_row, probe_row = slices
            first_out = low_back(low(one_layer(sequence, [tensor[0] for tensor in weights], seg_row))) + probe_row
            second = one_layer(first_out, [tensor[1] for tensor in weights], seg_row)
            return (carried, (first_out, second))
        _, (firsts, seconds) = lax.scan(jax.checkpoint(per_sequence), jnp.zeros((), jnp.float32), (source, segments_all, probe_zero))
        return (firsts, seconds)
    (firsts, seconds), pullback = jax.vjp(forward, ordered, params, probe_in)
    grad_inputs, grad_params, grad_probe = pullback((jnp.zeros_like(firsts), cotangent.astype(jnp.float32)))
    activations = jnp.stack([firsts, seconds]).astype(jnp.bfloat16)
    input_grads = jnp.stack([grad_inputs, grad_probe]).astype(jnp.bfloat16)
    return (activations, input_grads, grad_params[0], grad_params[1], grad_params[2], grad_params[3], grad_params[4], grad_params[5], grad_params[6], grad_params[7], grad_params[8], grad_params[9], grad_params[10], grad_params[11])
```

```python
import jax
import jax.numpy as jnp
from jax import lax
from jax.experimental import pallas as pl
from jax.experimental.pallas import tpu as pltpu
from jax.sharding import PartitionSpec as P

D = 1088
HEADS = 17
HEAD_DIM = 64
FF = 4352
SHARDS = 16
DROWS = D // SHARDS
PROWS = 72
KPAD = SHARDS * PROWS
LANES = 1152
PAIRS = 9
FROWS = FF // SHARDS
SPLITS = FF // D
SCALE = HEAD_DIM ** (-0.5)

epsilon = 1e-05
bf16 = jnp.bfloat16
f32 = jnp.float32


def xor_pairs(k):
    return [(i, i ^ k) for i in range(SHARDS)]


def moved(value, k):
    return lax.ppermute(value, "fsdp", xor_pairs(k))


def gather_near(x):
    half = x.shape[0] // 2
    blocks = {0: x, 4: moved(x, 4), 12: moved(x, 12), 2: moved(x, 2)}
    blocks[8] = jnp.concatenate([moved(blocks[4][:half], 12), moved(blocks[12][half:], 4)], 0)
    blocks[6] = moved(blocks[2], 4)
    blocks[14] = moved(blocks[2], 12)
    blocks[10] = moved(blocks[8], 2)
    return jnp.stack([blocks[k] for k in range(0, SHARDS, 2)])


def gather_both(x):
    near = gather_near(x)
    return near, moved(near, 1)


def relative_device(me, place):
    return me ^ (2 * (place % 8) + place // 8)


def placing(me, relative):
    column = lax.broadcasted_iota(jnp.int32, (1, KPAD), 1)
    place, row = column // PROWS, column % PROWS
    owner = relative_device(me, place) if relative else place
    source = jnp.where(row < DROWS, owner * DROWS + row, -1)
    return (lax.broadcasted_iota(jnp.int32, (D, KPAD), 0) == source).astype(bf16)


def layer_norm(values, gain_vec, bias_vec):
    average = jnp.mean(values, axis=-1, keepdims=True)
    centred = values - average
    variance = jnp.mean(centred * centred, axis=-1, keepdims=True)
    return centred * lax.rsqrt(variance + epsilon) * gain_vec + bias_vec


def gelu_tanh(values):
    return jax.nn.gelu(values, approximate=True)


def matmul(left, right):
    return jnp.dot(left, right, preferred_element_type=f32)


def contract(left, right, ldim, rdim):
    return lax.dot_general(left, right, (((ldim,), (rdim,)), ((), ())), preferred_element_type=f32)


def split_two(values):
    high = lax.reduce_precision(values, 8, 7)
    return high.astype(bf16), (values - high).astype(bf16)


def unplaced(values, place):
    rows = values.shape[0]
    both = contract(jnp.concatenate(split_two(values), 0), place, 1, 1)
    return both[:rows] + both[rows:]


def two_heads(block):
    lane = lax.broadcasted_iota(jnp.int32, block.shape, 1)
    zero = jnp.zeros_like(block)
    return jnp.concatenate(
        [jnp.where(lane < HEAD_DIM, block, zero), jnp.where(lane < HEAD_DIM, zero, block)], 0
    )


def one_pair(both):
    rows = both.shape[0] // 2
    lane = lax.broadcasted_iota(jnp.int32, (rows, 128), 1)
    return jnp.where(lane < HEAD_DIM, both[:rows], both[rows:])


def rows_of(near_ref, far_ref):
    return jnp.concatenate(
        [near_ref[...].reshape(-1, 128), far_ref[...].reshape(-1, 128)], 0
    )


def forward_kernel(q_ref, kn_ref, kf_ref, vn_ref, vf_ref, bias_ref, out_ref, lse_ref):
    bias = bias_ref[0]
    keys, values = rows_of(kn_ref, kf_ref), rows_of(vn_ref, vf_ref)
    scores = contract(two_heads(q_ref[...]), keys, 1, 1) * SCALE
    scores = scores + jnp.concatenate([bias, bias], 0)
    top = jnp.max(scores, axis=1, keepdims=True)
    shifted = jnp.exp(scores - top)
    total = jnp.sum(shifted, axis=1, keepdims=True)
    probs = (shifted / total).astype(bf16)
    out_ref[...] = one_pair(matmul(probs, values)).astype(bf16)
    lse = top + jnp.log(total)
    lse_ref[0, 0] = jnp.transpose(jnp.broadcast_to(lse, (128, 128)))[:8]


def row_kernel(q_ref, do_ref, lse_ref, kn_ref, kf_ref, vn_ref, vf_ref, bias_ref, dq_ref):
    bias = bias_ref[0]
    keys, values = rows_of(kn_ref, kf_ref), rows_of(vn_ref, vf_ref)
    lse = jnp.transpose(jnp.broadcast_to(lse_ref[0, 0][:1], (128, 128)))[:, :1]
    scores = contract(two_heads(q_ref[...]), keys, 1, 1) * SCALE
    scores = scores + jnp.concatenate([bias, bias], 0)
    probs = jnp.exp(scores - lse)
    grad_probs = contract(two_heads(do_ref[...]), values, 1, 1)
    dots = jnp.sum(grad_probs * probs, axis=1, keepdims=True)
    grad_scores = (probs * (grad_probs - dots)).astype(bf16)
    dq_ref[...] = (one_pair(matmul(grad_scores, keys)) * SCALE).astype(bf16)


def column_kernel(me_ref, k_ref, v_ref, q_ref, a_ref, don_ref, dof_ref, lse_ref, bias_ref, dk_ref, dv_ref):
    me = me_ref[0]

    def ordered(ref):
        return jnp.concatenate(
            [ref[relative_device(me, place), 0, 0] for place in range(SHARDS)], 0
        )

    queries, attended, grads = ordered(q_ref), ordered(a_ref), rows_of(don_ref, dof_ref)
    rows = k_ref.shape[0]
    bias = bias_ref[0]
    lse = lse_ref[0, 0]
    product = attended.astype(f32) * grads.astype(f32)
    sides = (
        lax.broadcasted_iota(jnp.int32, (8, 128), 1) // HEAD_DIM
        == lax.broadcasted_iota(jnp.int32, (8, 128), 0)
    ).astype(bf16)
    high = product.astype(bf16)
    low = (product - high.astype(f32)).astype(bf16)
    dots = contract(sides, high, 1, 1) + contract(sides, low, 1, 1)
    spread = lambda pair: jnp.concatenate(
        [jnp.broadcast_to(pair[:1], (rows, pair.shape[1])), jnp.broadcast_to(pair[1:2], (rows, pair.shape[1]))], 0
    )
    scores = contract(two_heads(k_ref[...]), queries, 1, 1) * SCALE
    probs = jnp.exp(scores + jnp.concatenate([bias, bias], 0) - spread(lse))
    grad_probs = contract(two_heads(v_ref[...]), grads, 1, 1)
    grad_scores = (probs * (grad_probs - spread(dots))).astype(bf16)
    dk_ref[...] = (one_pair(matmul(grad_scores, queries)) * SCALE).astype(bf16)
    dv_ref[...] = one_pair(matmul(probs.astype(bf16), grads)).astype(bf16)


def kernel_call(body, n_matmuls, in_specs, out_specs, out_shape, operands):
    steps = 2 * PAIRS
    return pl.pallas_call(
        body,
        grid=(2, PAIRS),
        in_specs=in_specs,
        out_specs=out_specs,
        out_shape=out_shape,
        compiler_params=pltpu.CompilerParams(vmem_limit_bytes=32 * 1024 * 1024),
        cost_estimate=pl.CostEstimate(
            flops=steps * n_matmuls * 2 * 128 * 128 * 1024 * 4,
            bytes_accessed=steps * 2 * 1024 * 128 * 2,
            transcendentals=steps * 128 * 1024,
        ),
    )(*operands)


def own_spec(rows):
    return pl.BlockSpec((rows, 128), lambda m, h: (m, h))


def all_spec(kind, rows):
    return pl.BlockSpec((8, 1, 1, rows, 128), lambda m, h: (0, kind, m, 0, h))


def shards(
    inputs,
    segment_ids,
    sequence_order,
    ln1_gain,
    ln1_bias,
    w_qkv,
    qv_bias,
    w_out,
    out_bias,
    ln2_gain,
    ln2_bias,
    w_fc,
    fc_bias,
    w_proj,
    proj_bias,
    cotangent,
):
    section_index = lax.axis_index("section")
    me = lax.axis_index("fsdp")
    is_first = section_index == 0
    is_last = section_index == 1
    micro, span = inputs.shape[0], inputs.shape[1]
    tokens = micro * span
    seq_len = segment_ids.shape[1]

    def rows_padded(block):
        return jnp.pad(block, ((0, PROWS - block.shape[0]), (0, 0)))

    later = jnp.concatenate(
        [w_proj[0]]
        + [rows_padded(w_fc[0][:, j * D : (j + 1) * D]) for j in range(SPLITS)]
        + [rows_padded(w_out[0])],
        0,
    )
    later_all = lax.all_gather(later, "fsdp", axis=0, tiled=False)
    vectors = jnp.concatenate(
        [ln1_gain[0], ln1_bias[0], out_bias[0], ln2_gain[0], ln2_bias[0], proj_bias[0], qv_bias[0], fc_bias[0]]
    )
    vector_rows = jnp.pad(vectors[None], ((0, 7), (0, LANES - vectors.shape[0])))
    first = jnp.concatenate(
        [
            jnp.pad(w_qkv[0][:, j * D : (j + 1) * D], ((0, PROWS - DROWS), (0, LANES - D)))
            for j in range(3)
        ]
        + [vector_rows],
        0,
    )
    first_all = jnp.concatenate(gather_both(first), 0)
    weights_q, weights_k, weights_v = [
        first_all[:, j * PROWS : (j + 1) * PROWS].reshape(KPAD, LANES) for j in range(3)
    ]
    place_iota = jnp.arange(SHARDS)
    to_absolute = (relative_device(me, place_iota)[None, :] == place_iota[:, None]).astype(bf16)
    vector_all = matmul(to_absolute, first_all[:, 3 * PROWS])

    def vector(start, size):
        return vector_all[:, start : start + size].reshape(SHARDS * size)

    gain_one, bias_one, out_shift, gain_two, bias_two, proj_shift = [
        vector(j * DROWS, DROWS) for j in range(6)
    ]
    qv_full = vector(6 * DROWS, 2 * DROWS)
    fc_shift = vector(8 * DROWS, FROWS).reshape(SPLITS, 1, D)
    shift_q = jnp.pad(qv_full[:D], (0, LANES - D))
    shift_v = jnp.pad(qv_full[D:], (0, LANES - D))

    full_proj = later_all[:, :FROWS].reshape(SPLITS, D, D)
    full_fc = (
        later_all[:, FROWS : FROWS + SPLITS * PROWS]
        .reshape(SHARDS, SPLITS, PROWS, D)
        .transpose(1, 0, 2, 3)
        .reshape(SPLITS, KPAD, D)
    )
    full_out = later_all[:, FROWS + SPLITS * PROWS :].reshape(KPAD, D)

    place_rel = placing(me, True)
    place_abs = placing(me, False)

    swapped = sequence_order[0, 0] == 1
    ordered_inputs = jnp.where(swapped, inputs[::-1], inputs).reshape(tokens, D)
    ordered_segments = jnp.where(swapped, segment_ids[::-1], segment_ids)
    by_block = ordered_segments.reshape(micro, SHARDS, span)
    rel_devices = relative_device(me, place_iota)
    seg_rel = jnp.take(by_block, rel_devices, axis=1).reshape(micro, 1, seq_len)
    seg_own = lax.dynamic_index_in_dim(by_block, me, 1, keepdims=False)[:, :, None]
    pos_rel = (rel_devices[:, None] * span + jnp.arange(span)[None]).reshape(1, 1, seq_len)
    pos_own = (me * span + jnp.arange(span)).reshape(1, span, 1)
    same = seg_rel == seg_own
    row_bias = jnp.where(same & (pos_rel <= pos_own), 0.0, -1e30).astype(f32)
    column_bias = jnp.where(same & (pos_own <= pos_rel), 0.0, -1e30).astype(f32)

    bias_spec = pl.BlockSpec((1, span, seq_len), lambda m, h: (m, 0, 0))
    lse_spec = pl.BlockSpec((1, 1, 8, 128), lambda m, h: (m, h, 0, 0))
    kv_specs = [all_spec(0, span), all_spec(0, span), all_spec(1, span), all_spec(1, span)]
    token_shape = jax.ShapeDtypeStruct((tokens, LANES), bf16)

    def forward_layer(layer_in):
        layer_wide = layer_in.astype(f32)
        normed_one = layer_norm(layer_wide, gain_one, bias_one).astype(bf16)
        placed_one = matmul(normed_one, place_rel).astype(bf16)
        keys = matmul(placed_one, weights_k).astype(bf16)
        values = (matmul(placed_one, weights_v) + shift_v).astype(bf16)
        kv_near, kv_far = gather_both(jnp.concatenate([keys, values], 0))
        kv_near = kv_near.reshape(8, 2, micro, span, LANES)
        kv_far = kv_far.reshape(8, 2, micro, span, LANES)
        queries = (matmul(placed_one, weights_q) + shift_q).astype(bf16)
        attended, log_total = kernel_call(
            forward_kernel,
            2,
            [own_spec(span)] + kv_specs + [bias_spec],
            [own_spec(span), lse_spec],
            [token_shape, jax.ShapeDtypeStruct((micro, PAIRS, 8, 128), f32)],
            (queries, kv_near, kv_far, kv_near, kv_far, row_bias),
        )
        placed_att = matmul(attended[:, :D], place_abs).astype(bf16)
        hidden = layer_wide + matmul(placed_att, full_out) + out_shift
        normed_two = layer_norm(hidden, gain_two, bias_two).astype(bf16)
        placed_two = matmul(normed_two, place_abs).astype(bf16)
        pre_act = [matmul(placed_two, full_fc[j]) + fc_shift[j] for j in range(SPLITS)]
        total = hidden + proj_shift
        for j in range(SPLITS):
            total = total + matmul(gelu_tanh(pre_act[j]).astype(bf16), full_proj[j])
        out_low = total.astype(bf16)
        return out_low, (
            layer_wide, normed_one, queries, keys, values, kv_near, kv_far,
            attended, log_total, hidden, normed_two, pre_act,
        )

    sent_on, _ = forward_layer(ordered_inputs)
    received = lax.ppermute(sent_on, "section", [(0, 1)])
    layer_in = jnp.where(is_first, ordered_inputs, received)
    out_low, kept = forward_layer(layer_in)
    (
        layer_wide, normed_one, queries, keys, values, kv_near, kv_far,
        attended, log_total, hidden, normed_two, pre_act,
    ) = kept

    lse_own = log_total[:, :, 0]
    part_one = lax.reduce_precision(lse_own, 8, 7)
    part_two = lax.reduce_precision(lse_own - part_one, 8, 7)
    part_three = lse_own - part_one - part_two
    lse_rows = jnp.stack([part_one, part_two, part_three]).astype(bf16).reshape(6, LANES)
    qa_all = lax.all_gather(
        jnp.concatenate([queries, attended, lse_rows, jnp.zeros((2, LANES), bf16)], 0), "fsdp", axis=0
    )
    lse_parts = qa_all[:, 2 * tokens : 2 * tokens + 6].reshape(SHARDS, 3, micro, PAIRS, 2, span).astype(f32)
    lse_all = lse_parts[:, 0] + lse_parts[:, 1] + lse_parts[:, 2]
    lse_all = jnp.take(lse_all, rel_devices, axis=0).transpose(1, 2, 3, 0, 4).reshape(micro, PAIRS, 2, seq_len)
    lse_all = jnp.pad(lse_all, ((0, 0), (0, 0), (0, 6), (0, 0)))
    qa_tokens = qa_all[:, : 2 * tokens].reshape(SHARDS, 2, micro, span, LANES)
    nn_all = lax.all_gather(jnp.concatenate([normed_one, normed_two], 0), "fsdp", axis=0)
    me_scalar = me.astype(jnp.int32).reshape(1)

    def backward_layer(grad_out):
        grad_wide = grad_out.astype(f32)
        grad_pre = []
        grad_placed_two = 0.0
        for j in range(SPLITS):
            grad_act = contract(grad_out, full_proj[j], 1, 1)
            _, gelu_back = jax.vjp(gelu_tanh, pre_act[j])
            grad_pre.append(gelu_back(grad_act)[0].astype(bf16))
            grad_placed_two = grad_placed_two + contract(grad_pre[j], full_fc[j], 1, 1)
        _, norm_two_back = jax.vjp(layer_norm, hidden, gain_two, bias_two)
        grad_hidden_ln, grad_gain_two, grad_bias_two = norm_two_back(unplaced(grad_placed_two, place_abs))
        grad_hidden = grad_wide + grad_hidden_ln
        grad_branch = grad_hidden.astype(bf16)
        grad_att = contract(contract(grad_branch, full_out, 1, 1).astype(bf16), place_abs, 1, 1).astype(bf16)
        grad_att = jnp.pad(grad_att, ((0, 0), (0, LANES - D)))
        do_near, do_far = gather_both(grad_att)
        do_near = do_near.reshape(8, 1, micro, span, LANES)
        do_far = do_far.reshape(8, 1, micro, span, LANES)
        grad_q = kernel_call(
            row_kernel,
            3,
            [own_spec(span), own_spec(span), lse_spec] + kv_specs + [bias_spec],
            own_spec(span),
            token_shape,
            (queries, grad_att, log_total, kv_near, kv_far, kv_near, kv_far, row_bias),
        )
        whole = lambda kind: pl.BlockSpec((SHARDS, 1, 1, span, 128), lambda m, h: (0, kind, m, 0, h))
        grad_k, grad_v = kernel_call(
            column_kernel,
            5,
            [pl.BlockSpec(memory_space=pltpu.SMEM), own_spec(span), own_spec(span), whole(0), whole(1)]
            + [all_spec(0, span), all_spec(0, span)]
            + [pl.BlockSpec((1, 1, 8, seq_len), lambda m, h: (m, h, 0, 0)), bias_spec],
            [own_spec(span), own_spec(span)],
            [token_shape, token_shape],
            (me_scalar, keys, values, qa_tokens, qa_tokens, do_near, do_far, lse_all, column_bias),
        )
        grad_placed_one = (
            contract(grad_q, weights_q, 1, 1) + contract(grad_k, weights_k, 1, 1) + contract(grad_v, weights_v, 1, 1)
        )
        _, norm_one_back = jax.vjp(layer_norm, layer_wide, gain_one, bias_one)
        grad_in_ln, grad_gain_one, grad_bias_one = norm_one_back(unplaced(grad_placed_one, place_rel))
        grad_input = (grad_hidden + grad_in_ln).astype(bf16)
        norm_grads = jnp.stack([grad_gain_one, grad_bias_one, grad_gain_two, grad_bias_two])
        return grad_input, grad_branch, (grad_q, grad_k, grad_v), norm_grads

    own_cotangent = cotangent.reshape(tokens, D)
    sent_back, _, _, _ = backward_layer(own_cotangent)
    received_grad = lax.ppermute(sent_back, "section", [(1, 0)])
    grad_out = jnp.where(is_last, own_cotangent, received_grad)

    go_all = lax.all_gather(grad_out, "fsdp", axis=0).reshape(SHARDS * tokens, D)
    n1_all = nn_all[:, :tokens].reshape(SHARDS * tokens, D)
    n2_all = nn_all[:, tokens:].reshape(SHARDS * tokens, D)
    fc_block = lax.dynamic_index_in_dim(full_fc, me // 4, 0, keepdims=False)
    fc_own = lax.dynamic_slice_in_dim(fc_block, (me % 4) * FROWS, FROWS, 1)
    fc_own = matmul(place_abs, fc_own).astype(bf16)
    pre_own = matmul(n2_all, fc_own) + fc_bias[0].astype(f32)
    activ_own, gelu_own_back = jax.vjp(gelu_tanh, pre_own)
    grad_pre_own = gelu_own_back(contract(go_all, w_proj[0], 1, 1))[0].astype(bf16)
    grad_proj_w = contract(activ_own.astype(bf16), go_all, 0, 0).astype(bf16)
    grad_fc_w = contract(n2_all, grad_pre_own, 0, 0).astype(bf16)
    grad_fc_b = jnp.sum(grad_pre_own.astype(f32), axis=0)
    grad_proj_b = lax.dynamic_slice_in_dim(jnp.sum(go_all.astype(f32), axis=0), me * DROWS, DROWS)
    own_vectors = jnp.concatenate([grad_fc_b, grad_proj_b, jnp.zeros((D - FROWS - DROWS,), f32)]).astype(bf16)
    proj_rows = jnp.concatenate([grad_proj_w, jnp.pad(own_vectors[None], ((0, 7), (0, 0)))], 0)
    proj_total = lax.psum(proj_rows, "replica")

    grad_input, grad_branch, grad_qkv, norm_grads = backward_layer(grad_out)

    wide = jnp.concatenate([g[:, :D] for g in grad_qkv] + [grad_branch], 1)
    columns = lax.all_to_all(
        wide.reshape(tokens, SHARDS, FROWS).transpose(1, 0, 2), "fsdp", 0, 0
    ).reshape(SHARDS * tokens, FROWS)
    att_all = qa_all[:, tokens : 2 * tokens, :D].reshape(SHARDS * tokens, D)
    left = jnp.where(me < 12, n1_all, att_all)
    grad_columns = contract(left, columns, 0, 0).astype(bf16)
    column_sums = jnp.sum(columns.astype(f32), axis=0).astype(bf16)

    rows = jnp.concatenate(
        [
            grad_columns.reshape(SHARDS, DROWS, FROWS),
            grad_fc_w.reshape(SHARDS, DROWS, FROWS),
            norm_grads.astype(bf16).reshape(4, SHARDS, DROWS).transpose(1, 2, 0),
        ],
        2,
    )
    width = 640
    rows = jnp.pad(rows, ((0, 0), (0, 0), (0, width - rows.shape[2])))
    sums_row = jnp.broadcast_to(jnp.pad(column_sums, (0, width - FROWS))[None, None], (SHARDS, 1, width))
    rows = jnp.concatenate([rows, sums_row, jnp.zeros((SHARDS, PROWS - DROWS - 1, width), bf16)], 1)
    got = lax.all_to_all(rows, "fsdp", 0, 0)

    z = lax.axis_index("replica")
    quarter = got.reshape(4, 4, PROWS, width)
    pick = lambda k: lax.dynamic_index_in_dim(quarter, z ^ k, 0, keepdims=False)
    swap = lambda v, k: lax.ppermute(v, "replica", [(j, j ^ k) for j in range(4)])
    total = pick(0).astype(f32)
    for term in [swap(pick(k), k) for k in (1, 3, 2)]:
        total = total + term.astype(f32)
    total = total.astype(bf16)
    finished = jnp.stack([total] + [swap(total, k) for k in (1, 2, 3)])
    finished = jnp.take(finished, z ^ jnp.arange(4), axis=0).reshape(SHARDS, PROWS, width).astype(f32)

    def joined(block):
        return block.transpose(1, 0, 2).reshape(block.shape[1], -1)

    grad_w_qkv = joined(finished[:12, :DROWS, :FROWS])
    grad_w_out = joined(finished[12:, :DROWS, :FROWS])
    grad_w_fc = joined(finished[:, :DROWS, FROWS : 2 * FROWS])
    norm_sums = jnp.sum(finished[:, :DROWS, 2 * FROWS : 2 * FROWS + 4], axis=0)
    sums = finished[:, DROWS, :FROWS].reshape(SHARDS * FROWS)
    qv_sums = jnp.concatenate([sums[:D], sums[2 * D : 3 * D]])
    grad_qv_b = lax.dynamic_slice_in_dim(qv_sums, me * 2 * DROWS, 2 * DROWS)
    grad_out_b = lax.dynamic_slice_in_dim(sums, 3 * D + me * DROWS, DROWS)
    proj_total = proj_total.astype(f32)
    totals = (
        norm_sums[:, 0],
        norm_sums[:, 1],
        grad_w_qkv,
        grad_qv_b,
        grad_w_out,
        grad_out_b,
        norm_sums[:, 2],
        norm_sums[:, 3],
        grad_w_fc,
        proj_total[FROWS, :FROWS],
        proj_total[:FROWS],
        proj_total[FROWS, FROWS : FROWS + DROWS],
    )
    activations = out_low.reshape(1, micro, span, D)
    input_grads = grad_input.reshape(1, micro, span, D)
    return (activations, input_grads) + tuple((total[None] for total in totals))


def solution(mesh):
    return jax.shard_map(
        shards,
        mesh=mesh,
        in_specs=(
            P("replica", "fsdp", None),
            P("replica", None),
            P("replica", None),
            P("section", "fsdp"),
            P("section", "fsdp"),
            P("section", "fsdp", None),
            P("section", "fsdp"),
            P("section", "fsdp", None),
            P("section", "fsdp"),
            P("section", "fsdp"),
            P("section", "fsdp"),
            P("section", "fsdp", None),
            P("section", "fsdp"),
            P("section", "fsdp", None),
            P("section", "fsdp"),
            P("replica", "fsdp", None),
        ),
        out_specs=(
            P("section", "replica", "fsdp", None),
            P("section", "replica", "fsdp", None),
            P("section", "fsdp"),
            P("section", "fsdp"),
            P("section", "fsdp", None),
            P("section", "fsdp"),
            P("section", "fsdp", None),
            P("section", "fsdp"),
            P("section", "fsdp"),
            P("section", "fsdp"),
            P("section", "fsdp", None),
            P("section", "fsdp"),
            P("section", "fsdp", None),
            P("section", "fsdp"),
        ),
        check_vma=False,
    )
```

```python
import jax
import jax.numpy as jnp
from jax import lax
from jax.experimental import pallas as pl
from jax.experimental.pallas import tpu as pltpu
from jax.sharding import PartitionSpec as P

D = 1088
HEADS = 17
HEAD_DIM = 64
FF = 4352
SHARDS = 16
DROWS = D // SHARDS
PROWS = 80
KPAD = SHARDS * PROWS
LANES = 1152
PAIRS = 9
FROWS = FF // SHARDS
SPLITS = FF // D
SCALE = HEAD_DIM ** (-0.5)

HALF = KPAD // 2
OUT_AT = SPLITS * PROWS
PROJ_AT = OUT_AT + PROWS
GELU_C = 0.7978845608028654
GELU_A = 0.044715

epsilon = 1e-05
bf16 = jnp.bfloat16
f32 = jnp.float32


def xor_pairs(k):
    return [(i, i ^ k) for i in range(SHARDS)]


def moved(value, k):
    return lax.ppermute(value, "fsdp", xor_pairs(k))


def gather_near(x, beside=None):
    half = x.shape[0] // 2
    blocks = {0: x, 4: moved(x, 4), 12: moved(x, 12), 2: moved(x, 2)}
    result = None
    if beside is not None:
        blocks[4], blocks[12], blocks[2], result = lax.optimization_barrier(
            (blocks[4], blocks[12], blocks[2], beside())
        )
    blocks[8] = jnp.concatenate([moved(blocks[4][:half], 12), moved(blocks[12][half:], 4)], 0)
    blocks[6] = moved(blocks[2], 4)
    blocks[14] = moved(blocks[2], 12)
    blocks[10] = moved(blocks[8], 2)
    return jnp.stack([blocks[k] for k in range(0, SHARDS, 2)]), result


def gather_both(x):
    near, _ = gather_near(x)
    return near, moved(near, 1)


def relative_device(me, place):
    return me ^ (2 * (place % 8) + place // 8)


def placing(me, relative):
    column = lax.broadcasted_iota(jnp.int32, (1, KPAD), 1)
    place, row = column // PROWS, column % PROWS
    owner = relative_device(me, place) if relative else place
    source = jnp.where(row < DROWS, owner * DROWS + row, -1)
    return (lax.broadcasted_iota(jnp.int32, (D, KPAD), 0) == source).astype(bf16)


def matmul(left, right):
    return jnp.dot(left, right, preferred_element_type=f32)


def contract(left, right, ldim, rdim):
    return lax.dot_general(left, right, (((ldim,), (rdim,)), ((), ())), preferred_element_type=f32)


def split_two(values):
    high = lax.reduce_precision(values, 8, 7)
    return high.astype(bf16), (values - high).astype(bf16)


def unplaced(values, place):
    rows = values.shape[0]
    both = contract(jnp.concatenate(split_two(values), 0), place, 1, 1)
    return both[:rows] + both[rows:]


def two_heads(block):
    lane = lax.broadcasted_iota(jnp.int32, block.shape, 1)
    zero = jnp.zeros_like(block)
    return jnp.concatenate(
        [jnp.where(lane < HEAD_DIM, block, zero), jnp.where(lane < HEAD_DIM, zero, block)], 0
    )


def one_pair(both):
    rows = both.shape[0] // 2
    lane = lax.broadcasted_iota(jnp.int32, (rows, 128), 1)
    return jnp.where(lane < HEAD_DIM, both[:rows], both[rows:])


def rows_of(near_ref, far_ref):
    return jnp.concatenate(
        [near_ref[...].reshape(-1, 128), far_ref[...].reshape(-1, 128)], 0
    )


def forward_kernel(q_ref, kn_ref, kf_ref, vn_ref, vf_ref, bias_ref, out_ref, lse_ref):
    bias = bias_ref[0]
    keys, values = rows_of(kn_ref, kf_ref), rows_of(vn_ref, vf_ref)
    scores = contract(two_heads(q_ref[...]), keys, 1, 1) * SCALE
    scores = scores + jnp.concatenate([bias, bias], 0)
    top = jnp.max(scores, axis=1, keepdims=True)
    shifted = jnp.exp(scores - top)
    total = jnp.sum(shifted, axis=1, keepdims=True)
    probs = (shifted / total).astype(bf16)
    out_ref[...] = one_pair(matmul(probs, values)).astype(bf16)
    lse = top + jnp.log(total)
    lse_ref[0, 0] = jnp.transpose(jnp.broadcast_to(lse, (128, 128)))[:8]


def row_kernel(q_ref, do_ref, lse_ref, kn_ref, kf_ref, vn_ref, vf_ref, bias_ref, dq_ref):
    bias = bias_ref[0]
    keys, values = rows_of(kn_ref, kf_ref), rows_of(vn_ref, vf_ref)
    lse = jnp.transpose(jnp.broadcast_to(lse_ref[0, 0][:1], (128, 128)))[:, :1]
    scores = contract(two_heads(q_ref[...]), keys, 1, 1) * SCALE
    scores = scores + jnp.concatenate([bias, bias], 0)
    probs = jnp.exp(scores - lse)
    grad_probs = contract(two_heads(do_ref[...]), values, 1, 1)
    dots = jnp.sum(grad_probs * probs, axis=1, keepdims=True)
    grad_scores = (probs * (grad_probs - dots)).astype(bf16)
    dq_ref[...] = (one_pair(matmul(grad_scores, keys)) * SCALE).astype(bf16)


def normalized(values):
    centred = values - jnp.mean(values, axis=1, keepdims=True)
    scale = lax.rsqrt(jnp.mean(centred * centred, axis=1, keepdims=True) + epsilon)
    return centred * scale, scale


def norm_back(values, gain, grad):
    z, scale = normalized(values)
    weighted = grad * gain
    by_values = scale * (
        weighted
        - jnp.mean(weighted, axis=1, keepdims=True)
        - z * jnp.mean(weighted * z, axis=1, keepdims=True)
    )
    row = lax.broadcasted_iota(jnp.int32, (8, D), 0)
    gain_sum = jnp.sum(grad * z, axis=0, keepdims=True)
    bias_sum = jnp.sum(grad, axis=0, keepdims=True)
    return by_values, jnp.where(row == 0, gain_sum, jnp.where(row == 1, bias_sum, 0.0))


def gelu_parts(v):
    t = jnp.tanh(GELU_C * (v + GELU_A * v * v * v))
    return 0.5 * v * (1.0 + t), t


def gelu_slope(v, t):
    return 0.5 * (1.0 + t) + 0.5 * v * (1.0 - t * t) * (GELU_C * (1.0 + 3.0 * GELU_A * v * v))


def unplaced(values, place):
    rows = values.shape[0]
    high = values.astype(bf16)
    low = (values - high.astype(f32)).astype(bf16)
    both = contract(jnp.concatenate([high, low], 0), place, 1, 1)
    return both[:rows] + both[rows:]


def input_weight(near_ref, far_ref, j):
    rows = slice(j * PROWS, (j + 1) * PROWS)
    return near_ref[:, rows, :].reshape(HALF, LANES), far_ref[:, rows, :].reshape(HALF, LANES)


def qkv_kernel(x_ref, near_ref, far_ref, place_ref, gain_ref, bias_ref, sq_ref, sv_ref, n1_ref, q_ref, kv_ref):
    z, _ = normalized(x_ref[...].astype(f32))
    normed = (z * gain_ref[...] + bias_ref[...]).astype(bf16)
    n1_ref[...] = normed
    placed = matmul(normed, place_ref[...]).astype(bf16)
    rows = placed.shape[0]

    def product(j):
        near, far = input_weight(near_ref, far_ref, j)
        return matmul(placed[:, :HALF], near) + matmul(placed[:, HALF:], far)

    kv_ref[:rows] = product(1).astype(bf16)
    kv_ref[rows:] = (product(2) + sv_ref[...]).astype(bf16)
    q_ref[...] = (product(0) + sq_ref[...]).astype(bf16)


def qkv_back_kernel(dq_ref, dk_ref, dv_ref, near_ref, far_ref, place_ref, x_ref, gain_ref, gh_ref, gin_ref, sums_ref):
    near_sum, far_sum = 0.0, 0.0
    for j, ref in enumerate((dq_ref, dk_ref, dv_ref)):
        near, far = input_weight(near_ref, far_ref, j)
        near_sum = near_sum + contract(ref[...], near, 1, 1)
        far_sum = far_sum + contract(ref[...], far, 1, 1)
    grad = unplaced(jnp.concatenate([near_sum, far_sum], 1), place_ref[...])
    by_input, sums_ref[...] = norm_back(x_ref[...].astype(f32), gain_ref[...], grad)
    gin_ref[...] = (gh_ref[...] + by_input).astype(bf16)


def weight_copies(all_ref, fc_buf, out_buf, proj_buf, sems):
    out_copy = pltpu.make_async_copy(all_ref.at[:, pl.ds(OUT_AT, PROWS), :], out_buf, sems.at[0])
    fc = [
        pltpu.make_async_copy(all_ref.at[:, pl.ds(j * PROWS, PROWS), :], fc_buf.at[j], sems.at[1 + j])
        for j in range(SPLITS)
    ]
    proj = [
        pltpu.make_async_copy(
            all_ref.at[pl.ds(4 * j, 4), pl.ds(PROJ_AT, FROWS), :], proj_buf.at[j], sems.at[1 + SPLITS + j]
        )
        for j in range(SPLITS)
    ]
    return out_copy, fc, proj


def ffn_kernel(
    att_ref, x_ref, place_ref, os_ref, gain_ref, bias_ref, ps_ref, fs_ref, all_ref,
    hidden_ref, n2_ref, pre_ref, out_ref, fc_buf, out_buf, proj_buf, sems,
):
    out_copy, fc, proj = weight_copies(all_ref, fc_buf, out_buf, proj_buf, sems)
    out_copy.start()
    for j in range(SPLITS):
        fc[j].start()
        proj[j].start()
    place = place_ref[...]
    placed = matmul(att_ref[:, :D], place).astype(bf16)
    out_copy.wait()
    hidden = x_ref[...].astype(f32) + matmul(placed, out_buf[...].reshape(KPAD, D)) + os_ref[...]
    hidden_ref[...] = hidden
    z, _ = normalized(hidden)
    normed = (z * gain_ref[...] + bias_ref[...]).astype(bf16)
    n2_ref[...] = normed
    placed = matmul(normed, place).astype(bf16)
    total = hidden + ps_ref[...]
    for j in range(SPLITS):
        fc[j].wait()
        pre = matmul(placed, fc_buf[j].reshape(KPAD, D)) + fs_ref[j : j + 1]
        pre_ref[j] = pre
        activ, _ = gelu_parts(pre)
        proj[j].wait()
        total = total + matmul(activ.astype(bf16), proj_buf[j].reshape(D, D))
    out_ref[...] = total.astype(bf16)


def ffn_back_kernel(
    go_ref, pre_ref, hidden_ref, place_ref, gain_ref, all_ref,
    gh_ref, gb_ref, ga_ref, sums_ref, fc_buf, out_buf, proj_buf, sems,
):
    out_copy, fc, proj = weight_copies(all_ref, fc_buf, out_buf, proj_buf, sems)
    for j in range(SPLITS):
        proj[j].start()
        fc[j].start()
    out_copy.start()
    grad_out = go_ref[...]
    placed = 0.0
    for j in range(SPLITS):
        pre = pre_ref[j]
        _, t = gelu_parts(pre)
        slope = gelu_slope(pre, t)
        proj[j].wait()
        grad_pre = (contract(grad_out, proj_buf[j].reshape(D, D), 1, 1) * slope).astype(bf16)
        fc[j].wait()
        placed = placed + contract(grad_pre, fc_buf[j].reshape(KPAD, D), 1, 1)
    place = place_ref[...]
    by_hidden, sums_ref[...] = norm_back(hidden_ref[...], gain_ref[...], unplaced(placed, place))
    grad_hidden = grad_out.astype(f32) + by_hidden
    gh_ref[...] = grad_hidden
    branch = grad_hidden.astype(bf16)
    gb_ref[...] = branch
    out_copy.wait()
    grad_att = contract(branch, out_buf[...].reshape(KPAD, D), 1, 1).astype(bf16)
    ga_ref[...] = jnp.zeros_like(ga_ref)
    ga_ref[:, :D] = contract(grad_att, place, 1, 1).astype(bf16)


def column_kernel(me_ref, k_ref, v_ref, q_ref, a_ref, lse_ref, don_ref, dof_ref, bias_ref, dk_ref, dv_ref):
    me = me_ref[0]
    owners = [relative_device(me, place) for place in range(SHARDS)]
    queries = jnp.concatenate([q_ref[owner] for owner in owners], 0)
    attended = jnp.concatenate([a_ref[owner] for owner in owners], 0)
    grads = rows_of(don_ref, dof_ref)
    rows = k_ref.shape[0]
    span = q_ref.shape[1]
    bias = bias_ref[0]
    micro = pl.program_id(0)
    term_row = lax.broadcasted_iota(jnp.int32, (16, 128), 0)
    place_of = (
        lax.broadcasted_iota(jnp.int32, (SHARDS, SHARDS * span), 1) // span
        == lax.broadcasted_iota(jnp.int32, (SHARDS, SHARDS * span), 0)
    ).astype(bf16)
    spread_lse = 0.0
    for term in range(3):
        picked = [
            jnp.sum(jnp.where(term_row == 2 * term + micro, lse_ref[owner].astype(f32), 0.0), axis=0, keepdims=True)
            for owner in owners
        ]
        spread_lse = spread_lse + contract(jnp.concatenate(picked, 0).astype(bf16), place_of, 0, 0)
    on_diagonal = (
        lax.broadcasted_iota(jnp.int32, spread_lse.shape, 0) % span
        == lax.broadcasted_iota(jnp.int32, spread_lse.shape, 1) % span
    )
    spread_lse = jnp.where(on_diagonal, spread_lse, 0.0)
    lse_a = jnp.sum(spread_lse[:span], axis=0, keepdims=True)
    lse_b = jnp.sum(spread_lse[span:], axis=0, keepdims=True)
    product = attended.astype(f32) * grads.astype(f32)
    sides = (
        lax.broadcasted_iota(jnp.int32, (8, 128), 1) // HEAD_DIM
        == lax.broadcasted_iota(jnp.int32, (8, 128), 0)
    ).astype(bf16)
    high = product.astype(bf16)
    low = (product - high.astype(f32)).astype(bf16)
    dots = contract(sides, high, 1, 1) + contract(sides, low, 1, 1)

    def spread(row_a, row_b):
        return jnp.concatenate(
            [jnp.broadcast_to(row_a, (rows, row_a.shape[1])), jnp.broadcast_to(row_b, (rows, row_b.shape[1]))], 0
        )

    scores = contract(two_heads(k_ref[...]), queries, 1, 1) * SCALE
    probs = jnp.exp(scores + jnp.concatenate([bias, bias], 0) - spread(lse_a, lse_b))
    grad_probs = contract(two_heads(v_ref[...]), grads, 1, 1)
    grad_scores = (probs * (grad_probs - spread(dots[:1], dots[1:2]))).astype(bf16)
    dk_ref[...] = (one_pair(matmul(grad_scores, queries)) * SCALE).astype(bf16)
    dv_ref[...] = one_pair(matmul(probs.astype(bf16), grads)).astype(bf16)


def hidden_units_kernel(n2_ref, go_ref, fc_ref, fb_ref, proj_ref, gp_ref, gf_out_ref, bsum_ref, osum_ref):
    step = pl.program_id(0)

    @pl.when(step == 0)
    def _():
        for ref in (gp_ref, gf_out_ref, bsum_ref, osum_ref):
            ref[...] = jnp.zeros_like(ref)

    n2 = n2_ref[...].reshape(-1, D)
    go = go_ref[...].reshape(-1, D)
    pre = matmul(n2, fc_ref[...]) + fb_ref[...]
    activ, t = gelu_parts(pre)
    grad_pre = (contract(go, proj_ref[...], 1, 1) * gelu_slope(pre, t)).astype(bf16)
    gp_ref[...] += contract(activ.astype(bf16), go, 0, 0)
    gf_out_ref[...] += contract(n2, grad_pre, 0, 0)
    bsum_ref[...] += jnp.broadcast_to(jnp.sum(grad_pre.astype(f32), axis=0, keepdims=True), bsum_ref.shape)
    osum_ref[...] += jnp.broadcast_to(jnp.sum(go.astype(f32), axis=0, keepdims=True), osum_ref.shape)


def columns_kernel(me_ref, n1_ref, a_ref, cols_ref, grad_ref, sums_ref):
    step = pl.program_id(0)

    @pl.when(step == 0)
    def _():
        grad_ref[...] = jnp.zeros_like(grad_ref)
        sums_ref[...] = jnp.zeros_like(sums_ref)

    att = a_ref[...].reshape(-1, LANES)[:, :D]
    left = jnp.where(me_ref[0] < 12, n1_ref[...].reshape(-1, D), att)
    cols = cols_ref[...].reshape(-1, FROWS)
    grad_ref[...] += contract(left, cols, 0, 0)
    sums_ref[...] += jnp.broadcast_to(jnp.sum(cols.astype(f32), axis=0, keepdims=True), sums_ref.shape)


def params(flops, bytes_accessed, transcendentals=0, vmem=32):
    return dict(
        compiler_params=pltpu.CompilerParams(vmem_limit_bytes=vmem * 1024 * 1024),
        cost_estimate=pl.CostEstimate(
            flops=flops, bytes_accessed=bytes_accessed, transcendentals=transcendentals
        ),
    )


def shape(*dims, dtype=bf16):
    return jax.ShapeDtypeStruct(dims, dtype)


def whole_call(body, out_shape, operands, in_hbm=(), scratch=(), flops=0, bytes_accessed=0, vmem=56):
    vm, hbm = pl.BlockSpec(memory_space=pltpu.VMEM), pl.BlockSpec(memory_space=pl.ANY)
    return pl.pallas_call(
        body,
        in_specs=[hbm if i in in_hbm else vm for i in range(len(operands))],
        out_specs=[vm] * len(out_shape),
        out_shape=out_shape,
        scratch_shapes=list(scratch),
        **params(flops, bytes_accessed, 0, vmem),
    )(*operands)


def pair_call(body, n_matmuls, in_specs, out_specs, out_shape, operands):
    steps = 2 * PAIRS
    return pl.pallas_call(
        body,
        grid=(2, PAIRS),
        in_specs=in_specs,
        out_specs=out_specs,
        out_shape=out_shape,
        **params(
            steps * n_matmuls * 2 * 128 * 128 * 1024 * 4, steps * 2 * 1024 * 128 * 2, steps * 128 * 1024
        ),
    )(*operands)


def own_spec(rows):
    return pl.BlockSpec((rows, 128), lambda m, h: (m, h))


def all_spec(kind, rows):
    return pl.BlockSpec((8, 1, 1, rows, 128), lambda m, h: (0, kind, m, 0, h))


def shards(
    inputs,
    segment_ids,
    sequence_order,
    ln1_gain,
    ln1_bias,
    w_qkv,
    qv_bias,
    w_out,
    out_bias,
    ln2_gain,
    ln2_bias,
    w_fc,
    fc_bias,
    w_proj,
    proj_bias,
    cotangent,
):
    section_index = lax.axis_index("section")
    me = lax.axis_index("fsdp")
    is_first = section_index == 0
    is_last = section_index == 1
    micro, span = inputs.shape[0], inputs.shape[1]
    tokens = micro * span
    seq_len = segment_ids.shape[1]

    def rows_padded(block):
        return jnp.pad(block, ((0, PROWS - block.shape[0]), (0, 0)))

    later = jnp.concatenate(
        [rows_padded(w_fc[0][:, j * D : (j + 1) * D]) for j in range(SPLITS)]
        + [rows_padded(w_out[0]), w_proj[0]],
        0,
    )
    later_all = lax.all_gather(later, "fsdp", axis=0, tiled=False)
    vectors = jnp.concatenate(
        [ln1_gain[0], ln1_bias[0], out_bias[0], ln2_gain[0], ln2_bias[0], proj_bias[0], qv_bias[0], fc_bias[0]]
    )
    vector_rows = jnp.pad(vectors[None], ((0, 15), (0, LANES - vectors.shape[0])))
    first = jnp.concatenate(
        [
            jnp.pad(w_qkv[0][:, j * D : (j + 1) * D], ((0, PROWS - DROWS), (0, LANES - D)))
            for j in range(3)
        ]
        + [vector_rows],
        0,
    )
    first_near, first_far = gather_both(first)
    place_iota = jnp.arange(SHARDS)
    to_absolute = (relative_device(me, place_iota)[None, :] == place_iota[:, None]).astype(bf16)
    vector_rel = jnp.concatenate([first_near[:, 3 * PROWS], first_far[:, 3 * PROWS]], 0)
    vector_all = matmul(to_absolute, vector_rel)

    def vector(start, size):
        return vector_all[:, start : start + size].reshape(1, SHARDS * size)

    gain_one, bias_one, out_shift, gain_two, bias_two, proj_shift = [
        vector(j * DROWS, DROWS) for j in range(6)
    ]
    qv_full = vector(6 * DROWS, 2 * DROWS)
    fc_shift = vector(8 * DROWS, FROWS).reshape(SPLITS, D)
    shift_q = jnp.pad(qv_full[:, :D], ((0, 0), (0, LANES - D)))
    shift_v = jnp.pad(qv_full[:, D:], ((0, 0), (0, LANES - D)))

    place_rel = placing(me, True)
    place_abs = placing(me, False)

    swapped = sequence_order[0, 0] == 1
    ordered_inputs = jnp.where(swapped, inputs[::-1], inputs).reshape(tokens, D)
    ordered_segments = jnp.where(swapped, segment_ids[::-1], segment_ids)
    by_block = ordered_segments.reshape(micro, SHARDS, span)
    rel_devices = relative_device(me, place_iota)
    seg_rel = jnp.take(by_block, rel_devices, axis=1).reshape(micro, 1, seq_len)
    seg_own = lax.dynamic_index_in_dim(by_block, me, 1, keepdims=False)[:, :, None]
    pos_rel = (rel_devices[:, None] * span + jnp.arange(span)[None]).reshape(1, 1, seq_len)
    pos_own = (me * span + jnp.arange(span)).reshape(1, span, 1)
    same = seg_rel == seg_own
    row_bias = jnp.where(same & (pos_rel <= pos_own), 0.0, -1e30).astype(f32)
    column_bias = jnp.where(same & (pos_own <= pos_rel), 0.0, -1e30).astype(f32)
    me_scalar = me.astype(jnp.int32).reshape(1)

    bias_spec = pl.BlockSpec((1, span, seq_len), lambda m, h: (m, 0, 0))
    lse_spec = pl.BlockSpec((1, 1, 8, 128), lambda m, h: (m, h, 0, 0))
    kv_specs = [all_spec(0, span), all_spec(0, span), all_spec(1, span), all_spec(1, span)]
    token_shape = shape(tokens, LANES)
    buffers = [
        pltpu.VMEM((SPLITS, SHARDS, PROWS, D), bf16),
        pltpu.VMEM((SHARDS, PROWS, D), bf16),
        pltpu.VMEM((SPLITS, 4, FROWS, D), bf16),
        pltpu.SemaphoreType.DMA((1 + 2 * SPLITS,)),
    ]
    ffn_cost = dict(flops=4 * 2 * tokens * D * FF, bytes_accessed=2 * SHARDS * 672 * D, scratch=buffers)
    qkv_cost = dict(flops=4 * 2 * tokens * D * 3 * D, bytes_accessed=2 * SHARDS * 256 * LANES)

    def by_kind(block):
        return block.reshape(8, -1, micro, span, LANES)

    def forward_layer(layer_in):
        normed_one, queries, keys_values = whole_call(
            qkv_kernel,
            [shape(tokens, D), token_shape, shape(2 * tokens, LANES)],
            (layer_in, first_near, first_far, place_rel, gain_one, bias_one, shift_q, shift_v),
            **qkv_cost,
        )
        kv_near, kv_far = [by_kind(b) for b in gather_both(keys_values)]
        attended, log_total = pair_call(
            forward_kernel,
            2,
            [own_spec(span)] + kv_specs + [bias_spec],
            [own_spec(span), lse_spec],
            [token_shape, shape(micro, PAIRS, 8, 128, dtype=f32)],
            (queries, kv_near, kv_far, kv_near, kv_far, row_bias),
        )
        hidden, normed_two, pre_act, out_low = whole_call(
            ffn_kernel,
            [shape(tokens, D, dtype=f32), shape(tokens, D), shape(SPLITS, tokens, D, dtype=f32), shape(tokens, D)],
            (attended, layer_in, place_abs, out_shift, gain_two, bias_two, proj_shift, fc_shift, later_all),
            in_hbm=(8,),
            **ffn_cost,
        )
        return out_low, (normed_one, queries, keys_values, kv_near, kv_far, attended, log_total, hidden, normed_two, pre_act)

    sent_on, _ = forward_layer(ordered_inputs)
    received = lax.ppermute(sent_on, "section", [(0, 1)])
    layer_in = jnp.where(is_first, ordered_inputs, received)
    out_low, kept = forward_layer(layer_in)
    normed_one, queries, keys_values, kv_near, kv_far, attended, log_total, hidden, normed_two, pre_act = kept

    lse_own = log_total[:, :, 0]
    part_one = lax.reduce_precision(lse_own, 8, 7)
    part_two = lax.reduce_precision(lse_own - part_one, 8, 7)
    part_three = lse_own - part_one - part_two
    lse_rows = jnp.stack([part_one, part_two, part_three]).astype(bf16).reshape(6, LANES)
    qa_all = lax.all_gather(
        jnp.concatenate([queries, attended, lse_rows, jnp.zeros((10, LANES), bf16)], 0), "fsdp", axis=0
    )
    nn_all = lax.all_gather(jnp.concatenate([normed_one, normed_two], 0), "fsdp", axis=0)

    def backward_layer(grad_out):
        grad_hidden, grad_branch, grad_att, sums_two = whole_call(
            ffn_back_kernel,
            [shape(tokens, D, dtype=f32), shape(tokens, D), token_shape, shape(8, D, dtype=f32)],
            (grad_out, pre_act, hidden, place_abs, gain_two, later_all),
            in_hbm=(5,),
            **ffn_cost,
        )
        def row_part():
            return pair_call(
                row_kernel,
                3,
                [own_spec(span), own_spec(span), lse_spec] + kv_specs + [bias_spec],
                own_spec(span),
                token_shape,
                (queries, grad_att, log_total, kv_near, kv_far, kv_near, kv_far, row_bias),
            )

        near, grad_q = gather_near(grad_att, row_part)
        do_near, do_far = by_kind(near), by_kind(moved(near, 1))
        own_half = lambda half: pl.BlockSpec((span, 128), lambda m, h: (2 * half + m, h))
        grad_k, grad_v = pair_call(
            column_kernel,
            5,
            [
                pl.BlockSpec(memory_space=pltpu.SMEM),
                own_half(0),
                own_half(1),
                pl.BlockSpec((SHARDS, span, 128), lambda m, h: (0, m, h)),
                pl.BlockSpec((SHARDS, span, 128), lambda m, h: (0, 2 + m, h)),
                pl.BlockSpec((SHARDS, 16, 128), lambda m, h: (0, 16, h)),
            ]
            + [all_spec(0, span), all_spec(0, span), bias_spec],
            [own_spec(span), own_spec(span)],
            [token_shape, token_shape],
            (
                me_scalar, keys_values, keys_values, qa_all, qa_all, qa_all, do_near, do_far, column_bias,
            ),
        )
        grad_input, sums_one = whole_call(
            qkv_back_kernel,
            [shape(tokens, D), shape(8, D, dtype=f32)],
            (grad_q, grad_k, grad_v, first_near, first_far, place_rel, layer_in, gain_one, grad_hidden),
            **qkv_cost,
        )
        norm_grads = jnp.concatenate([sums_one[:2], sums_two[:2]], 0)
        return grad_input, grad_branch, (grad_q, grad_k, grad_v), norm_grads

    own_cotangent = cotangent.reshape(tokens, D)
    sent_back, _, _, _ = backward_layer(own_cotangent)
    received_grad = lax.ppermute(sent_back, "section", [(1, 0)])
    grad_out = jnp.where(is_last, own_cotangent, received_grad)
    go_all = lax.all_gather(grad_out, "fsdp", axis=0)
    grad_input, grad_branch, grad_qkv, norm_grads = backward_layer(grad_out)

    fc_own = lax.dynamic_slice(later_all, (0, (me // 4) * PROWS, (me % 4) * FROWS), (SHARDS, PROWS, FROWS))
    fc_own = fc_own[:, :DROWS].reshape(D, FROWS)
    fixed = lambda *dims: pl.BlockSpec(dims, lambda s: (0,) * len(dims))
    chip = lambda kind, width: pl.BlockSpec((2, tokens, width), lambda s: (s, kind, 0))
    grad_proj_w, grad_fc_w, grad_fc_b, out_sums = pl.pallas_call(
        hidden_units_kernel,
        grid=(8,),
        in_specs=[chip(1, D), chip(0, D), fixed(D, FROWS), fixed(1, FROWS), fixed(FROWS, D)],
        out_specs=[fixed(FROWS, D), fixed(D, FROWS), fixed(8, FROWS), fixed(8, D)],
        out_shape=[shape(FROWS, D, dtype=f32), shape(D, FROWS, dtype=f32), shape(8, FROWS, dtype=f32), shape(8, D, dtype=f32)],
        **params(4 * 4 * 2 * SHARDS * tokens * D * FROWS, 3 * 2 * SHARDS * tokens * D),
    )(nn_all, go_all, fc_own, fc_bias.astype(f32), w_proj[0])
    grad_proj_b = lax.dynamic_slice_in_dim(out_sums[0], me * DROWS, DROWS)
    wide = jnp.concatenate([g[:, :D] for g in grad_qkv] + [grad_branch], 1)
    wide = wide.reshape(tokens, SHARDS, FROWS).transpose(1, 0, 2)
    columns = lax.all_to_all(wide, "fsdp", 0, 0)
    grad_columns, column_sums = pl.pallas_call(
        columns_kernel,
        grid=(8,),
        in_specs=[pl.BlockSpec(memory_space=pltpu.SMEM), chip(0, D), chip(1, LANES), chip(0, FROWS)],
        out_specs=[fixed(D, FROWS), fixed(8, FROWS)],
        out_shape=[shape(D, FROWS, dtype=f32), shape(8, FROWS, dtype=f32)],
        **params(4 * 2 * SHARDS * tokens * D * FROWS, 4 * 2 * SHARDS * tokens * D),
    )(me_scalar, nn_all, qa_all, columns)

    rows = jnp.concatenate(
        [
            grad_columns.astype(bf16).reshape(SHARDS, DROWS, FROWS),
            grad_fc_w.astype(bf16).reshape(SHARDS, DROWS, FROWS),
            norm_grads.astype(bf16).reshape(4, SHARDS, DROWS).transpose(1, 2, 0),
        ],
        2,
    )
    width, height = 640, 72
    rows = jnp.pad(rows, ((0, 0), (0, 0), (0, width - rows.shape[2])))
    sums_row = jnp.broadcast_to(
        jnp.pad(column_sums[0].astype(bf16), (0, width - FROWS))[None, None], (SHARDS, 1, width)
    )
    rows = jnp.concatenate([rows, sums_row, jnp.zeros((SHARDS, height - DROWS - 1, width), bf16)], 1)
    got = lax.all_to_all(rows, "fsdp", 0, 0)

    z = lax.axis_index("replica")
    own_vectors = jnp.concatenate([grad_fc_b[0], grad_proj_b, jnp.zeros((2 * width - FROWS - DROWS,), f32)])
    proj_part = jnp.pad(grad_proj_w.reshape(4, DROWS, D), ((0, 0), (0, 0), (0, 2 * width - D)))
    own_part = jnp.broadcast_to(own_vectors[None, None], (4, height - DROWS, 2 * width))
    proj_part = jnp.concatenate([proj_part, own_part], 1).astype(bf16)
    quarter = jnp.concatenate(
        [got.reshape(4, 4, height, width), proj_part[:, None, :, :width], proj_part[:, None, :, width:]], 1
    )
    pick = lambda k: lax.dynamic_index_in_dim(quarter, z ^ k, 0, keepdims=False)
    swap = lambda v, k: lax.ppermute(v, "replica", [(j, j ^ k) for j in range(4)])
    total = pick(0).astype(f32)
    for term in [swap(pick(k), k) for k in (1, 3, 2)]:
        total = total + term.astype(f32)
    total = total.astype(bf16)
    finished = jnp.stack([total] + [swap(total, k) for k in (1, 2, 3)])
    finished = jnp.take(finished, z ^ jnp.arange(4), axis=0).astype(f32)
    proj_total = jnp.concatenate([finished[:, 4], finished[:, 5]], 2)
    finished = finished[:, :4].reshape(SHARDS, height, width)

    def joined(block):
        return block.transpose(1, 0, 2).reshape(block.shape[1], -1)

    grad_w_qkv = joined(finished[:12, :DROWS, :FROWS])
    grad_w_out = joined(finished[12:, :DROWS, :FROWS])
    grad_w_fc = joined(finished[:, :DROWS, FROWS : 2 * FROWS])
    norm_sums = jnp.sum(finished[:, :DROWS, 2 * FROWS : 2 * FROWS + 4], axis=0)
    sums = finished[:, DROWS, :FROWS].reshape(SHARDS * FROWS)
    qv_sums = jnp.concatenate([sums[:D], sums[2 * D : 3 * D]])
    grad_qv_b = lax.dynamic_slice_in_dim(qv_sums, me * 2 * DROWS, 2 * DROWS)
    grad_out_b = lax.dynamic_slice_in_dim(sums, 3 * D + me * DROWS, DROWS)
    totals = (
        norm_sums[:, 0],
        norm_sums[:, 1],
        grad_w_qkv,
        grad_qv_b,
        grad_w_out,
        grad_out_b,
        norm_sums[:, 2],
        norm_sums[:, 3],
        grad_w_fc,
        proj_total[0, DROWS, :FROWS],
        proj_total[:, :DROWS, :D].reshape(FROWS, D),
        proj_total[0, DROWS, FROWS : FROWS + DROWS],
    )
    activations = out_low.reshape(1, micro, span, D)
    input_grads = grad_input.reshape(1, micro, span, D)
    return (activations, input_grads) + tuple((total[None] for total in totals))


def solution(mesh):
    return jax.shard_map(
        shards,
        mesh=mesh,
        in_specs=(
            P("replica", "fsdp", None),
            P("replica", None),
            P("replica", None),
            P("section", "fsdp"),
            P("section", "fsdp"),
            P("section", "fsdp", None),
            P("section", "fsdp"),
            P("section", "fsdp", None),
            P("section", "fsdp"),
            P("section", "fsdp"),
            P("section", "fsdp"),
            P("section", "fsdp", None),
            P("section", "fsdp"),
            P("section", "fsdp", None),
            P("section", "fsdp"),
            P("replica", "fsdp", None),
        ),
        out_specs=(
            P("section", "replica", "fsdp", None),
            P("section", "replica", "fsdp", None),
            P("section", "fsdp"),
            P("section", "fsdp"),
            P("section", "fsdp", None),
            P("section", "fsdp"),
            P("section", "fsdp", None),
            P("section", "fsdp"),
            P("section", "fsdp"),
            P("section", "fsdp"),
            P("section", "fsdp", None),
            P("section", "fsdp"),
            P("section", "fsdp", None),
            P("section", "fsdp"),
        ),
        check_vma=False,
    )
```

```python
import jax
import jax.numpy as jnp
from jax import lax
from jax.experimental import pallas as pl
from jax.experimental.pallas import tpu as pltpu
from jax.sharding import PartitionSpec as P

D = 1088
HEADS = 17
HEAD_DIM = 64
FF = 4352
SHARDS = 16
DROWS = D // SHARDS
PROWS = 80
KPAD = SHARDS * PROWS
LANES = 1152
PAIRS = 9
FROWS = FF // SHARDS
SPLITS = FF // D
SCALE = HEAD_DIM ** (-0.5)

HALF = KPAD // 2
OUT_AT = SPLITS * PROWS
PROJ_AT = OUT_AT + PROWS
GELU_C = 0.7978845608028654
GELU_A = 0.044715

epsilon = 1e-05
bf16 = jnp.bfloat16
f32 = jnp.float32


def xor_pairs(k):
    return [(i, i ^ k) for i in range(SHARDS)]


def moved(value, k):
    return lax.ppermute(value, "fsdp", xor_pairs(k))


def gather_near(x, beside=None):
    half = x.shape[0] // 2
    blocks = {0: x, 4: moved(x, 4), 12: moved(x, 12), 2: moved(x, 2)}
    result = None
    if beside is not None:
        blocks[4], blocks[12], blocks[2], result = lax.optimization_barrier(
            (blocks[4], blocks[12], blocks[2], beside())
        )
    blocks[8] = jnp.concatenate([moved(blocks[4][:half], 12), moved(blocks[12][half:], 4)], 0)
    blocks[6] = moved(blocks[2], 4)
    blocks[14] = moved(blocks[2], 12)
    blocks[10] = moved(blocks[8], 2)
    return jnp.stack([blocks[k] for k in range(0, SHARDS, 2)]), result


def gather_both(x):
    near, _ = gather_near(x)
    return near, moved(near, 1)


def relative_device(me, place):
    return me ^ (2 * (place % 8) + place // 8)


def placing(me, relative):
    column = lax.broadcasted_iota(jnp.int32, (1, KPAD), 1)
    place, row = column // PROWS, column % PROWS
    owner = relative_device(me, place) if relative else place
    source = jnp.where(row < DROWS, owner * DROWS + row, -1)
    return (lax.broadcasted_iota(jnp.int32, (D, KPAD), 0) == source).astype(bf16)


def matmul(left, right):
    return jnp.dot(left, right, preferred_element_type=f32)


def contract(left, right, ldim, rdim):
    return lax.dot_general(left, right, (((ldim,), (rdim,)), ((), ())), preferred_element_type=f32)


def split_two(values):
    high = lax.reduce_precision(values, 8, 7)
    return high.astype(bf16), (values - high).astype(bf16)


def unplaced(values, place):
    rows = values.shape[0]
    both = contract(jnp.concatenate(split_two(values), 0), place, 1, 1)
    return both[:rows] + both[rows:]


def two_heads(block):
    lane = lax.broadcasted_iota(jnp.int32, block.shape, 1)
    zero = jnp.zeros_like(block)
    return jnp.concatenate(
        [jnp.where(lane < HEAD_DIM, block, zero), jnp.where(lane < HEAD_DIM, zero, block)], 0
    )


def one_pair(both):
    rows = both.shape[0] // 2
    lane = lax.broadcasted_iota(jnp.int32, (rows, 128), 1)
    return jnp.where(lane < HEAD_DIM, both[:rows], both[rows:])


def rows_of(near_ref, far_ref):
    return jnp.concatenate(
        [near_ref[...].reshape(-1, 128), far_ref[...].reshape(-1, 128)], 0
    )


def forward_kernel(q_ref, kn_ref, kf_ref, vn_ref, vf_ref, bias_ref, out_ref, lse_ref):
    bias = bias_ref[0]
    keys, values = rows_of(kn_ref, kf_ref), rows_of(vn_ref, vf_ref)
    scores = contract(two_heads(q_ref[...]), keys, 1, 1) * SCALE
    scores = scores + jnp.concatenate([bias, bias], 0)
    top = jnp.max(scores, axis=1, keepdims=True)
    shifted = jnp.exp(scores - top)
    total = jnp.sum(shifted, axis=1, keepdims=True)
    probs = (shifted / total).astype(bf16)
    out_ref[...] = one_pair(matmul(probs, values)).astype(bf16)
    lse = top + jnp.log(total)
    lse_ref[0, 0] = jnp.transpose(jnp.broadcast_to(lse, (128, 128)))[:8]


def row_kernel(q_ref, do_ref, lse_ref, kn_ref, kf_ref, vn_ref, vf_ref, bias_ref, dq_ref):
    bias = bias_ref[0]
    keys, values = rows_of(kn_ref, kf_ref), rows_of(vn_ref, vf_ref)
    lse = jnp.transpose(jnp.broadcast_to(lse_ref[0, 0][:1], (128, 128)))[:, :1]
    scores = contract(two_heads(q_ref[...]), keys, 1, 1) * SCALE
    scores = scores + jnp.concatenate([bias, bias], 0)
    probs = jnp.exp(scores - lse)
    grad_probs = contract(two_heads(do_ref[...]), values, 1, 1)
    dots = jnp.sum(grad_probs * probs, axis=1, keepdims=True)
    grad_scores = (probs * (grad_probs - dots)).astype(bf16)
    dq_ref[...] = (one_pair(matmul(grad_scores, keys)) * SCALE).astype(bf16)


def normalized(values):
    centred = values - jnp.mean(values, axis=1, keepdims=True)
    scale = lax.rsqrt(jnp.mean(centred * centred, axis=1, keepdims=True) + epsilon)
    return centred * scale, scale


def norm_back(values, gain, grad):
    z, scale = normalized(values)
    weighted = grad * gain
    by_values = scale * (
        weighted
        - jnp.mean(weighted, axis=1, keepdims=True)
        - z * jnp.mean(weighted * z, axis=1, keepdims=True)
    )
    row = lax.broadcasted_iota(jnp.int32, (8, D), 0)
    gain_sum = jnp.sum(grad * z, axis=0, keepdims=True)
    bias_sum = jnp.sum(grad, axis=0, keepdims=True)
    return by_values, jnp.where(row == 0, gain_sum, jnp.where(row == 1, bias_sum, 0.0))


def gelu_parts(v):
    t = jnp.tanh(GELU_C * (v + GELU_A * v * v * v))
    return 0.5 * v * (1.0 + t), t


def gelu_slope(v, t):
    return 0.5 * (1.0 + t) + 0.5 * v * (1.0 - t * t) * (GELU_C * (1.0 + 3.0 * GELU_A * v * v))


def unplaced(values, place):
    rows = values.shape[0]
    high = values.astype(bf16)
    low = (values - high.astype(f32)).astype(bf16)
    both = contract(jnp.concatenate([high, low], 0), place, 1, 1)
    return both[:rows] + both[rows:]


def input_weight(near_ref, far_ref, j):
    rows = slice(j * PROWS, (j + 1) * PROWS)
    return near_ref[:, rows, :].reshape(HALF, LANES), far_ref[:, rows, :].reshape(HALF, LANES)


def qkv_kernel(x_ref, near_ref, far_ref, place_ref, gain_ref, bias_ref, sq_ref, sv_ref, n1_ref, q_ref, kv_ref):
    z, _ = normalized(x_ref[...].astype(f32))
    normed = (z * gain_ref[...] + bias_ref[...]).astype(bf16)
    n1_ref[...] = normed
    placed = matmul(normed, place_ref[...]).astype(bf16)
    rows = placed.shape[0]

    def product(j):
        near, far = input_weight(near_ref, far_ref, j)
        return matmul(placed[:, :HALF], near) + matmul(placed[:, HALF:], far)

    kv_ref[:rows] = product(1).astype(bf16)
    kv_ref[rows:] = (product(2) + sv_ref[...]).astype(bf16)
    q_ref[...] = (product(0) + sq_ref[...]).astype(bf16)


def qkv_back_kernel(dq_ref, dk_ref, dv_ref, near_ref, far_ref, place_ref, x_ref, gain_ref, gh_ref, gin_ref, sums_ref):
    near_sum, far_sum = 0.0, 0.0
    for j, ref in enumerate((dq_ref, dk_ref, dv_ref)):
        near, far = input_weight(near_ref, far_ref, j)
        near_sum = near_sum + contract(ref[...], near, 1, 1)
        far_sum = far_sum + contract(ref[...], far, 1, 1)
    grad = unplaced(jnp.concatenate([near_sum, far_sum], 1), place_ref[...])
    by_input, sums_ref[...] = norm_back(x_ref[...].astype(f32), gain_ref[...], grad)
    gin_ref[...] = (gh_ref[...] + by_input).astype(bf16)


def weight_copies(all_ref, fc_buf, out_buf, proj_buf, sems):
    out_copy = pltpu.make_async_copy(all_ref.at[:, pl.ds(OUT_AT, PROWS), :], out_buf, sems.at[0])
    fc = [
        pltpu.make_async_copy(all_ref.at[:, pl.ds(j * PROWS, PROWS), :], fc_buf.at[j], sems.at[1 + j])
        for j in range(SPLITS)
    ]
    proj = [
        pltpu.make_async_copy(
            all_ref.at[pl.ds(4 * j, 4), pl.ds(PROJ_AT, FROWS), :], proj_buf.at[j], sems.at[1 + SPLITS + j]
        )
        for j in range(SPLITS)
    ]
    return out_copy, fc, proj


def ffn_kernel(
    att_ref, x_ref, place_ref, os_ref, gain_ref, bias_ref, ps_ref, fs_ref, all_ref,
    hidden_ref, n2_ref, pre_ref, out_ref, fc_buf, out_buf, proj_buf, sems,
):
    out_copy, fc, proj = weight_copies(all_ref, fc_buf, out_buf, proj_buf, sems)
    out_copy.start()
    for j in range(SPLITS):
        fc[j].start()
        proj[j].start()
    place = place_ref[...]
    placed = matmul(att_ref[:, :D], place).astype(bf16)
    out_copy.wait()
    hidden = x_ref[...].astype(f32) + matmul(placed, out_buf[...].reshape(KPAD, D)) + os_ref[...]
    hidden_ref[...] = hidden
    z, _ = normalized(hidden)
    normed = (z * gain_ref[...] + bias_ref[...]).astype(bf16)
    n2_ref[...] = normed
    placed = matmul(normed, place).astype(bf16)
    total = hidden + ps_ref[...]
    for j in range(SPLITS):
        fc[j].wait()
        pre = matmul(placed, fc_buf[j].reshape(KPAD, D)) + fs_ref[j : j + 1]
        pre_ref[j] = pre
        activ, _ = gelu_parts(pre)
        proj[j].wait()
        total = total + matmul(activ.astype(bf16), proj_buf[j].reshape(D, D))
    out_ref[...] = total.astype(bf16)


def ffn_back_kernel(
    go_ref, pre_ref, hidden_ref, place_ref, gain_ref, all_ref,
    gh_ref, gb_ref, ga_ref, sums_ref, fc_buf, out_buf, proj_buf, sems,
):
    out_copy, fc, proj = weight_copies(all_ref, fc_buf, out_buf, proj_buf, sems)
    for j in range(SPLITS):
        proj[j].start()
        fc[j].start()
    out_copy.start()
    grad_out = go_ref[...]
    placed = 0.0
    for j in range(SPLITS):
        pre = pre_ref[j]
        _, t = gelu_parts(pre)
        slope = gelu_slope(pre, t)
        proj[j].wait()
        grad_pre = (contract(grad_out, proj_buf[j].reshape(D, D), 1, 1) * slope).astype(bf16)
        fc[j].wait()
        placed = placed + contract(grad_pre, fc_buf[j].reshape(KPAD, D), 1, 1)
    place = place_ref[...]
    by_hidden, sums_ref[...] = norm_back(hidden_ref[...], gain_ref[...], unplaced(placed, place))
    grad_hidden = grad_out.astype(f32) + by_hidden
    gh_ref[...] = grad_hidden
    branch = grad_hidden.astype(bf16)
    gb_ref[...] = branch
    out_copy.wait()
    grad_att = contract(branch, out_buf[...].reshape(KPAD, D), 1, 1).astype(bf16)
    ga_ref[...] = jnp.zeros_like(ga_ref)
    ga_ref[:, :D] = contract(grad_att, place, 1, 1).astype(bf16)


def column_kernel(me_ref, k_ref, v_ref, q_ref, a_ref, lse_ref, don_ref, dof_ref, bias_ref, dk_ref, dv_ref):
    me = me_ref[0]
    owners = [relative_device(me, place) for place in range(SHARDS)]
    queries = jnp.concatenate([q_ref[owner] for owner in owners], 0)
    attended = jnp.concatenate([a_ref[owner] for owner in owners], 0)
    grads = rows_of(don_ref, dof_ref)
    rows = k_ref.shape[0]
    span = q_ref.shape[1]
    bias = bias_ref[0]
    micro = pl.program_id(0)
    term_row = lax.broadcasted_iota(jnp.int32, (16, 128), 0)
    place_of = (
        lax.broadcasted_iota(jnp.int32, (SHARDS, SHARDS * span), 1) // span
        == lax.broadcasted_iota(jnp.int32, (SHARDS, SHARDS * span), 0)
    ).astype(bf16)
    spread_lse = 0.0
    for term in range(3):
        picked = [
            jnp.sum(jnp.where(term_row == 2 * term + micro, lse_ref[owner].astype(f32), 0.0), axis=0, keepdims=True)
            for owner in owners
        ]
        spread_lse = spread_lse + contract(jnp.concatenate(picked, 0).astype(bf16), place_of, 0, 0)
    on_diagonal = (
        lax.broadcasted_iota(jnp.int32, spread_lse.shape, 0) % span
        == lax.broadcasted_iota(jnp.int32, spread_lse.shape, 1) % span
    )
    spread_lse = jnp.where(on_diagonal, spread_lse, 0.0)
    lse_a = jnp.sum(spread_lse[:span], axis=0, keepdims=True)
    lse_b = jnp.sum(spread_lse[span:], axis=0, keepdims=True)
    product = attended.astype(f32) * grads.astype(f32)
    sides = (
        lax.broadcasted_iota(jnp.int32, (8, 128), 1) // HEAD_DIM
        == lax.broadcasted_iota(jnp.int32, (8, 128), 0)
    ).astype(bf16)
    high = product.astype(bf16)
    low = (product - high.astype(f32)).astype(bf16)
    dots = contract(sides, high, 1, 1) + contract(sides, low, 1, 1)

    def spread(row_a, row_b):
        return jnp.concatenate(
            [jnp.broadcast_to(row_a, (rows, row_a.shape[1])), jnp.broadcast_to(row_b, (rows, row_b.shape[1]))], 0
        )

    scores = contract(two_heads(k_ref[...]), queries, 1, 1) * SCALE
    probs = jnp.exp(scores + jnp.concatenate([bias, bias], 0) - spread(lse_a, lse_b))
    grad_probs = contract(two_heads(v_ref[...]), grads, 1, 1)
    grad_scores = (probs * (grad_probs - spread(dots[:1], dots[1:2]))).astype(bf16)
    dk_ref[...] = (one_pair(matmul(grad_scores, queries)) * SCALE).astype(bf16)
    dv_ref[...] = one_pair(matmul(probs.astype(bf16), grads)).astype(bf16)


def hidden_units_kernel(n2_ref, go_ref, fc_ref, fb_ref, proj_ref, gp_ref, gf_out_ref, bsum_ref, osum_ref):
    step = pl.program_id(0)

    @pl.when(step == 0)
    def _():
        for ref in (gp_ref, gf_out_ref, bsum_ref, osum_ref):
            ref[...] = jnp.zeros_like(ref)

    n2 = n2_ref[...].reshape(-1, D)
    go = go_ref[...].reshape(-1, D)
    pre = matmul(n2, fc_ref[...]) + fb_ref[...]
    activ, t = gelu_parts(pre)
    grad_pre = (contract(go, proj_ref[...], 1, 1) * gelu_slope(pre, t)).astype(bf16)
    gp_ref[...] += contract(activ.astype(bf16), go, 0, 0)
    gf_out_ref[...] += contract(n2, grad_pre, 0, 0)
    bsum_ref[...] += jnp.broadcast_to(jnp.sum(grad_pre.astype(f32), axis=0, keepdims=True), bsum_ref.shape)
    osum_ref[...] += jnp.broadcast_to(jnp.sum(go.astype(f32), axis=0, keepdims=True), osum_ref.shape)


def columns_kernel(me_ref, n1_ref, a_ref, cols_ref, grad_ref, sums_ref):
    step = pl.program_id(0)

    @pl.when(step == 0)
    def _():
        grad_ref[...] = jnp.zeros_like(grad_ref)
        sums_ref[...] = jnp.zeros_like(sums_ref)

    att = a_ref[...].reshape(-1, LANES)[:, :D]
    left = jnp.where(me_ref[0] < 12, n1_ref[...].reshape(-1, D), att)
    cols = cols_ref[...].reshape(-1, FROWS)
    grad_ref[...] += contract(left, cols, 0, 0)
    sums_ref[...] += jnp.broadcast_to(jnp.sum(cols.astype(f32), axis=0, keepdims=True), sums_ref.shape)


def params(flops, bytes_accessed, transcendentals=0, vmem=32):
    return dict(
        compiler_params=pltpu.CompilerParams(vmem_limit_bytes=vmem * 1024 * 1024),
        cost_estimate=pl.CostEstimate(
            flops=flops, bytes_accessed=bytes_accessed, transcendentals=transcendentals
        ),
    )


def shape(*dims, dtype=bf16):
    return jax.ShapeDtypeStruct(dims, dtype)


def whole_call(body, out_shape, operands, in_hbm=(), scratch=(), flops=0, bytes_accessed=0, vmem=56):
    vm, hbm = pl.BlockSpec(memory_space=pltpu.VMEM), pl.BlockSpec(memory_space=pl.ANY)
    return pl.pallas_call(
        body,
        in_specs=[hbm if i in in_hbm else vm for i in range(len(operands))],
        out_specs=[vm] * len(out_shape),
        out_shape=out_shape,
        scratch_shapes=list(scratch),
        **params(flops, bytes_accessed, 0, vmem),
    )(*operands)


def pair_call(body, n_matmuls, in_specs, out_specs, out_shape, operands, vmem=32):
    steps = 2 * PAIRS
    return pl.pallas_call(
        body,
        grid=(2, PAIRS),
        in_specs=in_specs,
        out_specs=out_specs,
        out_shape=out_shape,
        **params(
            steps * n_matmuls * 2 * 128 * 128 * 1024 * 4, steps * 2 * 1024 * 128 * 2, steps * 128 * 1024, vmem
        ),
    )(*operands)


def own_spec(rows):
    return pl.BlockSpec((rows, 128), lambda m, h: (m, h))


def all_spec(kind, rows):
    return pl.BlockSpec((8, 1, 1, rows, 128), lambda m, h: (0, kind, m, 0, h))


def shards(
    inputs,
    segment_ids,
    sequence_order,
    ln1_gain,
    ln1_bias,
    w_qkv,
    qv_bias,
    w_out,
    out_bias,
    ln2_gain,
    ln2_bias,
    w_fc,
    fc_bias,
    w_proj,
    proj_bias,
    cotangent,
):
    section_index = lax.axis_index("section")
    me = lax.axis_index("fsdp")
    is_first = section_index == 0
    is_last = section_index == 1
    micro, span = inputs.shape[0], inputs.shape[1]
    tokens = micro * span
    seq_len = segment_ids.shape[1]

    def rows_padded(block):
        return jnp.pad(block, ((0, PROWS - block.shape[0]), (0, 0)))

    later = jnp.concatenate(
        [rows_padded(w_fc[0][:, j * D : (j + 1) * D]) for j in range(SPLITS)]
        + [rows_padded(w_out[0]), w_proj[0]],
        0,
    )
    later_all = lax.all_gather(later, "fsdp", axis=0, tiled=False)
    vectors = jnp.concatenate(
        [ln1_gain[0], ln1_bias[0], out_bias[0], ln2_gain[0], ln2_bias[0], proj_bias[0], qv_bias[0], fc_bias[0]]
    )
    vector_rows = jnp.pad(vectors[None], ((0, 15), (0, LANES - vectors.shape[0])))
    first = jnp.concatenate(
        [
            jnp.pad(w_qkv[0][:, j * D : (j + 1) * D], ((0, PROWS - DROWS), (0, LANES - D)))
            for j in range(3)
        ]
        + [vector_rows],
        0,
    )
    first_near, first_far = gather_both(first)
    place_iota = jnp.arange(SHARDS)
    to_absolute = (relative_device(me, place_iota)[None, :] == place_iota[:, None]).astype(bf16)
    vector_rel = jnp.concatenate([first_near[:, 3 * PROWS], first_far[:, 3 * PROWS]], 0)
    vector_all = matmul(to_absolute, vector_rel)

    def vector(start, size):
        return vector_all[:, start : start + size].reshape(1, SHARDS * size)

    gain_one, bias_one, out_shift, gain_two, bias_two, proj_shift = [
        vector(j * DROWS, DROWS) for j in range(6)
    ]
    qv_full = vector(6 * DROWS, 2 * DROWS)
    fc_shift = vector(8 * DROWS, FROWS).reshape(SPLITS, D)
    shift_q = jnp.pad(qv_full[:, :D], ((0, 0), (0, LANES - D)))
    shift_v = jnp.pad(qv_full[:, D:], ((0, 0), (0, LANES - D)))

    place_rel = placing(me, True)
    place_abs = placing(me, False)

    swapped = sequence_order[0, 0] == 1
    ordered_inputs = jnp.where(swapped, inputs[::-1], inputs).reshape(tokens, D)
    ordered_segments = jnp.where(swapped, segment_ids[::-1], segment_ids)
    by_block = ordered_segments.reshape(micro, SHARDS, span)
    rel_devices = relative_device(me, place_iota)
    seg_rel = jnp.take(by_block, rel_devices, axis=1).reshape(micro, 1, seq_len)
    seg_own = lax.dynamic_index_in_dim(by_block, me, 1, keepdims=False)[:, :, None]
    pos_rel = (rel_devices[:, None] * span + jnp.arange(span)[None]).reshape(1, 1, seq_len)
    pos_own = (me * span + jnp.arange(span)).reshape(1, span, 1)
    same = seg_rel == seg_own
    row_bias = jnp.where(same & (pos_rel <= pos_own), 0.0, -1e30).astype(f32)
    column_bias = jnp.where(same & (pos_own <= pos_rel), 0.0, -1e30).astype(f32)
    me_scalar = me.astype(jnp.int32).reshape(1)

    bias_spec = pl.BlockSpec((1, span, seq_len), lambda m, h: (m, 0, 0))
    lse_spec = pl.BlockSpec((1, 1, 8, 128), lambda m, h: (m, h, 0, 0))
    kv_specs = [all_spec(0, span), all_spec(0, span), all_spec(1, span), all_spec(1, span)]
    token_shape = shape(tokens, LANES)
    buffers = [
        pltpu.VMEM((SPLITS, SHARDS, PROWS, D), bf16),
        pltpu.VMEM((SHARDS, PROWS, D), bf16),
        pltpu.VMEM((SPLITS, 4, FROWS, D), bf16),
        pltpu.SemaphoreType.DMA((1 + 2 * SPLITS,)),
    ]
    ffn_cost = dict(flops=4 * 2 * tokens * D * FF, bytes_accessed=2 * SHARDS * 672 * D, scratch=buffers)
    qkv_cost = dict(flops=4 * 2 * tokens * D * 3 * D, bytes_accessed=2 * SHARDS * 256 * LANES)

    def by_kind(block):
        return block.reshape(8, -1, micro, span, LANES)

    def forward_layer(layer_in):
        normed_one, queries, keys_values = whole_call(
            qkv_kernel,
            [shape(tokens, D), token_shape, shape(2 * tokens, LANES)],
            (layer_in, first_near, first_far, place_rel, gain_one, bias_one, shift_q, shift_v),
            **qkv_cost,
        )
        kv_near, kv_far = [by_kind(b) for b in gather_both(keys_values)]
        attended, log_total = pair_call(
            forward_kernel,
            2,
            [own_spec(span)] + kv_specs + [bias_spec],
            [own_spec(span), lse_spec],
            [token_shape, shape(micro, PAIRS, 8, 128, dtype=f32)],
            (queries, kv_near, kv_far, kv_near, kv_far, row_bias),
        )
        hidden, normed_two, pre_act, out_low = whole_call(
            ffn_kernel,
            [shape(tokens, D, dtype=f32), shape(tokens, D), shape(SPLITS, tokens, D, dtype=f32), shape(tokens, D)],
            (attended, layer_in, place_abs, out_shift, gain_two, bias_two, proj_shift, fc_shift, later_all),
            in_hbm=(8,),
            **ffn_cost,
        )
        return out_low, (normed_one, queries, keys_values, kv_near, kv_far, attended, log_total, hidden, normed_two, pre_act)

    sent_on, _ = forward_layer(ordered_inputs)
    received = lax.ppermute(sent_on, "section", [(0, 1)])
    layer_in = jnp.where(is_first, ordered_inputs, received)
    out_low, kept = forward_layer(layer_in)
    normed_one, queries, keys_values, kv_near, kv_far, attended, log_total, hidden, normed_two, pre_act = kept

    lse_own = log_total[:, :, 0]
    part_one = lax.reduce_precision(lse_own, 8, 7)
    part_two = lax.reduce_precision(lse_own - part_one, 8, 7)
    part_three = lse_own - part_one - part_two
    lse_rows = jnp.stack([part_one, part_two, part_three]).astype(bf16).reshape(6, LANES)
    qa_all = lax.all_gather(
        jnp.concatenate([queries, attended, lse_rows, jnp.zeros((10, LANES), bf16)], 0), "fsdp", axis=0
    )
    nn_all = lax.all_gather(jnp.concatenate([normed_one, normed_two], 0), "fsdp", axis=0)

    def backward_layer(grad_out):
        grad_hidden, grad_branch, grad_att, sums_two = whole_call(
            ffn_back_kernel,
            [shape(tokens, D, dtype=f32), shape(tokens, D), token_shape, shape(8, D, dtype=f32)],
            (grad_out, pre_act, hidden, place_abs, gain_two, later_all),
            in_hbm=(5,),
            **ffn_cost,
        )
        def row_part():
            return pair_call(
                row_kernel,
                3,
                [own_spec(span), own_spec(span), lse_spec] + kv_specs + [bias_spec],
                own_spec(span),
                token_shape,
                (queries, grad_att, log_total, kv_near, kv_far, kv_near, kv_far, row_bias),
            )

        near, grad_q = gather_near(grad_att, row_part)
        do_near, do_far = by_kind(near), by_kind(moved(near, 1))
        own_half = lambda half: pl.BlockSpec((span, 128), lambda m, h: (2 * half + m, h))
        grad_k, grad_v = pair_call(
            column_kernel,
            5,
            [
                pl.BlockSpec(memory_space=pltpu.SMEM),
                own_half(0),
                own_half(1),
                pl.BlockSpec((SHARDS, span, 128), lambda m, h: (0, m, h)),
                pl.BlockSpec((SHARDS, span, 128), lambda m, h: (0, 2 + m, h)),
                pl.BlockSpec((SHARDS, 16, 128), lambda m, h: (0, 16, h)),
            ]
            + [all_spec(0, span), all_spec(0, span), bias_spec],
            [own_spec(span), own_spec(span)],
            [token_shape, token_shape],
            (
                me_scalar, keys_values, keys_values, qa_all, qa_all, qa_all, do_near, do_far, column_bias,
            ),
            vmem=60,
        )
        grad_input, sums_one = whole_call(
            qkv_back_kernel,
            [shape(tokens, D), shape(8, D, dtype=f32)],
            (grad_q, grad_k, grad_v, first_near, first_far, place_rel, layer_in, gain_one, grad_hidden),
            **qkv_cost,
        )
        norm_grads = jnp.concatenate([sums_one[:2], sums_two[:2]], 0)
        return grad_input, grad_branch, (grad_q, grad_k, grad_v), norm_grads

    own_cotangent = cotangent.reshape(tokens, D)
    sent_back, _, _, _ = backward_layer(own_cotangent)
    received_grad = lax.ppermute(sent_back, "section", [(1, 0)])
    grad_out = jnp.where(is_last, own_cotangent, received_grad)
    go_all = lax.all_gather(grad_out, "fsdp", axis=0)
    grad_input, grad_branch, grad_qkv, norm_grads = backward_layer(grad_out)

    fc_own = lax.dynamic_slice(later_all, (0, (me // 4) * PROWS, (me % 4) * FROWS), (SHARDS, PROWS, FROWS))
    fc_own = fc_own[:, :DROWS].reshape(D, FROWS)
    fixed = lambda *dims: pl.BlockSpec(dims, lambda s: (0,) * len(dims))
    chip = lambda kind, width: pl.BlockSpec((2, tokens, width), lambda s: (s, kind, 0))
    grad_proj_w, grad_fc_w, grad_fc_b, out_sums = pl.pallas_call(
        hidden_units_kernel,
        grid=(8,),
        in_specs=[chip(1, D), chip(0, D), fixed(D, FROWS), fixed(1, FROWS), fixed(FROWS, D)],
        out_specs=[fixed(FROWS, D), fixed(D, FROWS), fixed(8, FROWS), fixed(8, D)],
        out_shape=[shape(FROWS, D, dtype=f32), shape(D, FROWS, dtype=f32), shape(8, FROWS, dtype=f32), shape(8, D, dtype=f32)],
        **params(4 * 4 * 2 * SHARDS * tokens * D * FROWS, 3 * 2 * SHARDS * tokens * D, vmem=60),
    )(nn_all, go_all, fc_own, fc_bias.astype(f32), w_proj[0])
    grad_proj_b = lax.dynamic_slice_in_dim(out_sums[0], me * DROWS, DROWS)
    wide = jnp.concatenate([g[:, :D] for g in grad_qkv] + [grad_branch], 1)
    wide = wide.reshape(tokens, SHARDS, FROWS).transpose(1, 0, 2)
    columns = lax.all_to_all(wide, "fsdp", 0, 0)
    columns, grad_fc_w, grad_proj_w = lax.optimization_barrier((columns, grad_fc_w, grad_proj_w))
    grad_columns, column_sums = pl.pallas_call(
        columns_kernel,
        grid=(8,),
        in_specs=[pl.BlockSpec(memory_space=pltpu.SMEM), chip(0, D), chip(1, LANES), chip(0, FROWS)],
        out_specs=[fixed(D, FROWS), fixed(8, FROWS)],
        out_shape=[shape(D, FROWS, dtype=f32), shape(8, FROWS, dtype=f32)],
        **params(4 * 2 * SHARDS * tokens * D * FROWS, 4 * 2 * SHARDS * tokens * D, vmem=60),
    )(me_scalar, nn_all, qa_all, columns)

    width, height = 384, 72
    z = lax.axis_index("replica")

    def to_owners(columns_of_rows):
        pads = ((0, 0), (0, height - columns_of_rows.shape[1]), (0, width - columns_of_rows.shape[2]))
        return lax.all_to_all(jnp.pad(columns_of_rows, pads), "fsdp", 0, 0)

    def over_replicas(quarter):
        pick = lambda k: lax.dynamic_index_in_dim(quarter, z ^ k, 0, keepdims=False)
        swap = lambda v, k: lax.ppermute(v, "replica", [(j, j ^ k) for j in range(4)])
        total = pick(0).astype(f32)
        for term in [swap(pick(k), k) for k in (1, 3, 2)]:
            total = total + term.astype(f32)
        total = total.astype(bf16)
        finished = jnp.stack([total] + [swap(total, k) for k in (1, 2, 3)])
        return jnp.take(finished, z ^ jnp.arange(4), axis=0)

    got_fc = to_owners(grad_fc_w.astype(bf16).reshape(SHARDS, DROWS, FROWS)).reshape(4, 4, height, width)
    own_vectors = jnp.concatenate([grad_fc_b[0], grad_proj_b, jnp.zeros((3 * width - FROWS - DROWS,), f32)])
    proj_part = jnp.pad(grad_proj_w.reshape(4, DROWS, D), ((0, 0), (0, 0), (0, 3 * width - D)))
    own_part = jnp.broadcast_to(own_vectors[None, None], (4, height - DROWS, 3 * width))
    proj_part = jnp.concatenate([proj_part, own_part], 1).astype(bf16)
    proj_parts = [proj_part[:, None, :, j * width : (j + 1) * width] for j in range(3)]
    ffn_total = over_replicas(jnp.concatenate([got_fc] + proj_parts, 1))

    rows = jnp.concatenate(
        [
            grad_columns.astype(bf16).reshape(SHARDS, DROWS, FROWS),
            norm_grads.astype(bf16).reshape(4, SHARDS, DROWS).transpose(1, 2, 0),
        ],
        2,
    )
    rows = jnp.pad(rows, ((0, 0), (0, 0), (0, width - rows.shape[2])))
    sums_row = jnp.broadcast_to(
        jnp.pad(column_sums[0].astype(bf16), (0, width - FROWS))[None, None], (SHARDS, 1, width)
    )
    got = to_owners(jnp.concatenate([rows, sums_row], 1))
    got, ffn_total = lax.optimization_barrier((got, ffn_total))
    finished = over_replicas(got.reshape(4, 4, height, width)).reshape(SHARDS, height, width).astype(f32)
    proj_total = jnp.concatenate([ffn_total[:, 4], ffn_total[:, 5], ffn_total[:, 6]], 2).astype(f32)
    fc_total = ffn_total[:, :4].reshape(SHARDS, height, width).astype(f32)

    def joined(block):
        return block.transpose(1, 0, 2).reshape(block.shape[1], -1)

    grad_w_qkv = joined(finished[:12, :DROWS, :FROWS])
    grad_w_out = joined(finished[12:, :DROWS, :FROWS])
    grad_w_fc = joined(fc_total[:, :DROWS, :FROWS])
    norm_sums = jnp.sum(finished[:, :DROWS, FROWS : FROWS + 4], axis=0)
    sums = finished[:, DROWS, :FROWS].reshape(SHARDS * FROWS)
    qv_sums = jnp.concatenate([sums[:D], sums[2 * D : 3 * D]])
    grad_qv_b = lax.dynamic_slice_in_dim(qv_sums, me * 2 * DROWS, 2 * DROWS)
    grad_out_b = lax.dynamic_slice_in_dim(sums, 3 * D + me * DROWS, DROWS)
    totals = (
        norm_sums[:, 0],
        norm_sums[:, 1],
        grad_w_qkv,
        grad_qv_b,
        grad_w_out,
        grad_out_b,
        norm_sums[:, 2],
        norm_sums[:, 3],
        grad_w_fc,
        proj_total[0, DROWS, :FROWS],
        proj_total[:, :DROWS, :D].reshape(FROWS, D),
        proj_total[0, DROWS, FROWS : FROWS + DROWS],
    )
    activations = out_low.reshape(1, micro, span, D)
    input_grads = grad_input.reshape(1, micro, span, D)
    return (activations, input_grads) + tuple((total[None] for total in totals))


def solution(mesh):
    return jax.shard_map(
        shards,
        mesh=mesh,
        in_specs=(
            P("replica", "fsdp", None),
            P("replica", None),
            P("replica", None),
            P("section", "fsdp"),
            P("section", "fsdp"),
            P("section", "fsdp", None),
            P("section", "fsdp"),
            P("section", "fsdp", None),
            P("section", "fsdp"),
            P("section", "fsdp"),
            P("section", "fsdp"),
            P("section", "fsdp", None),
            P("section", "fsdp"),
            P("section", "fsdp", None),
            P("section", "fsdp"),
            P("replica", "fsdp", None),
        ),
        out_specs=(
            P("section", "replica", "fsdp", None),
            P("section", "replica", "fsdp", None),
            P("section", "fsdp"),
            P("section", "fsdp"),
            P("section", "fsdp", None),
            P("section", "fsdp"),
            P("section", "fsdp", None),
            P("section", "fsdp"),
            P("section", "fsdp"),
            P("section", "fsdp"),
            P("section", "fsdp", None),
            P("section", "fsdp"),
            P("section", "fsdp", None),
            P("section", "fsdp"),
        ),
        check_vma=False,
    )
```

```python
import jax
import jax.numpy as jnp
from jax import lax
from jax.experimental import pallas as pl
from jax.experimental.pallas import tpu as pltpu
from jax.sharding import PartitionSpec as P

D = 1088
HEADS = 17
HEAD_DIM = 64
FF = 4352
SHARDS = 16
DROWS = D // SHARDS
PROWS = 80
KPAD = SHARDS * PROWS
LANES = 1152
PAIRS = 9
FROWS = FF // SHARDS
SPLITS = FF // D
SCALE = HEAD_DIM ** (-0.5)

HALF = KPAD // 2
OUT_AT = SPLITS * PROWS
PROJ_AT = OUT_AT + PROWS
GELU_C = 0.7978845608028654
GELU_A = 0.044715

epsilon = 1e-05
bf16 = jnp.bfloat16
f32 = jnp.float32


def xor_pairs(k):
    return [(i, i ^ k) for i in range(SHARDS)]


def moved(value, k):
    return lax.ppermute(value, "fsdp", xor_pairs(k))


def gather_near(x, beside=None):
    half = x.shape[0] // 2
    blocks = {0: x, 4: moved(x, 4), 12: moved(x, 12), 2: moved(x, 2)}
    result = None
    if beside is not None:
        blocks[4], blocks[12], blocks[2], result = lax.optimization_barrier(
            (blocks[4], blocks[12], blocks[2], beside())
        )
    blocks[8] = jnp.concatenate([moved(blocks[4][:half], 12), moved(blocks[12][half:], 4)], 0)
    blocks[6] = moved(blocks[2], 4)
    blocks[14] = moved(blocks[2], 12)
    blocks[10] = moved(blocks[8], 2)
    return jnp.stack([blocks[k] for k in range(0, SHARDS, 2)]), result


def gather_both(x):
    near, _ = gather_near(x)
    return near, moved(near, 1)


def relative_device(me, place):
    return me ^ (2 * (place % 8) + place // 8)


def placing(me, relative):
    column = lax.broadcasted_iota(jnp.int32, (1, KPAD), 1)
    place, row = column // PROWS, column % PROWS
    owner = relative_device(me, place) if relative else place
    source = jnp.where(row < DROWS, owner * DROWS + row, -1)
    return (lax.broadcasted_iota(jnp.int32, (D, KPAD), 0) == source).astype(bf16)


def matmul(left, right):
    return jnp.dot(left, right, preferred_element_type=f32)


def contract(left, right, ldim, rdim):
    return lax.dot_general(left, right, (((ldim,), (rdim,)), ((), ())), preferred_element_type=f32)


def split_two(values):
    high = lax.reduce_precision(values, 8, 7)
    return high.astype(bf16), (values - high).astype(bf16)


def unplaced(values, place):
    rows = values.shape[0]
    both = contract(jnp.concatenate(split_two(values), 0), place, 1, 1)
    return both[:rows] + both[rows:]


def two_heads(block):
    lane = lax.broadcasted_iota(jnp.int32, block.shape, 1)
    zero = jnp.zeros_like(block)
    return jnp.concatenate(
        [jnp.where(lane < HEAD_DIM, block, zero), jnp.where(lane < HEAD_DIM, zero, block)], 0
    )


def scaled(block):
    return (block.astype(f32) * SCALE).astype(bf16)


def one_pair(both):
    rows = both.shape[0] // 2
    lane = lax.broadcasted_iota(jnp.int32, (rows, 128), 1)
    return jnp.where(lane < HEAD_DIM, both[:rows], both[rows:])


def rows_of(near_ref, far_ref):
    return jnp.concatenate(
        [near_ref[...].reshape(-1, 128), far_ref[...].reshape(-1, 128)], 0
    )


def forward_kernel(q_ref, kn_ref, kf_ref, vn_ref, vf_ref, bias_ref, out_ref, lse_ref):
    bias = bias_ref[0]
    keys, values = rows_of(kn_ref, kf_ref), rows_of(vn_ref, vf_ref)
    scores = contract(two_heads(scaled(q_ref[...])), keys, 1, 1) + jnp.concatenate([bias, bias], 0)
    top = jnp.max(scores, axis=1, keepdims=True)
    shifted = jnp.exp(scores - top)
    total = jnp.sum(shifted, axis=1, keepdims=True)
    probs = (shifted / total).astype(bf16)
    out_ref[...] = one_pair(matmul(probs, values)).astype(bf16)
    lse = top + jnp.log(total)
    lse_ref[0, 0] = jnp.transpose(jnp.broadcast_to(lse, (128, 128)))[:8]


def row_kernel(q_ref, do_ref, lse_ref, kn_ref, kf_ref, vn_ref, vf_ref, bias_ref, dq_ref):
    bias = bias_ref[0]
    keys, values = rows_of(kn_ref, kf_ref), rows_of(vn_ref, vf_ref)
    lse = jnp.transpose(jnp.broadcast_to(lse_ref[0, 0][:1], (128, 128)))[:, :1]
    scores = contract(two_heads(scaled(q_ref[...])), keys, 1, 1) + jnp.concatenate([bias, bias], 0)
    probs = jnp.exp(scores - lse)
    grad_probs = contract(two_heads(do_ref[...]), values, 1, 1)
    dots = jnp.sum(grad_probs * probs, axis=1, keepdims=True)
    grad_scores = (probs * (grad_probs - dots)).astype(bf16)
    dq_ref[...] = (one_pair(matmul(grad_scores, keys)) * SCALE).astype(bf16)


def normalized(values):
    centred = values - jnp.mean(values, axis=1, keepdims=True)
    scale = lax.rsqrt(jnp.mean(centred * centred, axis=1, keepdims=True) + epsilon)
    return centred * scale, scale


def norm_back(values, gain, grad):
    z, scale = normalized(values)
    weighted = grad * gain
    by_values = scale * (
        weighted
        - jnp.mean(weighted, axis=1, keepdims=True)
        - z * jnp.mean(weighted * z, axis=1, keepdims=True)
    )
    row = lax.broadcasted_iota(jnp.int32, (8, D), 0)
    gain_sum = jnp.sum(grad * z, axis=0, keepdims=True)
    bias_sum = jnp.sum(grad, axis=0, keepdims=True)
    return by_values, jnp.where(row == 0, gain_sum, jnp.where(row == 1, bias_sum, 0.0))


def gelu_parts(v):
    t = jnp.tanh(GELU_C * (v + GELU_A * v * v * v))
    return 0.5 * v * (1.0 + t), t


def gelu_slope(v, t):
    return 0.5 * (1.0 + t) + 0.5 * v * (1.0 - t * t) * (GELU_C * (1.0 + 3.0 * GELU_A * v * v))


def unplaced(values, place):
    rows = values.shape[0]
    high = values.astype(bf16)
    low = (values - high.astype(f32)).astype(bf16)
    both = contract(jnp.concatenate([high, low], 0), place, 1, 1)
    return both[:rows] + both[rows:]


def input_weight(near_ref, far_ref, j):
    rows = slice(j * PROWS, (j + 1) * PROWS)
    return near_ref[:, rows, :].reshape(HALF, LANES), far_ref[:, rows, :].reshape(HALF, LANES)


def qkv_kernel(x_ref, near_ref, far_ref, place_ref, gain_ref, bias_ref, sq_ref, sv_ref, n1_ref, q_ref, kv_ref):
    z, _ = normalized(x_ref[...].astype(f32))
    normed = (z * gain_ref[...] + bias_ref[...]).astype(bf16)
    n1_ref[...] = normed
    placed = matmul(normed, place_ref[...]).astype(bf16)
    rows = placed.shape[0]

    def product(j):
        near, far = input_weight(near_ref, far_ref, j)
        return matmul(placed[:, :HALF], near) + matmul(placed[:, HALF:], far)

    kv_ref[:rows] = product(1).astype(bf16)
    kv_ref[rows:] = (product(2) + sv_ref[...]).astype(bf16)
    q_ref[...] = (product(0) + sq_ref[...]).astype(bf16)


def kv_all_kernel(xn_ref, xf_ref, near_ref, far_ref, place_ref, gain_ref, bias_ref, sq_ref, sv_ref, q_ref, kn_ref, kf_ref):
    rows = xn_ref.shape[1]
    x = jnp.concatenate([xn_ref[0], xf_ref[0]], 0)[:, :D]
    z, _ = normalized(x.astype(f32))
    normed = (z * gain_ref[...] + bias_ref[...]).astype(bf16)
    placed = matmul(normed, place_ref[...]).astype(bf16)

    def product(left, j):
        near, far = input_weight(near_ref, far_ref, j)
        return matmul(left[:, :HALF], near) + matmul(left[:, HALF:], far)

    keys = product(placed, 1).astype(bf16)
    values = (product(placed, 2) + sv_ref[...]).astype(bf16)
    kn_ref[0, 0], kn_ref[0, 1] = keys[:rows], values[:rows]
    kf_ref[0, 0], kf_ref[0, 1] = keys[rows:], values[rows:]

    @pl.when(pl.program_id(0) == 0)
    def _():
        q_ref[...] = (product(placed[:rows], 0) + sq_ref[...]).astype(bf16)


def qkv_back_kernel(dq_ref, dk_ref, dv_ref, near_ref, far_ref, place_ref, x_ref, gain_ref, gh_ref, gin_ref, sums_ref):
    near_sum, far_sum = 0.0, 0.0
    for j, ref in enumerate((dq_ref, dk_ref, dv_ref)):
        near, far = input_weight(near_ref, far_ref, j)
        near_sum = near_sum + contract(ref[...], near, 1, 1)
        far_sum = far_sum + contract(ref[...], far, 1, 1)
    grad = unplaced(jnp.concatenate([near_sum, far_sum], 1), place_ref[...])
    by_input, sums_ref[...] = norm_back(x_ref[...].astype(f32), gain_ref[...], grad)
    gin_ref[...] = (gh_ref[...] + by_input).astype(bf16)


def weight_copies(all_ref, fc_buf, out_buf, proj_buf, sems):
    out_copy = pltpu.make_async_copy(all_ref.at[:, pl.ds(OUT_AT, PROWS), :], out_buf, sems.at[0])
    fc = [
        pltpu.make_async_copy(all_ref.at[:, pl.ds(j * PROWS, PROWS), :], fc_buf.at[j], sems.at[1 + j])
        for j in range(SPLITS)
    ]
    proj = [
        pltpu.make_async_copy(
            all_ref.at[pl.ds(4 * j, 4), pl.ds(PROJ_AT, FROWS), :], proj_buf.at[j], sems.at[1 + SPLITS + j]
        )
        for j in range(SPLITS)
    ]
    return out_copy, fc, proj


def ffn_forward(
    att_ref, x_ref, place_ref, os_ref, gain_ref, bias_ref, ps_ref, fs_ref, all_ref,
    hidden_ref, n2_ref, pre_ref, out_ref, fc_buf, out_buf, proj_buf, sems,
):
    out_copy, fc, proj = weight_copies(all_ref, fc_buf, out_buf, proj_buf, sems)
    out_copy.start()
    for j in range(SPLITS):
        fc[j].start()
        proj[j].start()
    place = place_ref[...]
    placed = matmul(att_ref[:, :D], place).astype(bf16)
    out_copy.wait()
    hidden = x_ref[...].astype(f32) + matmul(placed, out_buf[...].reshape(KPAD, D)) + os_ref[...]
    hidden_ref[...] = hidden
    z, _ = normalized(hidden)
    normed = (z * gain_ref[...] + bias_ref[...]).astype(bf16)
    n2_ref[...] = normed
    placed = matmul(normed, place).astype(bf16)
    total = hidden + ps_ref[...]
    for j in range(SPLITS):
        fc[j].wait()
        pre = matmul(placed, fc_buf[j].reshape(KPAD, D)) + fs_ref[j : j + 1]
        pre_ref[j] = pre
        activ, _ = gelu_parts(pre)
        proj[j].wait()
        total = total + matmul(activ.astype(bf16), proj_buf[j].reshape(D, D))
    out_ref[...] = total.astype(bf16)


def ffn_backward(
    go_ref, pre_ref, hidden_ref, place_ref, gain_ref, ready,
    gh_ref, gb_ref, ga_ref, sums_ref, fc_buf, out_buf, proj_buf,
):
    grad_out = go_ref[...]
    placed = 0.0
    for j in range(SPLITS):
        pre = pre_ref[j]
        _, t = gelu_parts(pre)
        slope = gelu_slope(pre, t)
        ready("proj", j)
        grad_pre = (contract(grad_out, proj_buf[j].reshape(D, D), 1, 1) * slope).astype(bf16)
        ready("fc", j)
        placed = placed + contract(grad_pre, fc_buf[j].reshape(KPAD, D), 1, 1)
    place = place_ref[...]
    by_hidden, sums_ref[...] = norm_back(hidden_ref[...], gain_ref[...], unplaced(placed, place))
    grad_hidden = grad_out.astype(f32) + by_hidden
    gh_ref[...] = grad_hidden
    branch = grad_hidden.astype(bf16)
    gb_ref[...] = branch
    ready("out", 0)
    grad_att = contract(branch, out_buf[...].reshape(KPAD, D), 1, 1).astype(bf16)
    ga_ref[...] = jnp.zeros_like(ga_ref)
    ga_ref[:, :D] = contract(grad_att, place, 1, 1).astype(bf16)


def ffn_back_kernel(
    go_ref, pre_ref, hidden_ref, place_ref, gain_ref, all_ref,
    gh_ref, gb_ref, ga_ref, sums_ref, fc_buf, out_buf, proj_buf, sems,
):
    out_copy, fc, proj = weight_copies(all_ref, fc_buf, out_buf, proj_buf, sems)
    for j in range(SPLITS):
        proj[j].start()
        fc[j].start()
    out_copy.start()
    copies = {"proj": proj, "fc": fc, "out": [out_copy]}
    ffn_backward(
        go_ref, pre_ref, hidden_ref, place_ref, gain_ref, lambda kind, j: copies[kind][j].wait(),
        gh_ref, gb_ref, ga_ref, sums_ref, fc_buf, out_buf, proj_buf,
    )


def ffn_both_kernel(
    att_ref, x_ref, place_ref, os_ref, gain_ref, bias_ref, ps_ref, fs_ref, all_ref, go_ref,
    hidden_ref, n2_ref, pre_ref, out_ref, gh_ref, gb_ref, ga_ref, sums_ref, fc_buf, out_buf, proj_buf, sems,
):
    ffn_forward(
        att_ref, x_ref, place_ref, os_ref, gain_ref, bias_ref, ps_ref, fs_ref, all_ref,
        hidden_ref, n2_ref, pre_ref, out_ref, fc_buf, out_buf, proj_buf, sems,
    )
    ffn_backward(
        go_ref, pre_ref, hidden_ref, place_ref, gain_ref, lambda kind, j: None,
        gh_ref, gb_ref, ga_ref, sums_ref, fc_buf, out_buf, proj_buf,
    )


def column_kernel(me_ref, k_ref, v_ref, q_ref, a_ref, lse_ref, don_ref, dof_ref, bias_ref, dk_ref, dv_ref):
    me = me_ref[0]
    owners = [relative_device(me, place) for place in range(SHARDS)]
    queries = jnp.concatenate([q_ref[owner] for owner in owners], 0)
    attended = jnp.concatenate([a_ref[owner] for owner in owners], 0)
    grads = rows_of(don_ref, dof_ref)
    rows = k_ref.shape[0]
    span = q_ref.shape[1]
    bias = bias_ref[0]
    micro = pl.program_id(0)
    term_row = lax.broadcasted_iota(jnp.int32, (16, 128), 0)
    terms = (3 * SHARDS, SHARDS * span)
    place_of = (
        lax.broadcasted_iota(jnp.int32, terms, 1) // span == lax.broadcasted_iota(jnp.int32, terms, 0) % SHARDS
    ).astype(bf16)
    picked = [
        jnp.sum(jnp.where(term_row == 2 * term + micro, lse_ref[owner].astype(f32), 0.0), axis=0, keepdims=True)
        for term in range(3)
        for owner in owners
    ]
    spread_lse = contract(jnp.concatenate(picked, 0).astype(bf16), place_of, 0, 0)
    on_diagonal = (
        lax.broadcasted_iota(jnp.int32, spread_lse.shape, 0) % span
        == lax.broadcasted_iota(jnp.int32, spread_lse.shape, 1) % span
    )
    spread_lse = jnp.where(on_diagonal, spread_lse, 0.0)
    lse_a = jnp.sum(spread_lse[:span], axis=0, keepdims=True)
    lse_b = jnp.sum(spread_lse[span:], axis=0, keepdims=True)
    product = attended.astype(f32) * grads.astype(f32)
    sides = (
        lax.broadcasted_iota(jnp.int32, (8, 256), 1) % 128 // HEAD_DIM
        == lax.broadcasted_iota(jnp.int32, (8, 256), 0)
    ).astype(bf16)
    high = product.astype(bf16)
    low = (product - high.astype(f32)).astype(bf16)
    dots = contract(sides, jnp.concatenate([high, low], 1), 1, 1)

    def spread(row_a, row_b):
        return jnp.concatenate(
            [jnp.broadcast_to(row_a, (rows, row_a.shape[1])), jnp.broadcast_to(row_b, (rows, row_b.shape[1]))], 0
        )

    scores = contract(two_heads(scaled(k_ref[...])), queries, 1, 1)
    probs = jnp.exp(scores + jnp.concatenate([bias, bias], 0) - spread(lse_a, lse_b))
    grad_probs = contract(two_heads(v_ref[...]), grads, 1, 1)
    grad_scores = (probs * (grad_probs - spread(dots[:1], dots[1:2]))).astype(bf16)
    dk_ref[...] = (one_pair(matmul(grad_scores, queries)) * SCALE).astype(bf16)
    dv_ref[...] = one_pair(matmul(probs.astype(bf16), grads)).astype(bf16)


def hidden_units_kernel(n2_ref, go_ref, fc_ref, fb_ref, proj_ref, gp_ref, gf_out_ref, bsum_ref, osum_ref):
    step = pl.program_id(0)

    @pl.when(step == 0)
    def _():
        for ref in (gp_ref, gf_out_ref, bsum_ref, osum_ref):
            ref[...] = jnp.zeros_like(ref)

    n2 = n2_ref[...].reshape(-1, D)
    go = go_ref[...].reshape(-1, D)
    pre = matmul(n2, fc_ref[...]) + fb_ref[...]
    activ, t = gelu_parts(pre)
    grad_pre = (contract(go, proj_ref[...], 1, 1) * gelu_slope(pre, t)).astype(bf16)
    gp_ref[...] += contract(activ.astype(bf16), go, 0, 0)
    gf_out_ref[...] += contract(n2, grad_pre, 0, 0)
    bsum_ref[...] += jnp.broadcast_to(jnp.sum(grad_pre.astype(f32), axis=0, keepdims=True), bsum_ref.shape)
    osum_ref[...] += jnp.broadcast_to(jnp.sum(go.astype(f32), axis=0, keepdims=True), osum_ref.shape)


def columns_kernel(me_ref, n1_ref, a_ref, cols_ref, grad_ref, sums_ref):
    step = pl.program_id(0)

    @pl.when(step == 0)
    def _():
        grad_ref[...] = jnp.zeros_like(grad_ref)
        sums_ref[...] = jnp.zeros_like(sums_ref)

    att = a_ref[...].reshape(-1, LANES)[:, :D]
    left = jnp.where(me_ref[0] < 12, n1_ref[...].reshape(-1, D), att)
    cols = cols_ref[...].reshape(-1, FROWS)
    grad_ref[...] += contract(left, cols, 0, 0)
    sums_ref[...] += jnp.broadcast_to(jnp.sum(cols.astype(f32), axis=0, keepdims=True), sums_ref.shape)


def params(flops, bytes_accessed, transcendentals=0, vmem=32):
    return dict(
        compiler_params=pltpu.CompilerParams(vmem_limit_bytes=vmem * 1024 * 1024),
        cost_estimate=pl.CostEstimate(
            flops=flops, bytes_accessed=bytes_accessed, transcendentals=transcendentals
        ),
    )


def shape(*dims, dtype=bf16):
    return jax.ShapeDtypeStruct(dims, dtype)


def whole_call(body, out_shape, operands, in_hbm=(), first_rows=(), scratch=(), flops=0, bytes_accessed=0, vmem=56):
    vm, hbm = pl.BlockSpec(memory_space=pltpu.VMEM), pl.BlockSpec(memory_space=pl.ANY)
    weight = pl.BlockSpec((8, 256, LANES), lambda s: (0, 0, 0))
    return pl.pallas_call(
        body,
        grid=(1,) if first_rows else (),
        in_specs=[
            hbm if i in in_hbm else weight if i in first_rows else vm for i in range(len(operands))
        ],
        out_specs=[vm] * len(out_shape),
        out_shape=out_shape,
        scratch_shapes=list(scratch),
        **params(flops, bytes_accessed, 0, vmem),
    )(*operands)


def pair_call(body, n_matmuls, in_specs, out_specs, out_shape, operands, vmem=32):
    steps = 2 * PAIRS
    return pl.pallas_call(
        body,
        grid=(2, PAIRS),
        in_specs=in_specs,
        out_specs=out_specs,
        out_shape=out_shape,
        **params(
            steps * n_matmuls * 2 * 128 * 128 * 1024 * 4, steps * 2 * 1024 * 128 * 2, steps * 128 * 1024, vmem
        ),
    )(*operands)


def own_spec(rows):
    return pl.BlockSpec((rows, 128), lambda m, h: (m, h))


def all_spec(kind, rows):
    return pl.BlockSpec((8, 1, 1, rows, 128), lambda m, h: (0, kind, m, 0, h))


def shards(
    inputs,
    segment_ids,
    sequence_order,
    ln1_gain,
    ln1_bias,
    w_qkv,
    qv_bias,
    w_out,
    out_bias,
    ln2_gain,
    ln2_bias,
    w_fc,
    fc_bias,
    w_proj,
    proj_bias,
    cotangent,
):
    section_index = lax.axis_index("section")
    me = lax.axis_index("fsdp")
    is_first = section_index == 0
    is_last = section_index == 1
    micro, span = inputs.shape[0], inputs.shape[1]
    tokens = micro * span
    seq_len = segment_ids.shape[1]

    def rows_padded(block):
        return jnp.pad(block, ((0, PROWS - block.shape[0]), (0, 0)))

    swapped = sequence_order[0, 0] == 1
    ordered_inputs = jnp.where(swapped, inputs[::-1], inputs).reshape(tokens, D)

    later = jnp.concatenate(
        [rows_padded(w_fc[0][:, j * D : (j + 1) * D]) for j in range(SPLITS)]
        + [rows_padded(w_out[0]), w_proj[0]],
        0,
    )
    later_all = lax.all_gather(later, "fsdp", axis=0, tiled=False)
    vectors = jnp.concatenate(
        [ln1_gain[0], ln1_bias[0], out_bias[0], ln2_gain[0], ln2_bias[0], proj_bias[0], qv_bias[0], fc_bias[0]]
    )
    vector_rows = jnp.pad(vectors[None], ((0, 15), (0, LANES - vectors.shape[0])))
    first = jnp.concatenate(
        [
            jnp.pad(w_qkv[0][:, j * D : (j + 1) * D], ((0, PROWS - DROWS), (0, LANES - D)))
            for j in range(3)
        ]
        + [vector_rows, jnp.pad(ordered_inputs, ((0, 0), (0, LANES - D)))],
        0,
    )
    first_near, first_far = gather_both(first)
    place_iota = jnp.arange(SHARDS)
    to_absolute = (relative_device(me, place_iota)[None, :] == place_iota[:, None]).astype(bf16)
    vector_rel = jnp.concatenate([first_near[:, 3 * PROWS], first_far[:, 3 * PROWS]], 0)
    vector_all = matmul(to_absolute, vector_rel)

    def vector(start, size):
        return vector_all[:, start : start + size].reshape(1, SHARDS * size)

    gain_one, bias_one, out_shift, gain_two, bias_two, proj_shift = [
        vector(j * DROWS, DROWS) for j in range(6)
    ]
    qv_full = vector(6 * DROWS, 2 * DROWS)
    fc_shift = vector(8 * DROWS, FROWS).reshape(SPLITS, D)
    shift_q = jnp.pad(qv_full[:, :D], ((0, 0), (0, LANES - D)))
    shift_v = jnp.pad(qv_full[:, D:], ((0, 0), (0, LANES - D)))

    place_rel = placing(me, True)
    place_abs = placing(me, False)

    ordered_segments = jnp.where(swapped, segment_ids[::-1], segment_ids)
    by_block = ordered_segments.reshape(micro, SHARDS, span)
    rel_devices = relative_device(me, place_iota)
    seg_rel = jnp.take(by_block, rel_devices, axis=1).reshape(micro, 1, seq_len)
    seg_own = lax.dynamic_index_in_dim(by_block, me, 1, keepdims=False)[:, :, None]
    pos_rel = (rel_devices[:, None] * span + jnp.arange(span)[None]).reshape(1, 1, seq_len)
    pos_own = (me * span + jnp.arange(span)).reshape(1, span, 1)
    same = seg_rel == seg_own
    row_bias = jnp.where(same & (pos_rel <= pos_own), 0.0, -1e30).astype(f32)
    column_bias = jnp.where(same & (pos_own <= pos_rel), 0.0, -1e30).astype(f32)
    me_scalar = me.astype(jnp.int32).reshape(1)

    bias_spec = pl.BlockSpec((1, span, seq_len), lambda m, h: (m, 0, 0))
    lse_spec = pl.BlockSpec((1, 1, 8, 128), lambda m, h: (m, h, 0, 0))
    kv_specs = [all_spec(0, span), all_spec(0, span), all_spec(1, span), all_spec(1, span)]
    token_shape = shape(tokens, LANES)
    buffers = [
        pltpu.VMEM((SPLITS, SHARDS, PROWS, D), bf16),
        pltpu.VMEM((SHARDS, PROWS, D), bf16),
        pltpu.VMEM((SPLITS, 4, FROWS, D), bf16),
        pltpu.SemaphoreType.DMA((1 + 2 * SPLITS,)),
    ]
    ffn_cost = dict(flops=4 * 2 * tokens * D * FF, bytes_accessed=2 * SHARDS * 672 * D, scratch=buffers)
    qkv_cost = dict(flops=4 * 2 * tokens * D * 3 * D, bytes_accessed=2 * SHARDS * 256 * LANES)

    def by_kind(block):
        return block.reshape(8, -1, micro, span, LANES)

    def attention(queries, kv_near, kv_far):
        return pair_call(
            forward_kernel,
            2,
            [own_spec(span)] + kv_specs + [bias_spec],
            [own_spec(span), lse_spec],
            [token_shape, shape(micro, PAIRS, 8, 128, dtype=f32)],
            (queries, kv_near, kv_far, kv_near, kv_far, row_bias),
        )

    ffn_shapes = [shape(tokens, D, dtype=f32), shape(tokens, D), shape(SPLITS, tokens, D, dtype=f32), shape(tokens, D)]
    back_shapes = [shape(tokens, D, dtype=f32), shape(tokens, D), token_shape, shape(8, D, dtype=f32)]
    vectors_two = (out_shift, gain_two, bias_two, proj_shift, fc_shift)

    step_fixed = lambda *dims: pl.BlockSpec(dims, lambda s: (0,) * len(dims))
    x_spec = pl.BlockSpec((1, tokens, LANES), lambda s: (s, 2, 0))
    kv_out = pl.BlockSpec((1, 2, tokens, LANES), lambda s: (s, 0, 0, 0))
    queries, kv_near, kv_far = pl.pallas_call(
        kv_all_kernel,
        grid=(8,),
        in_specs=[x_spec, x_spec, step_fixed(8, 256, LANES), step_fixed(8, 256, LANES), step_fixed(D, KPAD)]
        + [step_fixed(1, D), step_fixed(1, D), step_fixed(1, LANES), step_fixed(1, LANES)],
        out_specs=[step_fixed(tokens, LANES), kv_out, kv_out],
        out_shape=[token_shape, shape(8, 2, tokens, LANES), shape(8, 2, tokens, LANES)],
        **params(2 * SHARDS * tokens * D * 3 * D, 4 * SHARDS * 384 * LANES, vmem=48),
    )(first_near, first_far, first_near, first_far, place_rel, gain_one, bias_one, shift_q, shift_v)
    attended, _ = attention(queries, by_kind(kv_near), by_kind(kv_far))
    _, _, _, sent_on = whole_call(
        ffn_forward,
        ffn_shapes,
        (attended, ordered_inputs, place_abs, *vectors_two, later_all),
        in_hbm=(8,),
        **ffn_cost,
    )
    received = lax.ppermute(sent_on, "section", [(0, 1)])
    layer_in = jnp.where(is_first, ordered_inputs, received)

    own_cotangent = cotangent.reshape(tokens, D)
    normed_one, queries, keys_values = whole_call(
        qkv_kernel,
        [shape(tokens, D), token_shape, shape(2 * tokens, LANES)],
        (layer_in, first_near, first_far, place_rel, gain_one, bias_one, shift_q, shift_v),
        first_rows=(1, 2),
        **qkv_cost,
    )
    kv_near, kv_far = [by_kind(b) for b in gather_both(keys_values)]
    attended, log_total = attention(queries, kv_near, kv_far)
    hidden, normed_two, pre_act, out_low, *first_back = whole_call(
        ffn_both_kernel,
        ffn_shapes + back_shapes,
        (attended, layer_in, place_abs, *vectors_two, later_all, own_cotangent),
        in_hbm=(8,),
        **ffn_cost,
    )

    lse_own = log_total[:, :, 0]
    part_one = lax.reduce_precision(lse_own, 8, 7)
    part_two = lax.reduce_precision(lse_own - part_one, 8, 7)
    part_three = lse_own - part_one - part_two
    lse_rows = jnp.stack([part_one, part_two, part_three]).astype(bf16).reshape(6, LANES)
    qa_all = lax.all_gather(
        jnp.concatenate([queries, attended, lse_rows, jnp.zeros((10, LANES), bf16)], 0), "fsdp", axis=0
    )
    nn_all = lax.all_gather(jnp.concatenate([normed_one, normed_two], 0), "fsdp", axis=0)

    def backward_layer(feed_forward):
        grad_hidden, grad_branch, grad_att, sums_two = feed_forward
        def row_part():
            return pair_call(
                row_kernel,
                3,
                [own_spec(span), own_spec(span), lse_spec] + kv_specs + [bias_spec],
                own_spec(span),
                token_shape,
                (queries, grad_att, log_total, kv_near, kv_far, kv_near, kv_far, row_bias),
            )

        near, grad_q = gather_near(grad_att, row_part)
        do_near, do_far = by_kind(near), by_kind(moved(near, 1))
        own_half = lambda half: pl.BlockSpec((span, 128), lambda m, h: (2 * half + m, h))
        grad_k, grad_v = pair_call(
            column_kernel,
            5,
            [
                pl.BlockSpec(memory_space=pltpu.SMEM),
                own_half(0),
                own_half(1),
                pl.BlockSpec((SHARDS, span, 128), lambda m, h: (0, m, h)),
                pl.BlockSpec((SHARDS, span, 128), lambda m, h: (0, 2 + m, h)),
                pl.BlockSpec((SHARDS, 16, 128), lambda m, h: (0, 16, h)),
            ]
            + [all_spec(0, span), all_spec(0, span), bias_spec],
            [own_spec(span), own_spec(span)],
            [token_shape, token_shape],
            (
                me_scalar, keys_values, keys_values, qa_all, qa_all, qa_all, do_near, do_far, column_bias,
            ),
            vmem=60,
        )
        grad_input, sums_one = whole_call(
            qkv_back_kernel,
            [shape(tokens, D), shape(8, D, dtype=f32)],
            (grad_q, grad_k, grad_v, first_near, first_far, place_rel, layer_in, gain_one, grad_hidden),
            first_rows=(3, 4),
            **qkv_cost,
        )
        norm_grads = jnp.concatenate([sums_one[:2], sums_two[:2]], 0)
        return grad_input, grad_branch, (grad_q, grad_k, grad_v), norm_grads

    sent_back, _, _, _ = backward_layer(first_back)
    received_grad = lax.ppermute(sent_back, "section", [(1, 0)])
    grad_out = jnp.where(is_last, own_cotangent, received_grad)
    go_all = lax.all_gather(grad_out, "fsdp", axis=0)
    grad_input, grad_branch, grad_qkv, norm_grads = backward_layer(
        whole_call(
            ffn_back_kernel,
            back_shapes,
            (grad_out, pre_act, hidden, place_abs, gain_two, later_all),
            in_hbm=(5,),
            **ffn_cost,
        )
    )

    fc_own = lax.dynamic_slice(later_all, (0, (me // 4) * PROWS, (me % 4) * FROWS), (SHARDS, PROWS, FROWS))
    fc_own = fc_own[:, :DROWS].reshape(D, FROWS)
    fixed = lambda *dims: pl.BlockSpec(dims, lambda s: (0,) * len(dims))
    chip = lambda kind, width: pl.BlockSpec((2, tokens, width), lambda s: (s, kind, 0))
    grad_proj_w, grad_fc_w, grad_fc_b, out_sums = pl.pallas_call(
        hidden_units_kernel,
        grid=(8,),
        in_specs=[chip(1, D), chip(0, D), fixed(D, FROWS), fixed(1, FROWS), fixed(FROWS, D)],
        out_specs=[fixed(FROWS, D), fixed(D, FROWS), fixed(8, FROWS), fixed(8, D)],
        out_shape=[shape(FROWS, D, dtype=f32), shape(D, FROWS, dtype=f32), shape(8, FROWS, dtype=f32), shape(8, D, dtype=f32)],
        **params(4 * 4 * 2 * SHARDS * tokens * D * FROWS, 3 * 2 * SHARDS * tokens * D, vmem=60),
    )(nn_all, go_all, fc_own, fc_bias.astype(f32), w_proj[0])
    grad_proj_b = lax.dynamic_slice_in_dim(out_sums[0], me * DROWS, DROWS)
    wide = jnp.concatenate([g[:, :D] for g in grad_qkv] + [grad_branch], 1)
    wide = wide.reshape(tokens, SHARDS, FROWS).transpose(1, 0, 2)
    columns = lax.all_to_all(wide, "fsdp", 0, 0)
    columns, grad_fc_w, grad_proj_w = lax.optimization_barrier((columns, grad_fc_w, grad_proj_w))
    grad_columns, column_sums = pl.pallas_call(
        columns_kernel,
        grid=(8,),
        in_specs=[pl.BlockSpec(memory_space=pltpu.SMEM), chip(0, D), chip(1, LANES), chip(0, FROWS)],
        out_specs=[fixed(D, FROWS), fixed(8, FROWS)],
        out_shape=[shape(D, FROWS, dtype=f32), shape(8, FROWS, dtype=f32)],
        **params(4 * 2 * SHARDS * tokens * D * FROWS, 4 * 2 * SHARDS * tokens * D, vmem=60),
    )(me_scalar, nn_all, qa_all, columns)

    width, height = 384, 72
    z = lax.axis_index("replica")

    def to_owners(columns_of_rows):
        pads = ((0, 0), (0, height - columns_of_rows.shape[1]), (0, width - columns_of_rows.shape[2]))
        return lax.all_to_all(jnp.pad(columns_of_rows, pads), "fsdp", 0, 0)

    def over_replicas(quarter):
        pick = lambda k: lax.dynamic_index_in_dim(quarter, z ^ k, 0, keepdims=False)
        swap = lambda v, k: lax.ppermute(v, "replica", [(j, j ^ k) for j in range(4)])
        total = pick(0).astype(f32)
        for term in [swap(pick(k), k) for k in (1, 3, 2)]:
            total = total + term.astype(f32)
        total = total.astype(bf16)
        finished = jnp.stack([total] + [swap(total, k) for k in (1, 2, 3)])
        return jnp.take(finished, z ^ jnp.arange(4), axis=0)

    got_fc = to_owners(grad_fc_w.astype(bf16).reshape(SHARDS, DROWS, FROWS)).reshape(4, 4, height, width)
    got_fc, grad_columns = lax.optimization_barrier((got_fc, grad_columns))
    own_vectors = jnp.concatenate([grad_fc_b[0], grad_proj_b, jnp.zeros((3 * width - FROWS - DROWS,), f32)])
    proj_part = jnp.pad(grad_proj_w.reshape(4, DROWS, D), ((0, 0), (0, 0), (0, 3 * width - D)))
    own_part = jnp.broadcast_to(own_vectors[None, None], (4, height - DROWS, 3 * width))
    proj_part = jnp.concatenate([proj_part, own_part], 1).astype(bf16)
    proj_parts = [proj_part[:, None, :, j * width : (j + 1) * width] for j in range(3)]
    ffn_total = over_replicas(jnp.concatenate([got_fc] + proj_parts, 1))

    rows = jnp.concatenate(
        [
            grad_columns.astype(bf16).reshape(SHARDS, DROWS, FROWS),
            norm_grads.astype(bf16).reshape(4, SHARDS, DROWS).transpose(1, 2, 0),
        ],
        2,
    )
    rows = jnp.pad(rows, ((0, 0), (0, 0), (0, width - rows.shape[2])))
    sums_row = jnp.broadcast_to(
        jnp.pad(column_sums[0].astype(bf16), (0, width - FROWS))[None, None], (SHARDS, 1, width)
    )
    got = to_owners(jnp.concatenate([rows, sums_row], 1))
    got, ffn_total = lax.optimization_barrier((got, ffn_total))
    finished = over_replicas(got.reshape(4, 4, height, width)).reshape(SHARDS, height, width).astype(f32)
    proj_total = jnp.concatenate([ffn_total[:, 4], ffn_total[:, 5], ffn_total[:, 6]], 2).astype(f32)
    fc_total = ffn_total[:, :4].reshape(SHARDS, height, width).astype(f32)

    def joined(block):
        return block.transpose(1, 0, 2).reshape(block.shape[1], -1)

    grad_w_qkv = joined(finished[:12, :DROWS, :FROWS])
    grad_w_out = joined(finished[12:, :DROWS, :FROWS])
    grad_w_fc = joined(fc_total[:, :DROWS, :FROWS])
    norm_sums = jnp.sum(finished[:, :DROWS, FROWS : FROWS + 4], axis=0)
    sums = finished[:, DROWS, :FROWS].reshape(SHARDS * FROWS)
    qv_sums = jnp.concatenate([sums[:D], sums[2 * D : 3 * D]])
    grad_qv_b = lax.dynamic_slice_in_dim(qv_sums, me * 2 * DROWS, 2 * DROWS)
    grad_out_b = lax.dynamic_slice_in_dim(sums, 3 * D + me * DROWS, DROWS)
    totals = (
        norm_sums[:, 0],
        norm_sums[:, 1],
        grad_w_qkv,
        grad_qv_b,
        grad_w_out,
        grad_out_b,
        norm_sums[:, 2],
        norm_sums[:, 3],
        grad_w_fc,
        proj_total[0, DROWS, :FROWS],
        proj_total[:, :DROWS, :D].reshape(FROWS, D),
        proj_total[0, DROWS, FROWS : FROWS + DROWS],
    )
    activations = out_low.reshape(1, micro, span, D)
    input_grads = grad_input.reshape(1, micro, span, D)
    return (activations, input_grads) + tuple((total[None] for total in totals))


def solution(mesh):
    return jax.shard_map(
        shards,
        mesh=mesh,
        in_specs=(
            P("replica", "fsdp", None),
            P("replica", None),
            P("replica", None),
            P("section", "fsdp"),
            P("section", "fsdp"),
            P("section", "fsdp", None),
            P("section", "fsdp"),
            P("section", "fsdp", None),
            P("section", "fsdp"),
            P("section", "fsdp"),
            P("section", "fsdp"),
            P("section", "fsdp", None),
            P("section", "fsdp"),
            P("section", "fsdp", None),
            P("section", "fsdp"),
            P("replica", "fsdp", None),
        ),
        out_specs=(
            P("section", "replica", "fsdp", None),
            P("section", "replica", "fsdp", None),
            P("section", "fsdp"),
            P("section", "fsdp"),
            P("section", "fsdp", None),
            P("section", "fsdp"),
            P("section", "fsdp", None),
            P("section", "fsdp"),
            P("section", "fsdp"),
            P("section", "fsdp"),
            P("section", "fsdp", None),
            P("section", "fsdp"),
            P("section", "fsdp", None),
            P("section", "fsdp"),
        ),
        check_vma=False,
    )
```

```python
import jax
import jax.numpy as jnp
from jax import lax
from jax.experimental import pallas as pl
from jax.experimental.pallas import tpu as pltpu
from jax.sharding import PartitionSpec as P

D = 1088
HEADS = 17
HEAD_DIM = 64
FF = 4352
SHARDS = 16
DROWS = D // SHARDS
PROWS = 80
KPAD = SHARDS * PROWS
LANES = 1152
PAIRS = 9
FROWS = FF // SHARDS
SPLITS = FF // D
SCALE = HEAD_DIM ** (-0.5)

HALF = KPAD // 2
OUT_AT = SPLITS * PROWS
PROJ_AT = OUT_AT + PROWS
GELU_C = 0.7978845608028654
GELU_A = 0.044715

epsilon = 1e-05
bf16 = jnp.bfloat16
f32 = jnp.float32


def xor_pairs(k):
    return [(i, i ^ k) for i in range(SHARDS)]


def moved(value, k):
    return lax.ppermute(value, "fsdp", xor_pairs(k))


def gather_near(x, beside=None):
    half = x.shape[0] // 2
    blocks = {0: x, 4: moved(x, 4), 12: moved(x, 12), 2: moved(x, 2)}
    result = None
    if beside is not None:
        blocks[8] = moved(x, 8)
        first = (4, 12, 2, 8)
        *arrived, result = lax.optimization_barrier((*[blocks[k] for k in first], beside()))
        blocks.update(zip(first, arrived))
    else:
        blocks[8] = jnp.concatenate([moved(blocks[4][:half], 12), moved(blocks[12][half:], 4)], 0)
    blocks[6] = moved(blocks[2], 4)
    blocks[14] = moved(blocks[2], 12)
    blocks[10] = moved(blocks[8], 2)
    return jnp.stack([blocks[k] for k in range(0, SHARDS, 2)]), result


def gather_both(x):
    near, _ = gather_near(x)
    return near, moved(near, 1)


def relative_device(me, place):
    return me ^ (2 * (place % 8) + place // 8)


def placing(me, relative):
    column = lax.broadcasted_iota(jnp.int32, (1, KPAD), 1)
    place, row = column // PROWS, column % PROWS
    owner = relative_device(me, place) if relative else place
    source = jnp.where(row < DROWS, owner * DROWS + row, -1)
    return (lax.broadcasted_iota(jnp.int32, (D, KPAD), 0) == source).astype(bf16)


def matmul(left, right):
    return jnp.dot(left, right, preferred_element_type=f32)


def contract(left, right, ldim, rdim):
    return lax.dot_general(left, right, (((ldim,), (rdim,)), ((), ())), preferred_element_type=f32)


def split_two(values):
    high = lax.reduce_precision(values, 8, 7)
    return high.astype(bf16), (values - high).astype(bf16)


def unplaced(values, place):
    rows = values.shape[0]
    both = contract(jnp.concatenate(split_two(values), 0), place, 1, 1)
    return both[:rows] + both[rows:]


def two_heads(block):
    lane = lax.broadcasted_iota(jnp.int32, block.shape, 1)
    zero = jnp.zeros_like(block)
    return jnp.concatenate(
        [jnp.where(lane < HEAD_DIM, block, zero), jnp.where(lane < HEAD_DIM, zero, block)], 0
    )


def scaled(block):
    return (block.astype(f32) * SCALE).astype(bf16)


def one_pair(both):
    rows = both.shape[0] // 2
    lane = lax.broadcasted_iota(jnp.int32, (rows, 128), 1)
    return jnp.where(lane < HEAD_DIM, both[:rows], both[rows:])


def rows_of(near_ref, far_ref):
    return jnp.concatenate(
        [near_ref[...].reshape(-1, 128), far_ref[...].reshape(-1, 128)], 0
    )


def forward_kernel(q_ref, kn_ref, kf_ref, vn_ref, vf_ref, bias_ref, out_ref, lse_ref):
    bias = bias_ref[0]
    keys, values = rows_of(kn_ref, kf_ref), rows_of(vn_ref, vf_ref)
    scores = contract(two_heads(scaled(q_ref[...])), keys, 1, 1) + jnp.concatenate([bias, bias], 0)
    top = jnp.max(scores, axis=1, keepdims=True)
    shifted = jnp.exp(scores - top)
    total = jnp.sum(shifted, axis=1, keepdims=True)
    probs = (shifted / total).astype(bf16)
    out_ref[...] = one_pair(matmul(probs, values)).astype(bf16)
    lse = top + jnp.log(total)
    lse_ref[0, 0] = jnp.transpose(jnp.broadcast_to(lse, (128, 128)))[:8]


def row_kernel(q_ref, do_ref, lse_ref, kn_ref, kf_ref, vn_ref, vf_ref, bias_ref, dq_ref):
    bias = bias_ref[0]
    keys, values = rows_of(kn_ref, kf_ref), rows_of(vn_ref, vf_ref)
    lse = jnp.transpose(jnp.broadcast_to(lse_ref[0, 0][:1], (128, 128)))[:, :1]
    scores = contract(two_heads(scaled(q_ref[...])), keys, 1, 1) + jnp.concatenate([bias, bias], 0)
    probs = jnp.exp(scores - lse)
    grad_probs = contract(two_heads(do_ref[...]), values, 1, 1)
    dots = jnp.sum(grad_probs * probs, axis=1, keepdims=True)
    grad_scores = (probs * (grad_probs - dots)).astype(bf16)
    dq_ref[...] = (one_pair(matmul(grad_scores, keys)) * SCALE).astype(bf16)


def normalized(values):
    centred = values - jnp.mean(values, axis=1, keepdims=True)
    scale = lax.rsqrt(jnp.mean(centred * centred, axis=1, keepdims=True) + epsilon)
    return centred * scale, scale


def norm_back(values, gain, grad):
    z, scale = normalized(values)
    weighted = grad * gain
    by_values = scale * (
        weighted
        - jnp.mean(weighted, axis=1, keepdims=True)
        - z * jnp.mean(weighted * z, axis=1, keepdims=True)
    )
    row = lax.broadcasted_iota(jnp.int32, (8, D), 0)
    gain_sum = jnp.sum(grad * z, axis=0, keepdims=True)
    bias_sum = jnp.sum(grad, axis=0, keepdims=True)
    return by_values, jnp.where(row == 0, gain_sum, jnp.where(row == 1, bias_sum, 0.0))


def gelu_parts(v):
    t = jnp.tanh(GELU_C * (v + GELU_A * v * v * v))
    return 0.5 * v * (1.0 + t), t


def gelu_slope(v, t):
    return 0.5 * (1.0 + t) + 0.5 * v * (1.0 - t * t) * (GELU_C * (1.0 + 3.0 * GELU_A * v * v))


def unplaced(values, place):
    rows = values.shape[0]
    high = values.astype(bf16)
    low = (values - high.astype(f32)).astype(bf16)
    both = contract(jnp.concatenate([high, low], 0), place, 1, 1)
    return both[:rows] + both[rows:]


def input_weight(near_ref, far_ref, j):
    rows = slice(j * PROWS, (j + 1) * PROWS)
    return near_ref[:, rows, :].reshape(HALF, LANES), far_ref[:, rows, :].reshape(HALF, LANES)


def qkv_kernel(x_ref, near_ref, far_ref, place_ref, gain_ref, bias_ref, sq_ref, sv_ref, n1_ref, q_ref, kv_ref):
    z, _ = normalized(x_ref[...].astype(f32))
    normed = (z * gain_ref[...] + bias_ref[...]).astype(bf16)
    n1_ref[...] = normed
    placed = matmul(normed, place_ref[...]).astype(bf16)
    rows = placed.shape[0]

    def product(j):
        near, far = input_weight(near_ref, far_ref, j)
        return matmul(placed[:, :HALF], near) + matmul(placed[:, HALF:], far)

    kv_ref[:rows] = product(1).astype(bf16)
    kv_ref[rows:] = (product(2) + sv_ref[...]).astype(bf16)
    q_ref[...] = (product(0) + sq_ref[...]).astype(bf16)


def kv_all_kernel(xn_ref, xf_ref, near_ref, far_ref, place_ref, gain_ref, bias_ref, sq_ref, sv_ref, q_ref, kn_ref, kf_ref):
    rows = xn_ref.shape[1]
    x = jnp.concatenate([xn_ref[0], xf_ref[0]], 0)[:, :D]
    z, _ = normalized(x.astype(f32))
    normed = (z * gain_ref[...] + bias_ref[...]).astype(bf16)
    placed = matmul(normed, place_ref[...]).astype(bf16)

    def product(left, j):
        near, far = input_weight(near_ref, far_ref, j)
        return matmul(left[:, :HALF], near) + matmul(left[:, HALF:], far)

    keys = product(placed, 1).astype(bf16)
    values = (product(placed, 2) + sv_ref[...]).astype(bf16)
    kn_ref[0, 0], kn_ref[0, 1] = keys[:rows], values[:rows]
    kf_ref[0, 0], kf_ref[0, 1] = keys[rows:], values[rows:]

    @pl.when(pl.program_id(0) == 0)
    def _():
        q_ref[...] = (product(placed[:rows], 0) + sq_ref[...]).astype(bf16)


def qkv_back_kernel(dq_ref, dk_ref, dv_ref, near_ref, far_ref, place_ref, x_ref, gain_ref, gh_ref, gin_ref, sums_ref):
    near_sum, far_sum = 0.0, 0.0
    for j, ref in enumerate((dq_ref, dk_ref, dv_ref)):
        near, far = input_weight(near_ref, far_ref, j)
        near_sum = near_sum + contract(ref[...], near, 1, 1)
        far_sum = far_sum + contract(ref[...], far, 1, 1)
    grad = unplaced(jnp.concatenate([near_sum, far_sum], 1), place_ref[...])
    by_input, sums_ref[...] = norm_back(x_ref[...].astype(f32), gain_ref[...], grad)
    gin_ref[...] = (gh_ref[...] + by_input).astype(bf16)


def weight_copies(all_ref, fc_buf, out_buf, proj_buf, sems):
    out_copy = pltpu.make_async_copy(all_ref.at[:, pl.ds(OUT_AT, PROWS), :], out_buf, sems.at[0])
    fc = [
        pltpu.make_async_copy(all_ref.at[:, pl.ds(j * PROWS, PROWS), :], fc_buf.at[j], sems.at[1 + j])
        for j in range(SPLITS)
    ]
    proj = [
        pltpu.make_async_copy(
            all_ref.at[pl.ds(4 * j, 4), pl.ds(PROJ_AT, FROWS), :], proj_buf.at[j], sems.at[1 + SPLITS + j]
        )
        for j in range(SPLITS)
    ]
    return out_copy, fc, proj


def ffn_forward(
    att_ref, x_ref, place_ref, os_ref, gain_ref, bias_ref, ps_ref, fs_ref, all_ref,
    hidden_ref, n2_ref, pre_ref, out_ref, fc_buf, out_buf, proj_buf, sems,
):
    out_copy, fc, proj = weight_copies(all_ref, fc_buf, out_buf, proj_buf, sems)
    out_copy.start()
    for j in range(SPLITS):
        fc[j].start()
        proj[j].start()
    place = place_ref[...]
    placed = matmul(att_ref[:, :D], place).astype(bf16)
    out_copy.wait()
    hidden = x_ref[...].astype(f32) + matmul(placed, out_buf[...].reshape(KPAD, D)) + os_ref[...]
    hidden_ref[...] = hidden
    z, _ = normalized(hidden)
    normed = (z * gain_ref[...] + bias_ref[...]).astype(bf16)
    n2_ref[...] = normed
    placed = matmul(normed, place).astype(bf16)
    total = hidden + ps_ref[...]
    for j in range(SPLITS):
        fc[j].wait()
        pre = matmul(placed, fc_buf[j].reshape(KPAD, D)) + fs_ref[j : j + 1]
        pre_ref[j] = pre
        activ, _ = gelu_parts(pre)
        proj[j].wait()
        total = total + matmul(activ.astype(bf16), proj_buf[j].reshape(D, D))
    out_ref[...] = total.astype(bf16)


def ffn_backward(
    go_ref, pre_ref, hidden_ref, place_ref, gain_ref, ready,
    gh_ref, gb_ref, ga_ref, sums_ref, fc_buf, out_buf, proj_buf,
):
    grad_out = go_ref[...]
    placed = 0.0
    for j in range(SPLITS):
        pre = pre_ref[j]
        _, t = gelu_parts(pre)
        slope = gelu_slope(pre, t)
        ready("proj", j)
        grad_pre = (contract(grad_out, proj_buf[j].reshape(D, D), 1, 1) * slope).astype(bf16)
        ready("fc", j)
        placed = placed + contract(grad_pre, fc_buf[j].reshape(KPAD, D), 1, 1)
    place = place_ref[...]
    by_hidden, sums_ref[...] = norm_back(hidden_ref[...], gain_ref[...], unplaced(placed, place))
    grad_hidden = grad_out.astype(f32) + by_hidden
    gh_ref[...] = grad_hidden
    branch = grad_hidden.astype(bf16)
    gb_ref[...] = branch
    ready("out", 0)
    grad_att = contract(branch, out_buf[...].reshape(KPAD, D), 1, 1).astype(bf16)
    ga_ref[...] = jnp.zeros_like(ga_ref)
    ga_ref[:, :D] = contract(grad_att, place, 1, 1).astype(bf16)


def ffn_back_kernel(
    go_ref, pre_ref, hidden_ref, place_ref, gain_ref, all_ref,
    gh_ref, gb_ref, ga_ref, sums_ref, fc_buf, out_buf, proj_buf, sems,
):
    out_copy, fc, proj = weight_copies(all_ref, fc_buf, out_buf, proj_buf, sems)
    for j in range(SPLITS):
        proj[j].start()
        fc[j].start()
    out_copy.start()
    copies = {"proj": proj, "fc": fc, "out": [out_copy]}
    ffn_backward(
        go_ref, pre_ref, hidden_ref, place_ref, gain_ref, lambda kind, j: copies[kind][j].wait(),
        gh_ref, gb_ref, ga_ref, sums_ref, fc_buf, out_buf, proj_buf,
    )


def ffn_both_kernel(
    att_ref, x_ref, place_ref, os_ref, gain_ref, bias_ref, ps_ref, fs_ref, all_ref, go_ref,
    hidden_ref, n2_ref, pre_ref, out_ref, gh_ref, gb_ref, ga_ref, sums_ref, fc_buf, out_buf, proj_buf, sems,
):
    ffn_forward(
        att_ref, x_ref, place_ref, os_ref, gain_ref, bias_ref, ps_ref, fs_ref, all_ref,
        hidden_ref, n2_ref, pre_ref, out_ref, fc_buf, out_buf, proj_buf, sems,
    )
    ffn_backward(
        go_ref, pre_ref, hidden_ref, place_ref, gain_ref, lambda kind, j: None,
        gh_ref, gb_ref, ga_ref, sums_ref, fc_buf, out_buf, proj_buf,
    )


def column_kernel(me_ref, k_ref, v_ref, q_ref, a_ref, lse_ref, don_ref, dof_ref, bias_ref, dk_ref, dv_ref):
    me = me_ref[0]
    owners = [relative_device(me, place) for place in range(SHARDS)]
    queries = jnp.concatenate([q_ref[owner] for owner in owners], 0)
    attended = jnp.concatenate([a_ref[owner] for owner in owners], 0)
    grads = rows_of(don_ref, dof_ref)
    rows = k_ref.shape[0]
    span = q_ref.shape[1]
    bias = bias_ref[0]
    micro = pl.program_id(0)
    term_row = lax.broadcasted_iota(jnp.int32, (16, 128), 0)
    terms = (3 * SHARDS, SHARDS * span)
    place_of = (
        lax.broadcasted_iota(jnp.int32, terms, 1) // span == lax.broadcasted_iota(jnp.int32, terms, 0) % SHARDS
    ).astype(bf16)
    picked = [
        jnp.sum(jnp.where(term_row == 2 * term + micro, lse_ref[owner].astype(f32), 0.0), axis=0, keepdims=True)
        for term in range(3)
        for owner in owners
    ]
    spread_lse = contract(jnp.concatenate(picked, 0).astype(bf16), place_of, 0, 0)
    on_diagonal = (
        lax.broadcasted_iota(jnp.int32, spread_lse.shape, 0) % span
        == lax.broadcasted_iota(jnp.int32, spread_lse.shape, 1) % span
    )
    spread_lse = jnp.where(on_diagonal, spread_lse, 0.0)
    lse_a = jnp.sum(spread_lse[:span], axis=0, keepdims=True)
    lse_b = jnp.sum(spread_lse[span:], axis=0, keepdims=True)
    product = attended.astype(f32) * grads.astype(f32)
    sides = (
        lax.broadcasted_iota(jnp.int32, (8, 256), 1) % 128 // HEAD_DIM
        == lax.broadcasted_iota(jnp.int32, (8, 256), 0)
    ).astype(bf16)
    high = product.astype(bf16)
    low = (product - high.astype(f32)).astype(bf16)
    dots = contract(sides, jnp.concatenate([high, low], 1), 1, 1)

    def spread(row_a, row_b):
        return jnp.concatenate(
            [jnp.broadcast_to(row_a, (rows, row_a.shape[1])), jnp.broadcast_to(row_b, (rows, row_b.shape[1]))], 0
        )

    scores = contract(two_heads(scaled(k_ref[...])), queries, 1, 1)
    probs = jnp.exp(scores + jnp.concatenate([bias, bias], 0) - spread(lse_a, lse_b))
    grad_probs = contract(two_heads(v_ref[...]), grads, 1, 1)
    grad_scores = (probs * (grad_probs - spread(dots[:1], dots[1:2]))).astype(bf16)
    dk_ref[...] = (one_pair(matmul(grad_scores, queries)) * SCALE).astype(bf16)
    dv_ref[...] = one_pair(matmul(probs.astype(bf16), grads)).astype(bf16)


def hidden_units_kernel(n2_ref, go_ref, fc_ref, fb_ref, proj_ref, gp_ref, gf_out_ref, bsum_ref, osum_ref):
    step = pl.program_id(0)

    @pl.when(step == 0)
    def _():
        for ref in (gp_ref, gf_out_ref, bsum_ref, osum_ref):
            ref[...] = jnp.zeros_like(ref)

    n2 = n2_ref[...].reshape(-1, D)
    go = go_ref[...].reshape(-1, D)
    pre = matmul(n2, fc_ref[...]) + fb_ref[...]
    activ, t = gelu_parts(pre)
    grad_pre = (contract(go, proj_ref[...], 1, 1) * gelu_slope(pre, t)).astype(bf16)
    gp_ref[...] += contract(activ.astype(bf16), go, 0, 0)
    gf_out_ref[...] += contract(n2, grad_pre, 0, 0)
    bsum_ref[...] += jnp.broadcast_to(jnp.sum(grad_pre.astype(f32), axis=0, keepdims=True), bsum_ref.shape)
    osum_ref[...] += jnp.broadcast_to(jnp.sum(go.astype(f32), axis=0, keepdims=True), osum_ref.shape)


def columns_kernel(me_ref, n1_ref, a_ref, cols_ref, grad_ref, sums_ref):
    step = pl.program_id(0)

    @pl.when(step == 0)
    def _():
        grad_ref[...] = jnp.zeros_like(grad_ref)
        sums_ref[...] = jnp.zeros_like(sums_ref)

    att = a_ref[...].reshape(-1, LANES)[:, :D]
    left = jnp.where(me_ref[0] < 12, n1_ref[...].reshape(-1, D), att)
    cols = cols_ref[...].reshape(-1, FROWS)
    grad_ref[...] += contract(left, cols, 0, 0)
    sums_ref[...] += jnp.broadcast_to(jnp.sum(cols.astype(f32), axis=0, keepdims=True), sums_ref.shape)


def params(flops, bytes_accessed, transcendentals=0, vmem=32):
    return dict(
        compiler_params=pltpu.CompilerParams(vmem_limit_bytes=vmem * 1024 * 1024),
        cost_estimate=pl.CostEstimate(
            flops=flops, bytes_accessed=bytes_accessed, transcendentals=transcendentals
        ),
    )


def shape(*dims, dtype=bf16):
    return jax.ShapeDtypeStruct(dims, dtype)


def whole_call(body, out_shape, operands, in_hbm=(), first_rows=(), scratch=(), flops=0, bytes_accessed=0, vmem=56):
    vm, hbm = pl.BlockSpec(memory_space=pltpu.VMEM), pl.BlockSpec(memory_space=pl.ANY)
    weight = pl.BlockSpec((8, 256, LANES), lambda s: (0, 0, 0))
    return pl.pallas_call(
        body,
        grid=(1,) if first_rows else (),
        in_specs=[
            hbm if i in in_hbm else weight if i in first_rows else vm for i in range(len(operands))
        ],
        out_specs=[vm] * len(out_shape),
        out_shape=out_shape,
        scratch_shapes=list(scratch),
        **params(flops, bytes_accessed, 0, vmem),
    )(*operands)


def pair_call(body, n_matmuls, in_specs, out_specs, out_shape, operands, vmem=32):
    steps = 2 * PAIRS
    return pl.pallas_call(
        body,
        grid=(2, PAIRS),
        in_specs=in_specs,
        out_specs=out_specs,
        out_shape=out_shape,
        **params(
            steps * n_matmuls * 2 * 128 * 128 * 1024 * 4, steps * 2 * 1024 * 128 * 2, steps * 128 * 1024, vmem
        ),
    )(*operands)


def own_spec(rows):
    return pl.BlockSpec((rows, 128), lambda m, h: (m, h))


def all_spec(kind, rows):
    return pl.BlockSpec((8, 1, 1, rows, 128), lambda m, h: (0, kind, m, 0, h))


def shards(
    inputs,
    segment_ids,
    sequence_order,
    ln1_gain,
    ln1_bias,
    w_qkv,
    qv_bias,
    w_out,
    out_bias,
    ln2_gain,
    ln2_bias,
    w_fc,
    fc_bias,
    w_proj,
    proj_bias,
    cotangent,
):
    section_index = lax.axis_index("section")
    me = lax.axis_index("fsdp")
    is_first = section_index == 0
    is_last = section_index == 1
    micro, span = inputs.shape[0], inputs.shape[1]
    tokens = micro * span
    seq_len = segment_ids.shape[1]

    def rows_padded(block):
        return jnp.pad(block, ((0, PROWS - block.shape[0]), (0, 0)))

    swapped = sequence_order[0, 0] == 1
    ordered_inputs = jnp.where(swapped, inputs[::-1], inputs).reshape(tokens, D)

    later = jnp.concatenate(
        [rows_padded(w_fc[0][:, j * D : (j + 1) * D]) for j in range(SPLITS)]
        + [rows_padded(w_out[0]), w_proj[0]],
        0,
    )
    later_all = lax.all_gather(later, "fsdp", axis=0, tiled=False)
    vectors = jnp.concatenate(
        [ln1_gain[0], ln1_bias[0], out_bias[0], ln2_gain[0], ln2_bias[0], proj_bias[0], qv_bias[0], fc_bias[0]]
    )
    vector_rows = jnp.pad(vectors[None], ((0, 15), (0, LANES - vectors.shape[0])))
    first = jnp.concatenate(
        [
            jnp.pad(w_qkv[0][:, j * D : (j + 1) * D], ((0, PROWS - DROWS), (0, LANES - D)))
            for j in range(3)
        ]
        + [vector_rows, jnp.pad(ordered_inputs, ((0, 0), (0, LANES - D)))],
        0,
    )
    first_near, first_far = gather_both(first)
    place_iota = jnp.arange(SHARDS)
    to_absolute = (relative_device(me, place_iota)[None, :] == place_iota[:, None]).astype(bf16)
    vector_rel = jnp.concatenate([first_near[:, 3 * PROWS], first_far[:, 3 * PROWS]], 0)
    vector_all = matmul(to_absolute, vector_rel)

    def vector(start, size):
        return vector_all[:, start : start + size].reshape(1, SHARDS * size)

    gain_one, bias_one, out_shift, gain_two, bias_two, proj_shift = [
        vector(j * DROWS, DROWS) for j in range(6)
    ]
    qv_full = vector(6 * DROWS, 2 * DROWS)
    fc_shift = vector(8 * DROWS, FROWS).reshape(SPLITS, D)
    shift_q = jnp.pad(qv_full[:, :D], ((0, 0), (0, LANES - D)))
    shift_v = jnp.pad(qv_full[:, D:], ((0, 0), (0, LANES - D)))

    place_rel = placing(me, True)
    place_abs = placing(me, False)

    ordered_segments = jnp.where(swapped, segment_ids[::-1], segment_ids)
    by_block = ordered_segments.reshape(micro, SHARDS, span)
    rel_devices = relative_device(me, place_iota)
    seg_rel = jnp.take(by_block, rel_devices, axis=1).reshape(micro, 1, seq_len)
    seg_own = lax.dynamic_index_in_dim(by_block, me, 1, keepdims=False)[:, :, None]
    pos_rel = (rel_devices[:, None] * span + jnp.arange(span)[None]).reshape(1, 1, seq_len)
    pos_own = (me * span + jnp.arange(span)).reshape(1, span, 1)
    same = seg_rel == seg_own
    row_bias = jnp.where(same & (pos_rel <= pos_own), 0.0, -1e30).astype(f32)
    column_bias = jnp.where(same & (pos_own <= pos_rel), 0.0, -1e30).astype(f32)
    me_scalar = me.astype(jnp.int32).reshape(1)

    bias_spec = pl.BlockSpec((1, span, seq_len), lambda m, h: (m, 0, 0))
    lse_spec = pl.BlockSpec((1, 1, 8, 128), lambda m, h: (m, h, 0, 0))
    kv_specs = [all_spec(0, span), all_spec(0, span), all_spec(1, span), all_spec(1, span)]
    token_shape = shape(tokens, LANES)
    buffers = [
        pltpu.VMEM((SPLITS, SHARDS, PROWS, D), bf16),
        pltpu.VMEM((SHARDS, PROWS, D), bf16),
        pltpu.VMEM((SPLITS, 4, FROWS, D), bf16),
        pltpu.SemaphoreType.DMA((1 + 2 * SPLITS,)),
    ]
    ffn_cost = dict(flops=4 * 2 * tokens * D * FF, bytes_accessed=2 * SHARDS * 672 * D, scratch=buffers)
    qkv_cost = dict(flops=4 * 2 * tokens * D * 3 * D, bytes_accessed=2 * SHARDS * 256 * LANES)

    def by_kind(block):
        return block.reshape(8, -1, micro, span, LANES)

    def attention(queries, kv_near, kv_far):
        return pair_call(
            forward_kernel,
            2,
            [own_spec(span)] + kv_specs + [bias_spec],
            [own_spec(span), lse_spec],
            [token_shape, shape(micro, PAIRS, 8, 128, dtype=f32)],
            (queries, kv_near, kv_far, kv_near, kv_far, row_bias),
        )

    ffn_shapes = [shape(tokens, D, dtype=f32), shape(tokens, D), shape(SPLITS, tokens, D, dtype=f32), shape(tokens, D)]
    back_shapes = [shape(tokens, D, dtype=f32), shape(tokens, D), token_shape, shape(8, D, dtype=f32)]
    vectors_two = (out_shift, gain_two, bias_two, proj_shift, fc_shift)

    step_fixed = lambda *dims: pl.BlockSpec(dims, lambda s: (0,) * len(dims))
    x_spec = pl.BlockSpec((1, tokens, LANES), lambda s: (s, 2, 0))
    kv_out = pl.BlockSpec((1, 2, tokens, LANES), lambda s: (s, 0, 0, 0))
    queries, kv_near, kv_far = pl.pallas_call(
        kv_all_kernel,
        grid=(8,),
        in_specs=[x_spec, x_spec, step_fixed(8, 256, LANES), step_fixed(8, 256, LANES), step_fixed(D, KPAD)]
        + [step_fixed(1, D), step_fixed(1, D), step_fixed(1, LANES), step_fixed(1, LANES)],
        out_specs=[step_fixed(tokens, LANES), kv_out, kv_out],
        out_shape=[token_shape, shape(8, 2, tokens, LANES), shape(8, 2, tokens, LANES)],
        **params(2 * SHARDS * tokens * D * 3 * D, 4 * SHARDS * 384 * LANES, vmem=48),
    )(first_near, first_far, first_near, first_far, place_rel, gain_one, bias_one, shift_q, shift_v)
    attended, _ = attention(queries, by_kind(kv_near), by_kind(kv_far))
    _, _, _, sent_on = whole_call(
        ffn_forward,
        ffn_shapes,
        (attended, ordered_inputs, place_abs, *vectors_two, later_all),
        in_hbm=(8,),
        **ffn_cost,
    )
    received = lax.ppermute(sent_on, "section", [(0, 1)])
    layer_in = jnp.where(is_first, ordered_inputs, received)

    own_cotangent = cotangent.reshape(tokens, D)
    normed_one, queries, keys_values = whole_call(
        qkv_kernel,
        [shape(tokens, D), token_shape, shape(2 * tokens, LANES)],
        (layer_in, first_near, first_far, place_rel, gain_one, bias_one, shift_q, shift_v),
        first_rows=(1, 2),
        **qkv_cost,
    )
    kv_near, kv_far = [by_kind(b) for b in gather_both(keys_values)]
    attended, log_total = attention(queries, kv_near, kv_far)
    hidden, normed_two, pre_act, out_low, *first_back = whole_call(
        ffn_both_kernel,
        ffn_shapes + back_shapes,
        (attended, layer_in, place_abs, *vectors_two, later_all, own_cotangent),
        in_hbm=(8,),
        **ffn_cost,
    )

    lse_own = log_total[:, :, 0]
    part_one = lax.reduce_precision(lse_own, 8, 7)
    part_two = lax.reduce_precision(lse_own - part_one, 8, 7)
    part_three = lse_own - part_one - part_two
    lse_rows = jnp.stack([part_one, part_two, part_three]).astype(bf16).reshape(6, LANES)
    qa_all = lax.all_gather(
        jnp.concatenate([queries, attended, lse_rows, jnp.zeros((10, LANES), bf16)], 0), "fsdp", axis=0
    )
    nn_all = lax.all_gather(jnp.concatenate([normed_one, normed_two], 0), "fsdp", axis=0)

    def backward_layer(feed_forward):
        grad_hidden, grad_branch, grad_att, sums_two = feed_forward
        def row_part():
            return pair_call(
                row_kernel,
                3,
                [own_spec(span), own_spec(span), lse_spec] + kv_specs + [bias_spec],
                own_spec(span),
                token_shape,
                (queries, grad_att, log_total, kv_near, kv_far, kv_near, kv_far, row_bias),
                vmem=60,
            )

        near, grad_q = gather_near(grad_att, row_part)
        do_near, do_far = by_kind(near), by_kind(moved(near, 1))
        own_half = lambda half: pl.BlockSpec((span, 128), lambda m, h: (2 * half + m, h))
        grad_k, grad_v = pair_call(
            column_kernel,
            5,
            [
                pl.BlockSpec(memory_space=pltpu.SMEM),
                own_half(0),
                own_half(1),
                pl.BlockSpec((SHARDS, span, 128), lambda m, h: (0, m, h)),
                pl.BlockSpec((SHARDS, span, 128), lambda m, h: (0, 2 + m, h)),
                pl.BlockSpec((SHARDS, 16, 128), lambda m, h: (0, 16, h)),
            ]
            + [all_spec(0, span), all_spec(0, span), bias_spec],
            [own_spec(span), own_spec(span)],
            [token_shape, token_shape],
            (
                me_scalar, keys_values, keys_values, qa_all, qa_all, qa_all, do_near, do_far, column_bias,
            ),
            vmem=60,
        )
        grad_input, sums_one = whole_call(
            qkv_back_kernel,
            [shape(tokens, D), shape(8, D, dtype=f32)],
            (grad_q, grad_k, grad_v, first_near, first_far, place_rel, layer_in, gain_one, grad_hidden),
            first_rows=(3, 4),
            **qkv_cost,
        )
        norm_grads = jnp.concatenate([sums_one[:2], sums_two[:2]], 0)
        return grad_input, grad_branch, (grad_q, grad_k, grad_v), norm_grads

    sent_back, _, _, _ = backward_layer(first_back)
    received_grad = lax.ppermute(sent_back, "section", [(1, 0)])
    grad_out = jnp.where(is_last, own_cotangent, received_grad)
    go_all = lax.all_gather(grad_out, "fsdp", axis=0)
    grad_input, grad_branch, grad_qkv, norm_grads = backward_layer(
        whole_call(
            ffn_back_kernel,
            back_shapes,
            (grad_out, pre_act, hidden, place_abs, gain_two, later_all),
            in_hbm=(5,),
            **ffn_cost,
        )
    )

    fc_own = lax.dynamic_slice(later_all, (0, (me // 4) * PROWS, (me % 4) * FROWS), (SHARDS, PROWS, FROWS))
    fc_own = fc_own[:, :DROWS].reshape(D, FROWS)
    fixed = lambda *dims: pl.BlockSpec(dims, lambda s: (0,) * len(dims))
    chip = lambda kind, width: pl.BlockSpec((2, tokens, width), lambda s: (s, kind, 0))
    grad_proj_w, grad_fc_w, grad_fc_b, out_sums = pl.pallas_call(
        hidden_units_kernel,
        grid=(8,),
        in_specs=[chip(1, D), chip(0, D), fixed(D, FROWS), fixed(1, FROWS), fixed(FROWS, D)],
        out_specs=[fixed(FROWS, D), fixed(D, FROWS), fixed(8, FROWS), fixed(8, D)],
        out_shape=[shape(FROWS, D, dtype=f32), shape(D, FROWS, dtype=f32), shape(8, FROWS, dtype=f32), shape(8, D, dtype=f32)],
        **params(4 * 4 * 2 * SHARDS * tokens * D * FROWS, 3 * 2 * SHARDS * tokens * D, vmem=60),
    )(nn_all, go_all, fc_own, fc_bias.astype(f32), w_proj[0])
    grad_proj_b = lax.dynamic_slice_in_dim(out_sums[0], me * DROWS, DROWS)
    wide = jnp.concatenate([g[:, :D] for g in grad_qkv] + [grad_branch], 1)
    wide = wide.reshape(tokens, SHARDS, FROWS).transpose(1, 0, 2)
    columns = lax.all_to_all(wide, "fsdp", 0, 0)
    columns, grad_fc_w, grad_proj_w, norm_grads = lax.optimization_barrier(
        (columns, grad_fc_w, grad_proj_w, norm_grads)
    )
    grad_columns, column_sums = pl.pallas_call(
        columns_kernel,
        grid=(8,),
        in_specs=[pl.BlockSpec(memory_space=pltpu.SMEM), chip(0, D), chip(1, LANES), chip(0, FROWS)],
        out_specs=[fixed(D, FROWS), fixed(8, FROWS)],
        out_shape=[shape(D, FROWS, dtype=f32), shape(8, FROWS, dtype=f32)],
        **params(4 * 2 * SHARDS * tokens * D * FROWS, 4 * 2 * SHARDS * tokens * D, vmem=60),
    )(me_scalar, nn_all, qa_all, columns)

    width, height = 384, 72
    z = lax.axis_index("replica")

    def to_owners(columns_of_rows):
        pads = ((0, 0), (0, height - columns_of_rows.shape[1]), (0, width - columns_of_rows.shape[2]))
        return lax.all_to_all(jnp.pad(columns_of_rows, pads), "fsdp", 0, 0)

    swap = lambda v, k: lax.ppermute(v, "replica", [(j, j ^ k) for j in range(4)])

    def own_quarter(quarter):
        pick = lambda k: lax.dynamic_index_in_dim(quarter, z ^ k, 0, keepdims=False)
        total = pick(0).astype(f32)
        for term in [swap(pick(k), k) for k in (1, 3, 2)]:
            total = total + term.astype(f32)
        return total.astype(bf16)

    def all_quarters(total):
        finished = jnp.stack([total] + [swap(total, k) for k in (1, 2, 3)])
        return jnp.take(finished, z ^ jnp.arange(4), axis=0)

    got_fc = to_owners(grad_fc_w.astype(bf16).reshape(SHARDS, DROWS, FROWS)).reshape(4, 4, height, width)
    got_fc, grad_columns = lax.optimization_barrier((got_fc, grad_columns))
    own_vectors = jnp.concatenate([grad_fc_b[0], grad_proj_b, jnp.zeros((3 * width - FROWS - DROWS,), f32)])
    proj_part = jnp.pad(grad_proj_w.reshape(4, DROWS, D), ((0, 0), (0, 0), (0, 3 * width - D)))
    own_part = jnp.broadcast_to(own_vectors[None, None], (4, height - DROWS, 3 * width))
    proj_part = jnp.concatenate([proj_part, own_part], 1).astype(bf16)
    proj_parts = [proj_part[:, None, :, j * width : (j + 1) * width] for j in range(3)]
    ffn_quarter = own_quarter(jnp.concatenate([got_fc] + proj_parts, 1))

    rows = jnp.concatenate(
        [
            grad_columns.astype(bf16).reshape(SHARDS, DROWS, FROWS),
            norm_grads.astype(bf16).reshape(4, SHARDS, DROWS).transpose(1, 2, 0),
        ],
        2,
    )
    rows = jnp.pad(rows, ((0, 0), (0, 0), (0, width - rows.shape[2])))
    sums_row = jnp.broadcast_to(
        jnp.pad(column_sums[0].astype(bf16), (0, width - FROWS))[None, None], (SHARDS, 1, width)
    )
    got = to_owners(jnp.concatenate([rows, sums_row], 1))
    got, ffn_quarter = lax.optimization_barrier((got, ffn_quarter))
    ffn_total = all_quarters(ffn_quarter)
    finished = all_quarters(own_quarter(got.reshape(4, 4, height, width)))
    finished = finished.reshape(SHARDS, height, width).astype(f32)
    proj_total = jnp.concatenate([ffn_total[:, 4], ffn_total[:, 5], ffn_total[:, 6]], 2).astype(f32)
    fc_total = ffn_total[:, :4].reshape(SHARDS, height, width).astype(f32)

    def joined(block):
        return block.transpose(1, 0, 2).reshape(block.shape[1], -1)

    grad_w_qkv = joined(finished[:12, :DROWS, :FROWS])
    grad_w_out = joined(finished[12:, :DROWS, :FROWS])
    grad_w_fc = joined(fc_total[:, :DROWS, :FROWS])
    norm_sums = jnp.sum(finished[:, :DROWS, FROWS : FROWS + 4], axis=0)
    sums = finished[:, DROWS, :FROWS].reshape(SHARDS * FROWS)
    qv_sums = jnp.concatenate([sums[:D], sums[2 * D : 3 * D]])
    grad_qv_b = lax.dynamic_slice_in_dim(qv_sums, me * 2 * DROWS, 2 * DROWS)
    grad_out_b = lax.dynamic_slice_in_dim(sums, 3 * D + me * DROWS, DROWS)
    totals = (
        norm_sums[:, 0],
        norm_sums[:, 1],
        grad_w_qkv,
        grad_qv_b,
        grad_w_out,
        grad_out_b,
        norm_sums[:, 2],
        norm_sums[:, 3],
        grad_w_fc,
        proj_total[0, DROWS, :FROWS],
        proj_total[:, :DROWS, :D].reshape(FROWS, D),
        proj_total[0, DROWS, FROWS : FROWS + DROWS],
    )
    activations = out_low.reshape(1, micro, span, D)
    input_grads = grad_input.reshape(1, micro, span, D)
    return (activations, input_grads) + tuple((total[None] for total in totals))


def solution(mesh):
    return jax.shard_map(
        shards,
        mesh=mesh,
        in_specs=(
            P("replica", "fsdp", None),
            P("replica", None),
            P("replica", None),
            P("section", "fsdp"),
            P("section", "fsdp"),
            P("section", "fsdp", None),
            P("section", "fsdp"),
            P("section", "fsdp", None),
            P("section", "fsdp"),
            P("section", "fsdp"),
            P("section", "fsdp"),
            P("section", "fsdp", None),
            P("section", "fsdp"),
            P("section", "fsdp", None),
            P("section", "fsdp"),
            P("replica", "fsdp", None),
        ),
        out_specs=(
            P("section", "replica", "fsdp", None),
            P("section", "replica", "fsdp", None),
            P("section", "fsdp"),
            P("section", "fsdp"),
            P("section", "fsdp", None),
            P("section", "fsdp"),
            P("section", "fsdp", None),
            P("section", "fsdp"),
            P("section", "fsdp"),
            P("section", "fsdp"),
            P("section", "fsdp", None),
            P("section", "fsdp"),
            P("section", "fsdp", None),
            P("section", "fsdp"),
        ),
        check_vma=False,
    )
```

```python
import jax
import jax.numpy as jnp
from jax import lax
from jax.experimental import pallas as pl
from jax.experimental.pallas import tpu as pltpu
from jax.sharding import PartitionSpec as P

D = 1088
HEADS = 17
HEAD_DIM = 64
FF = 4352
SHARDS = 16
DROWS = D // SHARDS
PROWS = 80
KPAD = SHARDS * PROWS
LANES = 1152
PAIRS = 9
FROWS = FF // SHARDS
SPLITS = FF // D
SCALE = HEAD_DIM ** (-0.5)

HALF = KPAD // 2
OUT_AT = SPLITS * PROWS
PROJ_AT = OUT_AT + PROWS
GELU_C = 0.7978845608028654
GELU_A = 0.044715

epsilon = 1e-05
bf16 = jnp.bfloat16
f32 = jnp.float32


def xor_pairs(k):
    return [(i, i ^ k) for i in range(SHARDS)]


def moved(value, k):
    return lax.ppermute(value, "fsdp", xor_pairs(k))


def gather_near(x, beside=None):
    half = x.shape[0] // 2
    blocks = {0: x, 4: moved(x, 4), 12: moved(x, 12), 2: moved(x, 2)}
    result = None
    if beside is not None:
        blocks[8] = moved(x, 8)
        first = (4, 12, 2, 8)
        *arrived, result = lax.optimization_barrier((*[blocks[k] for k in first], beside()))
        blocks.update(zip(first, arrived))
    else:
        blocks[8] = jnp.concatenate([moved(blocks[4][:half], 12), moved(blocks[12][half:], 4)], 0)
    blocks[6] = moved(blocks[2], 4)
    blocks[14] = moved(blocks[2], 12)
    blocks[10] = moved(blocks[8], 2)
    return jnp.stack([blocks[k] for k in range(0, SHARDS, 2)]), result


def gather_both(x):
    near, _ = gather_near(x)
    return near, moved(near, 1)


def relative_device(me, place):
    return me ^ (2 * (place % 8) + place // 8)


def placing(me, relative):
    column = lax.broadcasted_iota(jnp.int32, (1, KPAD), 1)
    place, row = column // PROWS, column % PROWS
    owner = relative_device(me, place) if relative else place
    source = jnp.where(row < DROWS, owner * DROWS + row, -1)
    return (lax.broadcasted_iota(jnp.int32, (D, KPAD), 0) == source).astype(bf16)


def matmul(left, right):
    return jnp.dot(left, right, preferred_element_type=f32)


def contract(left, right, ldim, rdim):
    return lax.dot_general(left, right, (((ldim,), (rdim,)), ((), ())), preferred_element_type=f32)


def split_two(values):
    high = lax.reduce_precision(values, 8, 7)
    return high.astype(bf16), (values - high).astype(bf16)


def unplaced(values, place):
    rows = values.shape[0]
    both = contract(jnp.concatenate(split_two(values), 0), place, 1, 1)
    return both[:rows] + both[rows:]


def two_heads(block):
    lane = lax.broadcasted_iota(jnp.int32, block.shape, 1)
    zero = jnp.zeros_like(block)
    return jnp.concatenate(
        [jnp.where(lane < HEAD_DIM, block, zero), jnp.where(lane < HEAD_DIM, zero, block)], 0
    )


def scaled(block):
    return (block.astype(f32) * SCALE).astype(bf16)


def one_pair(both):
    rows = both.shape[0] // 2
    lane = lax.broadcasted_iota(jnp.int32, (rows, 128), 1)
    return jnp.where(lane < HEAD_DIM, both[:rows], both[rows:])


def rows_of(near_ref, far_ref):
    return jnp.concatenate(
        [near_ref[...].reshape(-1, 128), far_ref[...].reshape(-1, 128)], 0
    )


def forward_kernel(q_ref, kn_ref, kf_ref, vn_ref, vf_ref, bias_ref, out_ref, lse_ref):
    bias = bias_ref[0]
    keys, values = rows_of(kn_ref, kf_ref), rows_of(vn_ref, vf_ref)
    scores = contract(two_heads(scaled(q_ref[...])), keys, 1, 1) + jnp.concatenate([bias, bias], 0)
    top = jnp.max(scores, axis=1, keepdims=True)
    shifted = jnp.exp(scores - top)
    total = jnp.sum(shifted, axis=1, keepdims=True)
    probs = (shifted / total).astype(bf16)
    out_ref[...] = one_pair(matmul(probs, values)).astype(bf16)
    lse = top + jnp.log(total)
    lse_ref[0, 0] = jnp.transpose(jnp.broadcast_to(lse, (128, 128)))[:8]


def row_kernel(q_ref, do_ref, lse_ref, kn_ref, kf_ref, vn_ref, vf_ref, bias_ref, dq_ref):
    bias = bias_ref[0]
    keys, values = rows_of(kn_ref, kf_ref), rows_of(vn_ref, vf_ref)
    lse = jnp.transpose(jnp.broadcast_to(lse_ref[0, 0][:1], (128, 128)))[:, :1]
    scores = contract(two_heads(scaled(q_ref[...])), keys, 1, 1) + jnp.concatenate([bias, bias], 0)
    probs = jnp.exp(scores - lse)
    grad_probs = contract(two_heads(do_ref[...]), values, 1, 1)
    dots = jnp.sum(grad_probs * probs, axis=1, keepdims=True)
    grad_scores = (probs * (grad_probs - dots)).astype(bf16)
    dq_ref[...] = (one_pair(matmul(grad_scores, keys)) * SCALE).astype(bf16)


def normalized(values):
    centred = values - jnp.mean(values, axis=1, keepdims=True)
    scale = lax.rsqrt(jnp.mean(centred * centred, axis=1, keepdims=True) + epsilon)
    return centred * scale, scale


def norm_back(values, gain, grad):
    z, scale = normalized(values)
    weighted = grad * gain
    by_values = scale * (
        weighted
        - jnp.mean(weighted, axis=1, keepdims=True)
        - z * jnp.mean(weighted * z, axis=1, keepdims=True)
    )
    row = lax.broadcasted_iota(jnp.int32, (8, D), 0)
    gain_sum = jnp.sum(grad * z, axis=0, keepdims=True)
    bias_sum = jnp.sum(grad, axis=0, keepdims=True)
    return by_values, jnp.where(row == 0, gain_sum, jnp.where(row == 1, bias_sum, 0.0))


def gelu_parts(v):
    t = jnp.tanh(GELU_C * (v + GELU_A * v * v * v))
    return 0.5 * v * (1.0 + t), t


def gelu_slope(v, t):
    return 0.5 * (1.0 + t) + 0.5 * v * (1.0 - t * t) * (GELU_C * (1.0 + 3.0 * GELU_A * v * v))


def unplaced(values, place):
    rows = values.shape[0]
    high = values.astype(bf16)
    low = (values - high.astype(f32)).astype(bf16)
    both = contract(jnp.concatenate([high, low], 0), place, 1, 1)
    return both[:rows] + both[rows:]


def input_weight(near_ref, far_ref, j):
    rows = slice(j * PROWS, (j + 1) * PROWS)
    return near_ref[:, rows, :].reshape(HALF, LANES), far_ref[:, rows, :].reshape(HALF, LANES)


def qkv_kernel(x_ref, near_ref, far_ref, place_ref, gain_ref, bias_ref, sq_ref, sv_ref, n1_ref, q_ref, kv_ref):
    z, _ = normalized(x_ref[...].astype(f32))
    normed = (z * gain_ref[...] + bias_ref[...]).astype(bf16)
    n1_ref[...] = normed
    placed = matmul(normed, place_ref[...]).astype(bf16)
    rows = placed.shape[0]

    def product(j):
        near, far = input_weight(near_ref, far_ref, j)
        return matmul(placed[:, :HALF], near) + matmul(placed[:, HALF:], far)

    kv_ref[:rows] = product(1).astype(bf16)
    kv_ref[rows:] = (product(2) + sv_ref[...]).astype(bf16)
    q_ref[...] = (product(0) + sq_ref[...]).astype(bf16)


def kv_all_kernel(xn_ref, xf_ref, near_ref, far_ref, place_ref, gain_ref, bias_ref, sq_ref, sv_ref, q_ref, kn_ref, kf_ref):
    rows = xn_ref.shape[1]
    x = jnp.concatenate([xn_ref[0], xf_ref[0]], 0)[:, :D]
    z, _ = normalized(x.astype(f32))
    normed = (z * gain_ref[...] + bias_ref[...]).astype(bf16)
    placed = matmul(normed, place_ref[...]).astype(bf16)

    def product(left, j):
        near, far = input_weight(near_ref, far_ref, j)
        return matmul(left[:, :HALF], near) + matmul(left[:, HALF:], far)

    keys = product(placed, 1).astype(bf16)
    values = (product(placed, 2) + sv_ref[...]).astype(bf16)
    kn_ref[0, 0], kn_ref[0, 1] = keys[:rows], values[:rows]
    kf_ref[0, 0], kf_ref[0, 1] = keys[rows:], values[rows:]

    @pl.when(pl.program_id(0) == 0)
    def _():
        q_ref[...] = (product(placed[:rows], 0) + sq_ref[...]).astype(bf16)


def qkv_back_kernel(dq_ref, dk_ref, dv_ref, near_ref, far_ref, place_ref, x_ref, gain_ref, gh_ref, gin_ref, sums_ref):
    near_sum, far_sum = 0.0, 0.0
    for j, ref in enumerate((dq_ref, dk_ref, dv_ref)):
        near, far = input_weight(near_ref, far_ref, j)
        near_sum = near_sum + contract(ref[...], near, 1, 1)
        far_sum = far_sum + contract(ref[...], far, 1, 1)
    grad = unplaced(jnp.concatenate([near_sum, far_sum], 1), place_ref[...])
    by_input, sums_ref[...] = norm_back(x_ref[...].astype(f32), gain_ref[...], grad)
    gin_ref[...] = (gh_ref[...] + by_input).astype(bf16)


def weight_copies(all_ref, fc_buf, out_buf, proj_buf, sems):
    out_copy = pltpu.make_async_copy(all_ref.at[:, pl.ds(OUT_AT, PROWS), :], out_buf, sems.at[0])
    fc = [
        pltpu.make_async_copy(all_ref.at[:, pl.ds(j * PROWS, PROWS), :], fc_buf.at[j], sems.at[1 + j])
        for j in range(SPLITS)
    ]
    proj = [
        pltpu.make_async_copy(
            all_ref.at[pl.ds(4 * j, 4), pl.ds(PROJ_AT, FROWS), :], proj_buf.at[j], sems.at[1 + SPLITS + j]
        )
        for j in range(SPLITS)
    ]
    return out_copy, fc, proj


def ffn_forward(
    att_ref, x_ref, place_ref, os_ref, gain_ref, bias_ref, ps_ref, fs_ref, all_ref,
    hidden_ref, n2_ref, pre_ref, out_ref, fc_buf, out_buf, proj_buf, sems,
):
    out_copy, fc, proj = weight_copies(all_ref, fc_buf, out_buf, proj_buf, sems)
    out_copy.start()
    for j in range(SPLITS):
        fc[j].start()
        proj[j].start()
    place = place_ref[...]
    placed = matmul(att_ref[:, :D], place).astype(bf16)
    out_copy.wait()
    hidden = x_ref[...].astype(f32) + matmul(placed, out_buf[...].reshape(KPAD, D)) + os_ref[...]
    hidden_ref[...] = hidden
    z, _ = normalized(hidden)
    normed = (z * gain_ref[...] + bias_ref[...]).astype(bf16)
    n2_ref[...] = normed
    placed = matmul(normed, place).astype(bf16)
    total = hidden + ps_ref[...]
    for j in range(SPLITS):
        fc[j].wait()
        pre = matmul(placed, fc_buf[j].reshape(KPAD, D)) + fs_ref[j : j + 1]
        pre_ref[j] = pre
        activ, _ = gelu_parts(pre)
        proj[j].wait()
        total = total + matmul(activ.astype(bf16), proj_buf[j].reshape(D, D))
    out_ref[...] = total.astype(bf16)


def ffn_backward(
    go_ref, pre_ref, hidden_ref, place_ref, gain_ref, ready,
    gh_ref, gb_ref, ga_ref, sums_ref, fc_buf, out_buf, proj_buf,
):
    grad_out = go_ref[...]
    placed = 0.0
    for j in range(SPLITS):
        pre = pre_ref[j]
        _, t = gelu_parts(pre)
        slope = gelu_slope(pre, t)
        ready("proj", j)
        grad_pre = (contract(grad_out, proj_buf[j].reshape(D, D), 1, 1) * slope).astype(bf16)
        ready("fc", j)
        placed = placed + contract(grad_pre, fc_buf[j].reshape(KPAD, D), 1, 1)
    place = place_ref[...]
    by_hidden, sums_ref[...] = norm_back(hidden_ref[...], gain_ref[...], unplaced(placed, place))
    grad_hidden = grad_out.astype(f32) + by_hidden
    gh_ref[...] = grad_hidden
    branch = grad_hidden.astype(bf16)
    gb_ref[...] = branch
    ready("out", 0)
    grad_att = contract(branch, out_buf[...].reshape(KPAD, D), 1, 1).astype(bf16)
    ga_ref[...] = jnp.zeros_like(ga_ref)
    ga_ref[:, :D] = contract(grad_att, place, 1, 1).astype(bf16)


def ffn_back_kernel(
    go_ref, pre_ref, hidden_ref, place_ref, gain_ref, all_ref,
    gh_ref, gb_ref, ga_ref, sums_ref, fc_buf, out_buf, proj_buf, sems,
):
    out_copy, fc, proj = weight_copies(all_ref, fc_buf, out_buf, proj_buf, sems)
    for j in range(SPLITS):
        proj[j].start()
        fc[j].start()
    out_copy.start()
    copies = {"proj": proj, "fc": fc, "out": [out_copy]}
    ffn_backward(
        go_ref, pre_ref, hidden_ref, place_ref, gain_ref, lambda kind, j: copies[kind][j].wait(),
        gh_ref, gb_ref, ga_ref, sums_ref, fc_buf, out_buf, proj_buf,
    )


def ffn_both_kernel(
    att_ref, x_ref, place_ref, os_ref, gain_ref, bias_ref, ps_ref, fs_ref, all_ref, go_ref,
    hidden_ref, n2_ref, pre_ref, out_ref, gh_ref, gb_ref, ga_ref, sums_ref, fc_buf, out_buf, proj_buf, sems,
):
    ffn_forward(
        att_ref, x_ref, place_ref, os_ref, gain_ref, bias_ref, ps_ref, fs_ref, all_ref,
        hidden_ref, n2_ref, pre_ref, out_ref, fc_buf, out_buf, proj_buf, sems,
    )
    ffn_backward(
        go_ref, pre_ref, hidden_ref, place_ref, gain_ref, lambda kind, j: None,
        gh_ref, gb_ref, ga_ref, sums_ref, fc_buf, out_buf, proj_buf,
    )


def column_kernel(me_ref, k_ref, v_ref, q_ref, a_ref, lse_ref, don_ref, dof_ref, bias_ref, dk_ref, dv_ref):
    me = me_ref[0]
    owners = [relative_device(me, place) for place in range(SHARDS)]
    queries = jnp.concatenate([q_ref[owner] for owner in owners], 0)
    attended = jnp.concatenate([a_ref[owner] for owner in owners], 0)
    grads = rows_of(don_ref, dof_ref)
    rows = k_ref.shape[0]
    span = q_ref.shape[1]
    bias = bias_ref[0]
    micro = pl.program_id(0)
    term_row = lax.broadcasted_iota(jnp.int32, (16, 128), 0)
    terms = (3 * SHARDS, SHARDS * span)
    place_of = (
        lax.broadcasted_iota(jnp.int32, terms, 1) // span == lax.broadcasted_iota(jnp.int32, terms, 0) % SHARDS
    ).astype(bf16)
    picked = [
        jnp.sum(jnp.where(term_row == 2 * term + micro, lse_ref[owner].astype(f32), 0.0), axis=0, keepdims=True)
        for term in range(3)
        for owner in owners
    ]
    spread_lse = contract(jnp.concatenate(picked, 0).astype(bf16), place_of, 0, 0)
    on_diagonal = (
        lax.broadcasted_iota(jnp.int32, spread_lse.shape, 0) % span
        == lax.broadcasted_iota(jnp.int32, spread_lse.shape, 1) % span
    )
    spread_lse = jnp.where(on_diagonal, spread_lse, 0.0)
    lse_a = jnp.sum(spread_lse[:span], axis=0, keepdims=True)
    lse_b = jnp.sum(spread_lse[span:], axis=0, keepdims=True)
    product = attended.astype(f32) * grads.astype(f32)
    sides = (
        lax.broadcasted_iota(jnp.int32, (8, 256), 1) % 128 // HEAD_DIM
        == lax.broadcasted_iota(jnp.int32, (8, 256), 0)
    ).astype(bf16)
    high = product.astype(bf16)
    low = (product - high.astype(f32)).astype(bf16)
    dots = contract(sides, jnp.concatenate([high, low], 1), 1, 1)

    def spread(row_a, row_b):
        return jnp.concatenate(
            [jnp.broadcast_to(row_a, (rows, row_a.shape[1])), jnp.broadcast_to(row_b, (rows, row_b.shape[1]))], 0
        )

    scores = contract(two_heads(scaled(k_ref[...])), queries, 1, 1)
    probs = jnp.exp(scores + jnp.concatenate([bias, bias], 0) - spread(lse_a, lse_b))
    grad_probs = contract(two_heads(v_ref[...]), grads, 1, 1)
    grad_scores = (probs * (grad_probs - spread(dots[:1], dots[1:2]))).astype(bf16)
    dk_ref[...] = (one_pair(matmul(grad_scores, queries)) * SCALE).astype(bf16)
    dv_ref[...] = one_pair(matmul(probs.astype(bf16), grads)).astype(bf16)


def hidden_units_kernel(n2_ref, go_ref, fc_ref, fb_ref, proj_ref, gp_ref, gf_out_ref, bsum_ref, osum_ref):
    step = pl.program_id(0)

    @pl.when(step == 0)
    def _():
        for ref in (gp_ref, gf_out_ref, bsum_ref, osum_ref):
            ref[...] = jnp.zeros_like(ref)

    n2 = n2_ref[...].reshape(-1, D)
    go = go_ref[...].reshape(-1, D)
    pre = matmul(n2, fc_ref[...]) + fb_ref[...]
    activ, t = gelu_parts(pre)
    grad_pre = (contract(go, proj_ref[...], 1, 1) * gelu_slope(pre, t)).astype(bf16)
    gp_ref[...] += contract(activ.astype(bf16), go, 0, 0)
    gf_out_ref[...] += contract(n2, grad_pre, 0, 0)
    bsum_ref[...] += jnp.broadcast_to(jnp.sum(grad_pre.astype(f32), axis=0, keepdims=True), bsum_ref.shape)
    osum_ref[...] += jnp.broadcast_to(jnp.sum(go.astype(f32), axis=0, keepdims=True), osum_ref.shape)


def columns_kernel(me_ref, n1_ref, a_ref, cols_ref, grad_ref, sums_ref):
    step = pl.program_id(0)

    @pl.when(step == 0)
    def _():
        grad_ref[...] = jnp.zeros_like(grad_ref)
        sums_ref[...] = jnp.zeros_like(sums_ref)

    att = a_ref[...].reshape(-1, LANES)[:, :D]
    left = jnp.where(me_ref[0] < 12, n1_ref[...].reshape(-1, D), att)
    cols = cols_ref[...].reshape(-1, FROWS)
    grad_ref[...] += contract(left, cols, 0, 0)
    sums_ref[...] += jnp.broadcast_to(jnp.sum(cols.astype(f32), axis=0, keepdims=True), sums_ref.shape)


def params(flops, bytes_accessed, transcendentals=0, vmem=32):
    return dict(
        compiler_params=pltpu.CompilerParams(vmem_limit_bytes=vmem * 1024 * 1024),
        cost_estimate=pl.CostEstimate(
            flops=flops, bytes_accessed=bytes_accessed, transcendentals=transcendentals
        ),
    )


def shape(*dims, dtype=bf16):
    return jax.ShapeDtypeStruct(dims, dtype)


def whole_call(body, out_shape, operands, in_hbm=(), first_rows=(), scratch=(), flops=0, bytes_accessed=0, vmem=56):
    vm, hbm = pl.BlockSpec(memory_space=pltpu.VMEM), pl.BlockSpec(memory_space=pl.ANY)
    weight = pl.BlockSpec((8, 256, LANES), lambda s: (0, 0, 0))
    return pl.pallas_call(
        body,
        grid=(1,) if first_rows else (),
        in_specs=[
            hbm if i in in_hbm else weight if i in first_rows else vm for i in range(len(operands))
        ],
        out_specs=[vm] * len(out_shape),
        out_shape=out_shape,
        scratch_shapes=list(scratch),
        **params(flops, bytes_accessed, 0, vmem),
    )(*operands)


def pair_call(body, n_matmuls, in_specs, out_specs, out_shape, operands, vmem=32):
    steps = 2 * PAIRS
    return pl.pallas_call(
        body,
        grid=(2, PAIRS),
        in_specs=in_specs,
        out_specs=out_specs,
        out_shape=out_shape,
        **params(
            steps * n_matmuls * 2 * 128 * 128 * 1024 * 4, steps * 2 * 1024 * 128 * 2, steps * 128 * 1024, vmem
        ),
    )(*operands)


def own_spec(rows):
    return pl.BlockSpec((rows, 128), lambda m, h: (m, h))


def all_spec(kind, rows):
    return pl.BlockSpec((8, 1, 1, rows, 128), lambda m, h: (0, kind, m, 0, h))


def shards(
    inputs,
    segment_ids,
    sequence_order,
    ln1_gain,
    ln1_bias,
    w_qkv,
    qv_bias,
    w_out,
    out_bias,
    ln2_gain,
    ln2_bias,
    w_fc,
    fc_bias,
    w_proj,
    proj_bias,
    cotangent,
):
    section_index = lax.axis_index("section")
    me = lax.axis_index("fsdp")
    is_first = section_index == 0
    is_last = section_index == 1
    micro, span = inputs.shape[0], inputs.shape[1]
    tokens = micro * span
    seq_len = segment_ids.shape[1]

    def rows_padded(block):
        return jnp.pad(block, ((0, PROWS - block.shape[0]), (0, 0)))

    swapped = sequence_order[0, 0] == 1
    ordered_inputs = jnp.where(swapped, inputs[::-1], inputs).reshape(tokens, D)

    later = jnp.concatenate(
        [rows_padded(w_fc[0][:, j * D : (j + 1) * D]) for j in range(SPLITS)]
        + [rows_padded(w_out[0]), w_proj[0]],
        0,
    )
    later_all = lax.all_gather(later, "fsdp", axis=0, tiled=False)
    vectors = jnp.concatenate(
        [ln1_gain[0], ln1_bias[0], out_bias[0], ln2_gain[0], ln2_bias[0], proj_bias[0], qv_bias[0], fc_bias[0]]
    )
    vector_rows = jnp.pad(vectors[None], ((0, 15), (0, LANES - vectors.shape[0])))
    first = jnp.concatenate(
        [
            jnp.pad(w_qkv[0][:, j * D : (j + 1) * D], ((0, PROWS - DROWS), (0, LANES - D)))
            for j in range(3)
        ]
        + [vector_rows, jnp.pad(ordered_inputs, ((0, 0), (0, LANES - D)))],
        0,
    )
    first_near, first_far = gather_both(first)
    place_iota = jnp.arange(SHARDS)
    to_absolute = (relative_device(me, place_iota)[None, :] == place_iota[:, None]).astype(bf16)
    vector_rel = jnp.concatenate([first_near[:, 3 * PROWS], first_far[:, 3 * PROWS]], 0)
    vector_all = matmul(to_absolute, vector_rel)

    def vector(start, size):
        return vector_all[:, start : start + size].reshape(1, SHARDS * size)

    gain_one, bias_one, out_shift, gain_two, bias_two, proj_shift = [
        vector(j * DROWS, DROWS) for j in range(6)
    ]
    qv_full = vector(6 * DROWS, 2 * DROWS)
    fc_shift = vector(8 * DROWS, FROWS).reshape(SPLITS, D)
    shift_q = jnp.pad(qv_full[:, :D], ((0, 0), (0, LANES - D)))
    shift_v = jnp.pad(qv_full[:, D:], ((0, 0), (0, LANES - D)))

    place_rel = placing(me, True)
    place_abs = placing(me, False)

    ordered_segments = jnp.where(swapped, segment_ids[::-1], segment_ids)
    by_block = ordered_segments.reshape(micro, SHARDS, span)
    rel_devices = relative_device(me, place_iota)
    seg_rel = jnp.take(by_block, rel_devices, axis=1).reshape(micro, 1, seq_len)
    seg_own = lax.dynamic_index_in_dim(by_block, me, 1, keepdims=False)[:, :, None]
    pos_rel = (rel_devices[:, None] * span + jnp.arange(span)[None]).reshape(1, 1, seq_len)
    pos_own = (me * span + jnp.arange(span)).reshape(1, span, 1)
    same = seg_rel == seg_own
    row_bias = jnp.where(same & (pos_rel <= pos_own), 0.0, -1e30).astype(f32)
    column_bias = jnp.where(same & (pos_own <= pos_rel), 0.0, -1e30).astype(f32)
    me_scalar = me.astype(jnp.int32).reshape(1)

    bias_spec = pl.BlockSpec((1, span, seq_len), lambda m, h: (m, 0, 0))
    lse_spec = pl.BlockSpec((1, 1, 8, 128), lambda m, h: (m, h, 0, 0))
    kv_specs = [all_spec(0, span), all_spec(0, span), all_spec(1, span), all_spec(1, span)]
    token_shape = shape(tokens, LANES)
    buffers = [
        pltpu.VMEM((SPLITS, SHARDS, PROWS, D), bf16),
        pltpu.VMEM((SHARDS, PROWS, D), bf16),
        pltpu.VMEM((SPLITS, 4, FROWS, D), bf16),
        pltpu.SemaphoreType.DMA((1 + 2 * SPLITS,)),
    ]
    ffn_cost = dict(flops=4 * 2 * tokens * D * FF, bytes_accessed=2 * SHARDS * 672 * D, scratch=buffers)
    qkv_cost = dict(flops=4 * 2 * tokens * D * 3 * D, bytes_accessed=2 * SHARDS * 256 * LANES)

    def by_kind(block):
        return block.reshape(8, -1, micro, span, LANES)

    def attention(queries, kv_near, kv_far):
        return pair_call(
            forward_kernel,
            2,
            [own_spec(span)] + kv_specs + [bias_spec],
            [own_spec(span), lse_spec],
            [token_shape, shape(micro, PAIRS, 8, 128, dtype=f32)],
            (queries, kv_near, kv_far, kv_near, kv_far, row_bias),
        )

    ffn_shapes = [shape(tokens, D, dtype=f32), shape(tokens, D), shape(SPLITS, tokens, D, dtype=f32), shape(tokens, D)]
    back_shapes = [shape(tokens, D, dtype=f32), shape(tokens, D), token_shape, shape(8, D, dtype=f32)]
    vectors_two = (out_shift, gain_two, bias_two, proj_shift, fc_shift)

    step_fixed = lambda *dims: pl.BlockSpec(dims, lambda s: (0,) * len(dims))
    x_spec = pl.BlockSpec((1, tokens, LANES), lambda s: (s, 2, 0))
    kv_out = pl.BlockSpec((1, 2, tokens, LANES), lambda s: (s, 0, 0, 0))
    queries, kv_near, kv_far = pl.pallas_call(
        kv_all_kernel,
        grid=(8,),
        in_specs=[x_spec, x_spec, step_fixed(8, 256, LANES), step_fixed(8, 256, LANES), step_fixed(D, KPAD)]
        + [step_fixed(1, D), step_fixed(1, D), step_fixed(1, LANES), step_fixed(1, LANES)],
        out_specs=[step_fixed(tokens, LANES), kv_out, kv_out],
        out_shape=[token_shape, shape(8, 2, tokens, LANES), shape(8, 2, tokens, LANES)],
        **params(2 * SHARDS * tokens * D * 3 * D, 4 * SHARDS * 384 * LANES, vmem=48),
    )(first_near, first_far, first_near, first_far, place_rel, gain_one, bias_one, shift_q, shift_v)
    attended, _ = attention(queries, by_kind(kv_near), by_kind(kv_far))
    _, _, _, sent_on = whole_call(
        ffn_forward,
        ffn_shapes,
        (attended, ordered_inputs, place_abs, *vectors_two, later_all),
        in_hbm=(8,),
        **ffn_cost,
    )
    received = lax.ppermute(sent_on, "section", [(0, 1)])
    layer_in = jnp.where(is_first, ordered_inputs, received)

    own_cotangent = cotangent.reshape(tokens, D)
    normed_one, queries, keys_values = whole_call(
        qkv_kernel,
        [shape(tokens, D), token_shape, shape(2 * tokens, LANES)],
        (layer_in, first_near, first_far, place_rel, gain_one, bias_one, shift_q, shift_v),
        first_rows=(1, 2),
        **qkv_cost,
    )
    q_all = lax.all_gather(queries, "fsdp", axis=0)
    kv_near, kv_far = [by_kind(b) for b in gather_both(keys_values)]
    attended, log_total = attention(queries, kv_near, kv_far)
    attended, q_all = lax.optimization_barrier((attended, q_all))
    hidden, normed_two, pre_act, out_low, *first_back = whole_call(
        ffn_both_kernel,
        ffn_shapes + back_shapes,
        (attended, layer_in, place_abs, *vectors_two, later_all, own_cotangent),
        in_hbm=(8,),
        **ffn_cost,
    )

    lse_own = log_total[:, :, 0]
    part_one = lax.reduce_precision(lse_own, 8, 7)
    part_two = lax.reduce_precision(lse_own - part_one, 8, 7)
    part_three = lse_own - part_one - part_two
    lse_rows = jnp.stack([part_one, part_two, part_three]).astype(bf16).reshape(6, LANES)
    att_all = lax.all_gather(
        jnp.concatenate([attended, lse_rows, jnp.zeros((10, LANES), bf16)], 0), "fsdp", axis=0
    )
    nn_all = lax.all_gather(jnp.concatenate([normed_one, normed_two], 0), "fsdp", axis=0)

    def backward_layer(feed_forward):
        grad_hidden, grad_branch, grad_att, sums_two = feed_forward
        def row_part():
            return pair_call(
                row_kernel,
                3,
                [own_spec(span), own_spec(span), lse_spec] + kv_specs + [bias_spec],
                own_spec(span),
                token_shape,
                (queries, grad_att, log_total, kv_near, kv_far, kv_near, kv_far, row_bias),
            )

        near, grad_q = gather_near(grad_att, row_part)
        do_near, do_far = by_kind(near), by_kind(moved(near, 1))
        own_half = lambda half: pl.BlockSpec((span, 128), lambda m, h: (2 * half + m, h))
        grad_k, grad_v = pair_call(
            column_kernel,
            5,
            [
                pl.BlockSpec(memory_space=pltpu.SMEM),
                own_half(0),
                own_half(1),
                pl.BlockSpec((SHARDS, span, 128), lambda m, h: (0, m, h)),
                pl.BlockSpec((SHARDS, span, 128), lambda m, h: (0, m, h)),
                pl.BlockSpec((SHARDS, 16, 128), lambda m, h: (0, 8, h)),
            ]
            + [all_spec(0, span), all_spec(0, span), bias_spec],
            [own_spec(span), own_spec(span)],
            [token_shape, token_shape],
            (
                me_scalar, keys_values, keys_values, q_all, att_all, att_all, do_near, do_far, column_bias,
            ),
            vmem=60,
        )
        grad_input, sums_one = whole_call(
            qkv_back_kernel,
            [shape(tokens, D), shape(8, D, dtype=f32)],
            (grad_q, grad_k, grad_v, first_near, first_far, place_rel, layer_in, gain_one, grad_hidden),
            first_rows=(3, 4),
            **qkv_cost,
        )
        norm_grads = jnp.concatenate([sums_one[:2], sums_two[:2]], 0)
        return grad_input, grad_branch, (grad_q, grad_k, grad_v), norm_grads

    sent_back, _, _, _ = backward_layer(first_back)
    received_grad = lax.ppermute(sent_back, "section", [(1, 0)])
    grad_out = jnp.where(is_last, own_cotangent, received_grad)
    go_all = lax.all_gather(grad_out, "fsdp", axis=0)
    grad_input, grad_branch, grad_qkv, norm_grads = backward_layer(
        whole_call(
            ffn_back_kernel,
            back_shapes,
            (grad_out, pre_act, hidden, place_abs, gain_two, later_all),
            in_hbm=(5,),
            **ffn_cost,
        )
    )

    fc_own = lax.dynamic_slice(later_all, (0, (me // 4) * PROWS, (me % 4) * FROWS), (SHARDS, PROWS, FROWS))
    fc_own = fc_own[:, :DROWS].reshape(D, FROWS)
    fixed = lambda *dims: pl.BlockSpec(dims, lambda s: (0,) * len(dims))
    chip = lambda kind, width: pl.BlockSpec((2, tokens, width), lambda s: (s, kind, 0))
    grad_proj_w, grad_fc_w, grad_fc_b, out_sums = pl.pallas_call(
        hidden_units_kernel,
        grid=(8,),
        in_specs=[chip(1, D), chip(0, D), fixed(D, FROWS), fixed(1, FROWS), fixed(FROWS, D)],
        out_specs=[fixed(FROWS, D), fixed(D, FROWS), fixed(8, FROWS), fixed(8, D)],
        out_shape=[shape(FROWS, D, dtype=f32), shape(D, FROWS, dtype=f32), shape(8, FROWS, dtype=f32), shape(8, D, dtype=f32)],
        **params(4 * 4 * 2 * SHARDS * tokens * D * FROWS, 3 * 2 * SHARDS * tokens * D, vmem=60),
    )(nn_all, go_all, fc_own, fc_bias.astype(f32), w_proj[0])
    grad_proj_b = lax.dynamic_slice_in_dim(out_sums[0], me * DROWS, DROWS)
    wide = jnp.concatenate([g[:, :D] for g in grad_qkv] + [grad_branch], 1)
    wide = wide.reshape(tokens, SHARDS, FROWS).transpose(1, 0, 2)
    columns = lax.all_to_all(wide, "fsdp", 0, 0)
    columns, grad_fc_w, grad_proj_w = lax.optimization_barrier((columns, grad_fc_w, grad_proj_w))
    grad_columns, column_sums = pl.pallas_call(
        columns_kernel,
        grid=(8,),
        in_specs=[pl.BlockSpec(memory_space=pltpu.SMEM), chip(0, D), chip(0, LANES), chip(0, FROWS)],
        out_specs=[fixed(D, FROWS), fixed(8, FROWS)],
        out_shape=[shape(D, FROWS, dtype=f32), shape(8, FROWS, dtype=f32)],
        **params(4 * 2 * SHARDS * tokens * D * FROWS, 4 * 2 * SHARDS * tokens * D, vmem=60),
    )(me_scalar, nn_all, att_all, columns)

    width, height = 384, 72
    z = lax.axis_index("replica")

    def to_owners(columns_of_rows):
        pads = ((0, 0), (0, height - columns_of_rows.shape[1]), (0, width - columns_of_rows.shape[2]))
        return lax.all_to_all(jnp.pad(columns_of_rows, pads), "fsdp", 0, 0)

    def over_replicas(quarter):
        pick = lambda k: lax.dynamic_index_in_dim(quarter, z ^ k, 0, keepdims=False)
        swap = lambda v, k: lax.ppermute(v, "replica", [(j, j ^ k) for j in range(4)])
        total = pick(0).astype(f32)
        for term in [swap(pick(k), k) for k in (1, 3, 2)]:
            total = total + term.astype(f32)
        total = total.astype(bf16)
        finished = jnp.stack([total] + [swap(total, k) for k in (1, 2, 3)])
        return jnp.take(finished, z ^ jnp.arange(4), axis=0)

    got_fc = to_owners(grad_fc_w.astype(bf16).reshape(SHARDS, DROWS, FROWS)).reshape(4, 4, height, width)
    got_fc, grad_columns = lax.optimization_barrier((got_fc, grad_columns))
    own_vectors = jnp.concatenate([grad_fc_b[0], grad_proj_b, jnp.zeros((3 * width - FROWS - DROWS,), f32)])
    proj_part = jnp.pad(grad_proj_w.reshape(4, DROWS, D), ((0, 0), (0, 0), (0, 3 * width - D)))
    own_part = jnp.broadcast_to(own_vectors[None, None], (4, height - DROWS, 3 * width))
    proj_part = jnp.concatenate([proj_part, own_part], 1).astype(bf16)
    proj_parts = [proj_part[:, None, :, j * width : (j + 1) * width] for j in range(3)]
    ffn_total = over_replicas(jnp.concatenate([got_fc] + proj_parts, 1))

    rows = jnp.concatenate(
        [
            grad_columns.astype(bf16).reshape(SHARDS, DROWS, FROWS),
            norm_grads.astype(bf16).reshape(4, SHARDS, DROWS).transpose(1, 2, 0),
        ],
        2,
    )
    rows = jnp.pad(rows, ((0, 0), (0, 0), (0, width - rows.shape[2])))
    sums_row = jnp.broadcast_to(
        jnp.pad(column_sums[0].astype(bf16), (0, width - FROWS))[None, None], (SHARDS, 1, width)
    )
    got = to_owners(jnp.concatenate([rows, sums_row], 1))
    got, ffn_total = lax.optimization_barrier((got, ffn_total))
    finished = over_replicas(got.reshape(4, 4, height, width)).reshape(SHARDS, height, width).astype(f32)
    proj_total = jnp.concatenate([ffn_total[:, 4], ffn_total[:, 5], ffn_total[:, 6]], 2).astype(f32)
    fc_total = ffn_total[:, :4].reshape(SHARDS, height, width).astype(f32)

    def joined(block):
        return block.transpose(1, 0, 2).reshape(block.shape[1], -1)

    grad_w_qkv = joined(finished[:12, :DROWS, :FROWS])
    grad_w_out = joined(finished[12:, :DROWS, :FROWS])
    grad_w_fc = joined(fc_total[:, :DROWS, :FROWS])
    norm_sums = jnp.sum(finished[:, :DROWS, FROWS : FROWS + 4], axis=0)
    sums = finished[:, DROWS, :FROWS].reshape(SHARDS * FROWS)
    qv_sums = jnp.concatenate([sums[:D], sums[2 * D : 3 * D]])
    grad_qv_b = lax.dynamic_slice_in_dim(qv_sums, me * 2 * DROWS, 2 * DROWS)
    grad_out_b = lax.dynamic_slice_in_dim(sums, 3 * D + me * DROWS, DROWS)
    totals = (
        norm_sums[:, 0],
        norm_sums[:, 1],
        grad_w_qkv,
        grad_qv_b,
        grad_w_out,
        grad_out_b,
        norm_sums[:, 2],
        norm_sums[:, 3],
        grad_w_fc,
        proj_total[0, DROWS, :FROWS],
        proj_total[:, :DROWS, :D].reshape(FROWS, D),
        proj_total[0, DROWS, FROWS : FROWS + DROWS],
    )
    activations = out_low.reshape(1, micro, span, D)
    input_grads = grad_input.reshape(1, micro, span, D)
    return (activations, input_grads) + tuple((total[None] for total in totals))


def solution(mesh):
    return jax.shard_map(
        shards,
        mesh=mesh,
        in_specs=(
            P("replica", "fsdp", None),
            P("replica", None),
            P("replica", None),
            P("section", "fsdp"),
            P("section", "fsdp"),
            P("section", "fsdp", None),
            P("section", "fsdp"),
            P("section", "fsdp", None),
            P("section", "fsdp"),
            P("section", "fsdp"),
            P("section", "fsdp"),
            P("section", "fsdp", None),
            P("section", "fsdp"),
            P("section", "fsdp", None),
            P("section", "fsdp"),
            P("replica", "fsdp", None),
        ),
        out_specs=(
            P("section", "replica", "fsdp", None),
            P("section", "replica", "fsdp", None),
            P("section", "fsdp"),
            P("section", "fsdp"),
            P("section", "fsdp", None),
            P("section", "fsdp"),
            P("section", "fsdp", None),
            P("section", "fsdp"),
            P("section", "fsdp"),
            P("section", "fsdp"),
            P("section", "fsdp", None),
            P("section", "fsdp"),
            P("section", "fsdp", None),
            P("section", "fsdp"),
        ),
        check_vma=False,
    )
```
